32 devices in a mesh: gx: 8 (over z, y), gy: 4 (over x, core).
Axes of the slice: x: 2, y: 2, z: 4, core: 2. Of those that a mesh axis runs over, the one named last changes fastest.
Arguments:
- mass_per_volume: float32 [64, 512, 32], P('gx', 'gy'), may hold values from 0.5 to 2
- momentum: float32 [3, 64, 512, 32], P(None, 'gx', 'gy'), may hold values from -0.9 to 0.9
- energy: float32 [64, 512, 32], P('gx', 'gy'), may hold values from 3 to 8
Outputs:
- tendency: float32 [5, 64, 512, 32], P(None, 'gx', 'gy')
- advanced: float32 [5, 64, 512, 32], P(None, 'gx', 'gy')
The draws below stay inside these ranges and needn't reach their ends.
All inputs are finite; a program needn't handle non-finite values.
Results may differ from the reference program's by a relative error of at most 0.00016.
Values sent between devices are 32-bit elements; how exact they have to be, the bound alone decides.
No kernel may reach another device: no remote copies, remote signals or barrier semaphores. Data moves between devices by JAX's collectives and lax.ppermute only.
A program may use at most 64 MiB of HBM per device.

```python
import math
import jax
import jax.numpy as jnp
import numpy as np
from jax import lax

CX = 8
CY = 8
NZ = 512
HALO = 4
NX = 64
NY = 32


def shard_levels(own_key, dims, shards, low, top_value):
    loudness, own = 1.0, jax.random.fold_in(own_key, 6)
    for dim, shards_of in shards:
        heights = jnp.exp(jax.random.uniform(jax.random.fold_in(own, dim), (shards_of,), jnp.float32, low / len(shards), top_value / len(shards)))
        loudness = loudness * jnp.repeat(heights, dims[dim] // shards_of).reshape([-1 if axis == dim else 1 for axis in range(len(dims))])
    return loudness


def setup_inputs(seed: int = 0) -> dict:
    seeds = jax.random.split(jax.random.key(seed), 4)
    mass_per_volume = jnp.clip(jnp.exp(math.log(2.0) - 1.3862944 * jax.random.uniform(seeds[0], (NX, NZ, NY), jnp.float32) ** shard_levels(seeds[0], (NX, NZ, NY), ((0, 8), (1, 4)), -0.2, 0.2)), 0.5, 2.0)
    momentum = jnp.clip(jax.random.uniform(seeds[1], (3, NX, NZ, NY), jnp.float32, -0.9, 0.9) * shard_levels(seeds[1], (3, NX, NZ, NY), ((1, 8), (2, 4)), -0.4, 0.0), -0.9, 0.9)
    energy = jnp.clip(jnp.exp(math.log(8.0) - 0.98082925 * jax.random.uniform(seeds[2], (NX, NZ, NY), jnp.float32) ** shard_levels(seeds[2], (NX, NZ, NY), ((0, 8), (1, 4)), -0.2, 0.2)), 3.0, 8.0)
    return dict(mass_per_volume=mass_per_volume, momentum=momentum, energy=energy)


heat_ratio = 1.4
shear_resistance_reference = 0.08
sutherland_power_law = 0.7
prandtl = 0.72
section_step = 0.05
compact_alpha = 1.0 / 3.0
compact_near = 14.0 / 9.0
compact_far = 1.0 / 9.0


def tridiagonal_inverse_product(length, stencil):
    solved = np.array(stencil)
    upper_ratio = np.zeros(length)
    for row_index in range(length):
        if row_index == 0:
            pivot_value = 1.0
            solved[row_index] = solved[row_index] / pivot_value
        else:
            pivot_value = 1.0 - compact_alpha * upper_ratio[row_index - 1]
            solved[row_index] = (solved[row_index] - compact_alpha * solved[row_index - 1]) / pivot_value
        upper_ratio[row_index] = compact_alpha / pivot_value
    for row_index in range(length - 2, -1, -1):
        solved[row_index] = solved[row_index] - upper_ratio[row_index] * solved[row_index + 1]
    return solved


def compact_matrix(block_size, margin):
    length = block_size + 2 * margin
    stencil = (compact_near / 2.0) * (np.eye(length, k=1) - np.eye(length, k=-1))
    stencil = stencil + (compact_far / 4.0) * (np.eye(length, k=2) - np.eye(length, k=-2))
    inverse_product = tridiagonal_inverse_product(length, stencil)
    return inverse_product[margin:margin + block_size].astype(np.float32)


def right_side(conserved, gradients_of, derive_x, derive_y, derive_z):
    mass_per_volume = conserved[0]
    momentum = conserved[1:4]
    energy = conserved[4]
    local_speed_vector = momentum / mass_per_volume
    kinetic = 0.5 * jnp.sum(momentum * local_speed_vector, axis=0)
    normal_force_per_area = (heat_ratio - 1.0) * (energy - kinetic)
    thermal_state = normal_force_per_area / mass_per_volume
    basic_quantities = jnp.concatenate([local_speed_vector, thermal_state[None]], 0)
    gradients = gradients_of(basic_quantities)
    shear_resistance = shear_resistance_reference * jnp.power(thermal_state, sutherland_power_law)
    conductivity = shear_resistance * heat_ratio / ((heat_ratio - 1.0) * prandtl)
    dilatation = gradients[0][0] + gradients[1][1] + gradients[2][2]
    derivers = (derive_x, derive_y, derive_z)
    accumulated = None
    for direction in range(3):
        stress_column = [shear_resistance * (gradients[direction][component] + gradients[component][direction]) for component in range(3)]
        stress_column[direction] = stress_column[direction] - (2.0 / 3.0) * shear_resistance * dilatation
        fluxes = [momentum[direction]]
        for component in range(3):
            moment_flux = momentum[component] * local_speed_vector[direction] - stress_column[component]
            if component == direction:
                moment_flux = moment_flux + normal_force_per_area
            fluxes.append(moment_flux)
        work_term = stress_column[0] * local_speed_vector[0] + stress_column[1] * local_speed_vector[1] + stress_column[2] * local_speed_vector[2]
        fluxes.append((energy + normal_force_per_area) * local_speed_vector[direction] - work_term - conductivity * gradients[direction][3])
        divergence_part = derivers[direction](jnp.stack(fluxes))
        accumulated = divergence_part if accumulated is None else accumulated + divergence_part
    return -accumulated


def along_blocks(values, axis_pos, block_size):
    matrix = jnp.asarray(compact_matrix(block_size, HALO), jnp.float32)
    rotated = jnp.moveaxis(values, axis_pos, 0)
    total = rotated.shape[0]
    padded = jnp.concatenate([rotated[total - HALO:], rotated, rotated[:HALO]], 0)
    positions = (np.arange(total // block_size)[:, None] * block_size + np.arange(block_size + 2 * HALO)[None, :]).astype(np.int32)
    segments = padded[positions]
    result = jnp.einsum("il,bl...->bi...", matrix, segments, precision=lax.Precision.HIGHEST)
    return jnp.moveaxis(result.reshape(rotated.shape), 0, axis_pos)


def along_span(values, axis_pos):
    total = values.shape[axis_pos]
    spectra = jnp.fft.rfft(values, axis=axis_pos)
    wavenumbers = 2.0 * np.pi * np.arange(total // 2 + 1) / total
    wavenumbers[-1] = 0.0
    shape_b = [1] * values.ndim
    shape_b[axis_pos] = total // 2 + 1
    factor = jnp.asarray(wavenumbers.reshape(shape_b), jnp.float32)
    return jnp.fft.irfft(spectra * (1j * factor), n=total, axis=axis_pos)


def per_component(function, stacked):
    return jnp.stack([function(stacked[position]) for position in range(stacked.shape[0])])


def derive_x(stacked):
    return per_component(lambda single: along_blocks(single, 0, CX), stacked)


def derive_y(stacked):
    return per_component(lambda single: along_blocks(single, 2, CY), stacked)


def derive_z(stacked):
    return per_component(lambda single: along_span(single, 1), stacked)


def gradients_all(basic_quantities):
    return (derive_x(basic_quantities), derive_y(basic_quantities), derive_z(basic_quantities))


def reference(mass_per_volume, momentum, energy):
    conserved = jnp.concatenate([mass_per_volume[None], momentum, energy[None]], 0)
    tendency = right_side(conserved, gradients_all, derive_x, derive_y, derive_z)
    return tendency, conserved + section_step * tendency
```

```python
import functools

import jax
import jax.numpy as jnp
import numpy as np
from jax import lax
from jax.experimental import pallas as pl
from jax.experimental.pallas import tpu as pltpu
from jax.sharding import PartitionSpec as P

CX = 8
CY = 8
NZ = 512
HALO = 4


heat_ratio = 1.4
shear_resistance_reference = 0.08
sutherland_power_law = 0.7
prandtl = 0.72
section_step = 0.05
compact_alpha = 1.0 / 3.0
compact_near = 14.0 / 9.0
compact_far = 1.0 / 9.0

conduction = heat_ratio / ((heat_ratio - 1.0) * prandtl)
enthalpy = heat_ratio / (heat_ratio - 1.0)


def tridiagonal_inverse_product(length, stencil):
    solved = np.array(stencil)
    upper_ratio = np.zeros(length)
    for row_index in range(length):
        if row_index == 0:
            pivot_value = 1.0
            solved[row_index] = solved[row_index] / pivot_value
        else:
            pivot_value = 1.0 - compact_alpha * upper_ratio[row_index - 1]
            solved[row_index] = (
                solved[row_index] - compact_alpha * solved[row_index - 1]
            ) / pivot_value
        upper_ratio[row_index] = compact_alpha / pivot_value
    for row_index in range(length - 2, -1, -1):
        solved[row_index] = solved[row_index] - upper_ratio[row_index] * solved[row_index + 1]
    return solved


def compact_matrix(block_size, margin):
    length = block_size + 2 * margin
    stencil = compact_near / 2.0 * (np.eye(length, k=1) - np.eye(length, k=-1))
    stencil = stencil + compact_far / 4.0 * (np.eye(length, k=2) - np.eye(length, k=-2))
    inverse_product = tridiagonal_inverse_product(length, stencil)
    return inverse_product[margin : margin + block_size].astype(np.float32)


def pitch_matrix(total, block_size):
    matrix = compact_matrix(block_size, HALO)
    result = np.zeros((total, total), np.float32)
    rows_all = np.arange(total)
    block_start = rows_all // block_size * block_size
    for offset in range(block_size + 2 * HALO):
        columns = (block_start - HALO + offset) % total
        result[rows_all, columns] += matrix[rows_all % block_size, offset]
    return result


def span_matrix(total):
    offsets = np.arange(total)[:, None] - np.arange(total)[None, :]
    angles = np.pi * offsets / total
    signs = np.where(offsets % 2 == 0, 1.0, -1.0)
    sines = np.where(offsets == 0, 1.0, np.sin(angles))
    result = np.where(offsets == 0, 0.0, np.pi / total * signs * np.cos(angles) / sines)
    return result.astype(np.float32)


F32 = jnp.float32
BF16 = jnp.bfloat16


def halves(matrix):
    high = matrix.astype(BF16)
    low = (matrix - np.asarray(high, np.float32)).astype(BF16)
    return jnp.asarray(high), jnp.asarray(low)


def split(values):
    high = values.astype(BF16)
    low = (values - high.astype(F32)).astype(BF16)
    return high, low


def dot(a, b):
    return jnp.dot(a, b, preferred_element_type=F32)


def right_product(values, matrix_high, matrix_low):
    high, low = split(values)
    return dot(high, matrix_high) + dot(low, matrix_high) + dot(high, matrix_low)


def left_product(matrix_high, matrix_low, values):
    high, low = split(values)
    return dot(matrix_high, high) + dot(matrix_high, low) + dot(matrix_low, high)


def compact_x(planes):
    matrix = compact_matrix(CX, HALO).astype(np.float64)
    length = CX + 2 * HALO
    half = length // 2
    odd = [planes[l] - planes[length - 1 - l] for l in range(half)]
    even = [planes[l] + planes[length - 1 - l] for l in range(half)]
    result = [None] * CX
    for i in range(CX // 2):
        first = None
        second = None
        for l in range(half):
            a = float(0.5 * (matrix[i, l] - matrix[i, length - 1 - l]))
            b = float(0.5 * (matrix[i, l] + matrix[i, length - 1 - l]))
            first = a * odd[l] if first is None else first + a * odd[l]
            second = b * even[l] if second is None else second + b * even[l]
        result[i] = first + second
        result[CX - 1 - i] = first - second
    return result


def extended_planes(before, own, after, field, rows):
    return (
        [before[field, l, rows, :] for l in range(HALO)]
        + [own[field, l, rows, :] for l in range(CX)]
        + [after[field, l, rows, :] for l in range(HALO)]
    )


def kernel_primitives(rho, mom, energy, prim, low, high):
    for x in range(CX):
        density = rho[x]
        inverse = 1.0 / density
        u = mom[0, x] * inverse
        v = mom[1, x] * inverse
        w = mom[2, x] * inverse
        kinetic = 0.5 * (mom[0, x] * u + mom[1, x] * v + mom[2, x] * w)
        temperature = (heat_ratio - 1.0) * (energy[x] - kinetic) * inverse
        target = (low, x) if x < HALO else (high, x - HALO)
        for f, value in enumerate((u, v, w, temperature)):
            prim[f, x] = value
            target[0][f, target[1]] = value
        prim[4, x] = density


def kernel_local_gradients(prim, before, after, y_high, y_low, dx, dy, mu, shared):
    rows_all = prim.shape[2]
    for start in range(0, rows_all, 8):
        rows = slice(start, start + 8)
        for f in range(4):
            derived = compact_x(extended_planes(before, prim, after, f, rows))
            for x in range(CX):
                dx[f, x, rows, :] = derived[x]
    for x in range(CX):
        viscosity = shear_resistance_reference * jnp.exp(
            sutherland_power_law * jnp.log(prim[3, x])
        )
        mu[x] = viscosity
        shared[0, x] = (2.0 / 3.0) * viscosity * dx[0, x]
        shared[1, x] = viscosity * dx[2, x]
    for f in range(4):
        values = prim[f].reshape(-1, prim.shape[-1])
        dy[f] = left_product(y_high[...], y_low[...], values).reshape(prim.shape[1:])


def kernel_flux_x(me, prim, lines, dx, dy, mu, z_high, z_low, dz, flux, low, high):
    count, _, _, rows, width = lines.shape
    column = pl.ds(pl.multiple_of(me[0] * width, width), width)
    for f in range(4):
        values = jnp.concatenate(
            [lines[s, f].reshape(-1, width) for s in range(count)], axis=1
        )
        dz[f] = right_product(values, z_high[:, column], z_low[:, column]).reshape(
            prim.shape[1:]
        )
    for x in range(CX):
        u, v, w, t, density = (prim[f, x] for f in range(5))
        viscosity = mu[x]
        dil = dx[0, x] + dy[1, x] + dz[2, x]
        s1 = viscosity * (2.0 * dx[0, x] - (2.0 / 3.0) * dil)
        s2 = viscosity * (dx[1, x] + dy[0, x])
        s3 = viscosity * (dx[2, x] + dz[0, x])
        m = density * u
        pressure = density * t
        total = m * (enthalpy * t + 0.5 * (u * u + v * v + w * w))
        values = (
            m,
            m * u + pressure - s1,
            m * v - s2,
            m * w - s3,
            total - (s1 * u + s2 * v + s3 * w) - conduction * viscosity * dx[3, x],
        )
        target = (low, x) if x < HALO else (high, x - HALO)
        for f in range(5):
            flux[f, x] = values[f]
            target[0][f, target[1]] = values[f]


def kernel_flux_yz(
    me, prim, lines, dx, dy, dz, mu, y_high, y_low, z_high, z_low, part,
    grad, dy_lines, flux, flux_y,
):
    count, _, _, rows, width = lines.shape
    total_rows = CX * rows
    column = pl.ds(pl.multiple_of(me[0] * width, width), width)
    for f in range(4):
        values = jnp.concatenate(
            [lines[s, f].reshape(total_rows, width) for s in range(count)], axis=1
        )
        grad[f] = right_product(values, z_high[...], z_low[...])
        if f in (1, 2):
            dy_lines[f - 1] = left_product(y_high[...], y_low[...], values)

    def flux_plane(x, carry):
        at = pl.ds(pl.multiple_of(x * rows, rows), rows)
        for s in range(count):
            lanes = slice(s * width, (s + 1) * width)
            u, v, w, t, density = (lines[s, f, x] for f in range(5))
            viscosity = shear_resistance_reference * jnp.exp(
                sutherland_power_law * jnp.log(t)
            )
            zu, zv, zw, zt = (grad[f, at, lanes] for f in range(4))
            yv = dy_lines[0, at, lanes]
            yw = dy_lines[1, at, lanes]
            s1 = viscosity * zu
            s2 = viscosity * (zv + yw)
            s3 = viscosity * ((4.0 / 3.0) * zw - (2.0 / 3.0) * yv)
            m = density * w
            total = m * (enthalpy * t + 0.5 * (u * u + v * v + w * w))
            flux[0, at, lanes] = m
            flux[1, at, lanes] = m * u - s1
            flux[2, at, lanes] = m * v - s2
            flux[3, at, lanes] = m * w + density * t - s3
            flux[4, at, lanes] = (
                total - (s1 * u + s2 * v + s3 * w) - conduction * viscosity * zt
            )
        u, v, w, t, density = (prim[f, x] for f in range(5))
        viscosity = mu[x]
        dil = dx[0, x] + dy[1, x] + dz[2, x]
        s1 = viscosity * (dy[0, x] + dx[1, x])
        s2 = viscosity * (2.0 * dy[1, x] - (2.0 / 3.0) * dil)
        s3 = viscosity * (dy[2, x] + dz[1, x])
        m = density * v
        total = m * (enthalpy * t + 0.5 * (u * u + v * v + w * w))
        flux_y[0, at, :] = m
        flux_y[1, at, :] = m * u - s1
        flux_y[2, at, :] = m * v + density * t - s2
        flux_y[3, at, :] = m * w - s3
        flux_y[4, at, :] = (
            total - (s1 * u + s2 * v + s3 * w) - conduction * viscosity * dy[3, x]
        )
        return carry

    lax.fori_loop(0, CX, flux_plane, 0)
    for f in range(5):
        result = right_product(flux[f], z_high[:, column], z_low[:, column])
        result = result + left_product(y_high[...], y_low[...], flux_y[f])
        part[f] = result.reshape(prim.shape[1:])


def kernel_finish(
    me, rho, mom, energy, lines, shared, part, flux, before, after, z_high, z_low,
    tendency, advanced, work,
):
    count, _, _, rows, width = lines.shape
    total_rows = CX * rows
    column = pl.ds(pl.multiple_of(me[0] * width, width), width)
    for x in range(CX):
        at = slice(x * rows, (x + 1) * rows)
        for s in range(count):
            lanes = slice(s * width, (s + 1) * width)
            normal = shared[s, 0, x]
            shear = shared[s, 1, x]
            work[0, at, lanes] = -shear
            work[1, at, lanes] = normal
            work[2, at, lanes] = normal * lines[s, 2, x] - shear * lines[s, 0, x]
    corrections = {}
    for position, f in enumerate((1, 3, 4)):
        corrections[f] = right_product(work[position], z_high[:, column], z_low[:, column])
    for f in range(5):
        total = part[f]
        if f in corrections:
            total = total + corrections[f].reshape(total.shape)
        tendency[f] = total
    for start in range(0, rows, 8):
        chunk = slice(start, start + 8)
        for f in range(5):
            derived = compact_x(extended_planes(before, flux, after, f, chunk))
            for x in range(CX):
                value = -(tendency[f, x, chunk, :] + derived[x])
                if f == 0:
                    old = rho[x, chunk, :]
                elif f == 4:
                    old = energy[x, chunk, :]
                else:
                    old = mom[f - 1, x, chunk, :]
                tendency[f, x, chunk, :] = value
                advanced[f, x, chunk, :] = old + section_step * value


def call(kernel, outputs, scratch, smem, cost, *operands):
    in_specs = [pl.BlockSpec(memory_space=pltpu.VMEM) for _ in operands]
    if smem:
        in_specs[0] = pl.BlockSpec(memory_space=pltpu.SMEM)
    return pl.pallas_call(
        kernel,
        out_shape=[jax.ShapeDtypeStruct(shape, F32) for shape in outputs],
        in_specs=in_specs,
        out_specs=[pl.BlockSpec(memory_space=pltpu.VMEM) for _ in outputs],
        scratch_shapes=scratch,
        cost_estimate=pl.CostEstimate(flops=cost, bytes_accessed=cost // 300, transcendentals=0),
        compiler_params=pltpu.CompilerParams(vmem_limit_bytes=48 * 1024 * 1024),
    )(*operands)


def fast_device(mass_per_volume, momentum, energy):
    rho = jnp.transpose(mass_per_volume, (0, 2, 1))
    mom = jnp.transpose(momentum, (0, 1, 3, 2))
    ene = jnp.transpose(energy, (0, 2, 1))
    _, rows, width = rho.shape
    count = lax.axis_size("gy")
    length = count * width
    me = lax.axis_index("gy").astype(jnp.int32).reshape(1)
    z_high, z_low = halves(span_matrix(length).T)
    y_high, y_low = halves(np.kron(np.eye(CX, dtype=np.float32), pitch_matrix(rows, CY)))
    block = (CX, rows, width)
    edge = (HALO, rows, width)
    devices = lax.axis_size("gx")
    up = [(i, (i + 1) % devices) for i in range(devices)]
    down = [(j, i) for i, j in up]

    prim, low, high = call(
        kernel_primitives, [(5,) + block, (4,) + edge, (4,) + edge], [], False, 10**9,
        rho, mom, ene,
    )
    lines = lax.all_gather(prim, "gy", axis=0, tiled=False)
    before = lax.ppermute(high, "gx", up)
    after = lax.ppermute(low, "gx", down)
    dx, dy, mu, mine = call(
        kernel_local_gradients, [(4,) + block, (4,) + block, block, (2,) + block], [],
        False, 2 * 10**9, prim, before, after, y_high, y_low,
    )
    shared = lax.all_gather(mine, "gy", axis=0, tiled=False)
    dz, flux, flux_low, flux_high = call(
        kernel_flux_x, [(4,) + block, (5,) + block, (5,) + edge, (5,) + edge], [],
        True, 2 * 10**9, me, prim, lines, dx, dy, mu, z_high, z_low,
    )
    flux_before = lax.ppermute(flux_high, "gx", up)
    flux_after = lax.ppermute(flux_low, "gx", down)
    (part,) = call(
        kernel_flux_yz, [(5,) + block],
        [
            pltpu.VMEM((4, CX * rows, length), F32),
            pltpu.VMEM((2, CX * rows, length), F32),
            pltpu.VMEM((5, CX * rows, length), F32),
            pltpu.VMEM((5, CX * rows, width), F32),
        ],
        True, 4 * 10**9, me, prim, lines, dx, dy, dz, mu, y_high, y_low, z_high, z_low,
    )
    tendency, advanced = call(
        kernel_finish, [(5,) + block, (5,) + block],
        [pltpu.VMEM((3, CX * rows, length), F32)],
        True, 2 * 10**9, me, rho, mom, ene, lines, shared, part, flux, flux_before, flux_after,
        z_high, z_low,
    )
    return (
        jnp.transpose(tendency, (0, 1, 3, 2)),
        jnp.transpose(advanced, (0, 1, 3, 2)),
    )


def padded(array, sides, width):
    for axis, dim in sides:
        devices, length = (lax.axis_size(axis), array.shape[dim])
        up = [(i, (i + 1) % devices) for i in range(devices)]
        down = [(j, i) for i, j in up]
        last = lax.slice_in_dim(array, length - width, length, axis=dim)
        initial = lax.slice_in_dim(array, 0, width, axis=dim)
        before = lax.ppermute(last, axis, up)
        after = lax.ppermute(initial, axis, down)
        array = jnp.concatenate([before, array, after], axis=dim)
    return array


def right_side(conserved, gradients_of, derive_x, derive_y, derive_z):
    mass_per_volume = conserved[0]
    momentum = conserved[1:4]
    energy = conserved[4]
    local_speed_vector = momentum / mass_per_volume
    kinetic = 0.5 * jnp.sum(momentum * local_speed_vector, axis=0)
    normal_force_per_area = (heat_ratio - 1.0) * (energy - kinetic)
    thermal_state = normal_force_per_area / mass_per_volume
    basic_quantities = jnp.concatenate([local_speed_vector, thermal_state[None]], 0)
    gradients = gradients_of(basic_quantities)
    shear_resistance = shear_resistance_reference * jnp.power(thermal_state, sutherland_power_law)
    conductivity = shear_resistance * heat_ratio / ((heat_ratio - 1.0) * prandtl)
    dilatation = gradients[0][0] + gradients[1][1] + gradients[2][2]
    derivers = (derive_x, derive_y, derive_z)
    accumulated = None
    for direction in range(3):
        stress_column = [
            shear_resistance * (gradients[direction][component] + gradients[component][direction])
            for component in range(3)
        ]
        stress_column[direction] = (
            stress_column[direction] - 2.0 / 3.0 * shear_resistance * dilatation
        )
        fluxes = [momentum[direction]]
        for component in range(3):
            moment_flux = (
                momentum[component] * local_speed_vector[direction] - stress_column[component]
            )
            if component == direction:
                moment_flux = moment_flux + normal_force_per_area
            fluxes.append(moment_flux)
        work_term = (
            stress_column[0] * local_speed_vector[0]
            + stress_column[1] * local_speed_vector[1]
            + stress_column[2] * local_speed_vector[2]
        )
        fluxes.append(
            (energy + normal_force_per_area) * local_speed_vector[direction]
            - work_term
            - conductivity * gradients[direction][3]
        )
        divergence_part = derivers[direction](jnp.stack(fluxes))
        accumulated = divergence_part if accumulated is None else accumulated + divergence_part
    return -accumulated


def plain_device(mass_per_volume, momentum, energy):
    conserved = jnp.concatenate([mass_per_volume[None], momentum, energy[None]], 0)
    highest = lax.Precision.HIGHEST
    x_matrix = jnp.asarray(compact_matrix(CX, HALO))
    z_matrix = jnp.asarray(span_matrix(NZ))

    def apply_x(extended):
        return jnp.einsum("il,flab->fiab", x_matrix, extended, precision=highest)

    def flux_x(values):
        return apply_x(padded(values, (("gx", 1),), HALO))

    y_matrix = jnp.asarray(pitch_matrix(conserved.shape[3], CY))

    def apply_y(values):
        return jnp.einsum("fabk,jk->fabj", values, y_matrix, precision=highest)

    def derive_span(values):
        lines = jnp.transpose(
            lax.all_to_all(values, "gy", split_axis=3, concat_axis=2, tiled=True), (0, 1, 3, 2)
        )
        derived = jnp.einsum("fack,jk->facj", lines, z_matrix, precision=highest)
        returned = lax.all_to_all(derived, "gy", split_axis=3, concat_axis=2, tiled=True)
        return jnp.transpose(returned, (0, 1, 3, 2))

    def gradients_of(basic_quantities):
        extended = padded(basic_quantities, (("gx", 1),), HALO)
        return (apply_x(extended), apply_y(basic_quantities), derive_span(basic_quantities))

    tendency = right_side(conserved, gradients_of, flux_x, apply_y, derive_span)
    advanced = conserved + section_step * tendency
    return (tendency, advanced)


def per_device(mass_per_volume, momentum, energy):
    planes, width, rows = mass_per_volume.shape
    if planes == CX and width % 128 == 0 and rows <= 32 and rows % CY == 0:
        return fast_device(mass_per_volume, momentum, energy)
    return plain_device(mass_per_volume, momentum, energy)


def solution(mesh):
    in_specs = (P("gx", "gy", None), P(None, "gx", "gy", None), P("gx", "gy", None))
    out_specs = (P(None, "gx", "gy", None), P(None, "gx", "gy", None))
    return jax.shard_map(
        per_device, mesh=mesh, in_specs=in_specs, out_specs=out_specs, check_vma=False
    )
```

```python
import functools

import jax
import jax.numpy as jnp
import numpy as np
from jax import lax
from jax.experimental import pallas as pl
from jax.experimental.pallas import tpu as pltpu
from jax.sharding import PartitionSpec as P

CX = 8
CY = 8
NZ = 512
HALO = 4


heat_ratio = 1.4
shear_resistance_reference = 0.08
sutherland_power_law = 0.7
prandtl = 0.72
section_step = 0.05
compact_alpha = 1.0 / 3.0
compact_near = 14.0 / 9.0
compact_far = 1.0 / 9.0

conduction = heat_ratio / ((heat_ratio - 1.0) * prandtl)
enthalpy = heat_ratio / (heat_ratio - 1.0)


def tridiagonal_inverse_product(length, stencil):
    solved = np.array(stencil)
    upper_ratio = np.zeros(length)
    for row_index in range(length):
        if row_index == 0:
            pivot_value = 1.0
            solved[row_index] = solved[row_index] / pivot_value
        else:
            pivot_value = 1.0 - compact_alpha * upper_ratio[row_index - 1]
            solved[row_index] = (
                solved[row_index] - compact_alpha * solved[row_index - 1]
            ) / pivot_value
        upper_ratio[row_index] = compact_alpha / pivot_value
    for row_index in range(length - 2, -1, -1):
        solved[row_index] = solved[row_index] - upper_ratio[row_index] * solved[row_index + 1]
    return solved


def exact_compact_matrix(block_size, margin):
    length = block_size + 2 * margin
    stencil = compact_near / 2.0 * (np.eye(length, k=1) - np.eye(length, k=-1))
    stencil = stencil + compact_far / 4.0 * (np.eye(length, k=2) - np.eye(length, k=-2))
    inverse_product = tridiagonal_inverse_product(length, stencil)
    return inverse_product[margin : margin + block_size]


def compact_matrix(block_size, margin):
    return exact_compact_matrix(block_size, margin).astype(np.float32)


def pitch_matrix(total, block_size):
    matrix = compact_matrix(block_size, HALO)
    result = np.zeros((total, total), np.float32)
    rows_all = np.arange(total)
    block_start = rows_all // block_size * block_size
    for offset in range(block_size + 2 * HALO):
        columns = (block_start - HALO + offset) % total
        result[rows_all, columns] += matrix[rows_all % block_size, offset]
    return result


def span_matrix(total):
    offsets = np.arange(total)[:, None] - np.arange(total)[None, :]
    angles = np.pi * offsets / total
    signs = np.where(offsets % 2 == 0, 1.0, -1.0)
    sines = np.where(offsets == 0, 1.0, np.sin(angles))
    result = np.where(offsets == 0, 0.0, np.pi / total * signs * np.cos(angles) / sines)
    return result.astype(np.float32)


F32 = jnp.float32
BF16 = jnp.bfloat16
U, W, V, T, R = range(5)
PLACES = (0, 2, 1, 3)
HALF = CX // 2


def halves(matrix):
    high = np.asarray(matrix, np.float32).astype(BF16)
    low = (matrix - high.astype(np.float32)).astype(BF16)
    return jnp.asarray(high), jnp.asarray(low)


def span_blocks(length, sources, targets):
    width = length // 4
    matrix = span_matrix(length).T
    both = []
    for core in range(2):
        columns = []
        for target in targets:
            to = core ^ target
            columns.append(
                np.concatenate(
                    [
                        matrix[
                            (core ^ source) * width : (core ^ source) * width + width,
                            to * width : to * width + width,
                        ]
                        for source in sources
                    ],
                    axis=0,
                )
            )
        both.append(np.concatenate(columns, axis=1))
    return halves(np.stack(both))


def halo_basis():
    matrix = exact_compact_matrix(CX, HALO)
    left = matrix[:, :HALO]
    basis = np.linalg.svd(left)[2][:2]
    inner = left @ basis.T
    outer = -inner[::-1]
    return basis, np.concatenate(
        [inner, matrix[:, HALO : HALO + CX], outer[:, ::-1]], axis=1
    )


def split(values):
    high = values.astype(BF16)
    low = (values - high.astype(F32)).astype(BF16)
    return high, low


def dot(a, b):
    return jnp.dot(a, b, preferred_element_type=F32)


def right_product(values, matrix_high, matrix_low):
    high, low = split(values)
    return dot(high, matrix_high) + dot(low, matrix_high) + dot(high, matrix_low)


def left_product(matrix_high, matrix_low, values):
    high, low = split(values)
    return dot(matrix_high, high) + dot(matrix_high, low) + dot(matrix_low, high)


def compact_x(planes):
    matrix = halo_basis()[1]
    length = CX + 4
    half = length // 2
    odd = [planes[l] - planes[length - 1 - l] for l in range(half)]
    even = [planes[l] + planes[length - 1 - l] for l in range(half)]
    result = [None] * CX
    for i in range(HALF):
        first = None
        second = None
        for l in range(half):
            a = float(0.5 * (matrix[i, l] - matrix[i, length - 1 - l]))
            b = float(0.5 * (matrix[i, l] + matrix[i, length - 1 - l]))
            first = a * odd[l] if first is None else first + a * odd[l]
            second = b * even[l] if second is None else second + b * even[l]
        result[i] = first + second
        result[CX - 1 - i] = first - second
    return result


def extended(before, own, after, f, rows):
    return (
        [before[f, 0, rows, :], before[f, 1, rows, :]]
        + [own[f, l, rows, :] for l in range(CX)]
        + [after[f, 1, rows, :], after[f, 0, rows, :]]
    )


def halo_sums(values, f, rows, up, down):
    basis = halo_basis()[0]
    for k in range(2):
        top = None
        bottom = None
        for l in range(HALO):
            a = float(basis[k, l]) * values[f, CX - HALO + l, rows, :]
            b = float(basis[k, l]) * values[f, HALO - 1 - l, rows, :]
            top = a if top is None else top + a
            bottom = b if bottom is None else bottom + b
        up[f, k, rows, :] = top
        down[f, k, rows, :] = bottom


def row_chunks(rows):
    return [slice(start, start + 8) for start in range(0, rows, 8)]


def flat(values):
    return values.reshape(-1, values.shape[-1])


def kernel_primitives(
    rho_in, mom_in, ene_in, own, first, second, up, down, rho, mom, ene, arrived
):
    copies = [
        pltpu.make_async_copy(source, target, arrived.at[k])
        for k, (source, target) in enumerate(((rho_in, rho), (mom_in, mom), (ene_in, ene)))
    ]
    for copy in copies:
        copy.start()
    for copy in copies:
        copy.wait()

    def plane(x, carry):
        density = rho[x]
        inverse = 1.0 / density
        u = mom[0, x] * inverse
        v = mom[1, x] * inverse
        w = mom[2, x] * inverse
        kinetic = 0.5 * (mom[0, x] * u + mom[1, x] * v + mom[2, x] * w)
        temperature = (heat_ratio - 1.0) * (ene[x] - kinetic) * inverse
        own[U, x] = u
        own[W, x] = w
        own[V, x] = v
        own[T, x] = temperature
        first[0, x] = u
        first[1, x] = w
        second[0, x] = v
        second[1, x] = temperature
        second[2, x] = density
        return carry

    lax.fori_loop(0, CX, plane, 0)

    def sums(f, carry):
        for rows in row_chunks(rho.shape[1]):
            halo_sums(own, f, rows, up, down)
        return carry

    lax.fori_loop(0, 4, sums, 0)


def kernel_pitch_gradients(own, y_high, y_low, dy, mu):
    for f in range(4):
        dy[f] = left_product(y_high[...], y_low[...], flat(own[f])).reshape(own.shape[1:])

    def plane(x, carry):
        mu[x] = shear_resistance_reference * jnp.exp(
            sutherland_power_law * jnp.log(own[T, x])
        )
        return carry

    lax.fori_loop(0, CX, plane, 0)


def kernel_stream_gradients(own, before, after, mu, dx, third):
    def field(f, carry):
        for rows in row_chunks(own.shape[2]):
            derived = compact_x(extended(before, own, after, f, rows))
            for x in range(CX):
                dx[f, x, rows, :] = derived[x]
        return carry

    lax.fori_loop(0, 4, field, 0)

    def plane(x, carry):
        third[0, x] = (2.0 / 3.0) * mu[x] * dx[U, x]
        third[1, x] = mu[x] * dx[W, x]
        return carry

    lax.fori_loop(0, CX, plane, 0)


def kernel_flux_x(
    parity, own, second, peer_first, mate, across_first, dx, dy, mu, z_high, z_low,
    dz, flux, up, down,
):
    width = own.shape[-1]
    odd = parity[0]
    for f in range(2):
        values = jnp.concatenate(
            [flat(own[f]), flat(peer_first[f]), flat(mate[f]), flat(across_first[f])], axis=1
        )
        dz[f] = right_product(values, z_high[odd], z_low[odd])

    rows = own.shape[2]

    def plane(x, carry):
        at = pl.ds(pl.multiple_of(x * rows, rows), rows)
        u, w, v, t = (own[f, x] for f in range(4))
        density = second[2, x]
        viscosity = mu[x]
        dil = dx[U, x] + dy[V, x] + dz[1, at, :width]
        s1 = viscosity * (2.0 * dx[U, x] - (2.0 / 3.0) * dil)
        s2 = viscosity * (dx[V, x] + dy[U, x])
        s3 = viscosity * (dx[W, x] + dz[0, at, :width])
        m = density * u
        total = m * (enthalpy * t + 0.5 * (u * u + v * v + w * w))
        flux[0, x] = m
        flux[1, x] = m * u + density * t - s1
        flux[2, x] = m * v - s2
        flux[3, x] = m * w - s3
        flux[4, x] = total - (s1 * u + s2 * v + s3 * w) - conduction * viscosity * dx[T, x]
        return carry

    lax.fori_loop(0, CX, plane, 0)

    def sums(f, carry):
        for chunk in row_chunks(rows):
            halo_sums(flux, f, chunk, up, down)
        return carry

    lax.fori_loop(0, 5, sums, 0)


def kernel_flux_yz(
    parity, own, second, peer_first, peer_second, mate, across_second, dz, dx, dy, mu,
    y_high, y_low, z_high, z_low, f_high, f_low, part, part_mate,
    dz_more, dy_peer, flux, flux_y,
):
    rows, width = own.shape[2:]
    odd = parity[0]
    for f in range(2):
        values = jnp.concatenate(
            [flat(own[V + f]), flat(peer_second[f]), flat(mate[V + f]), flat(across_second[f])],
            axis=1,
        )
        dz_more[f] = right_product(values, z_high[odd], z_low[odd])
    dy_peer[0] = left_product(y_high[...], y_low[...], flat(peer_second[0]))
    dy_peer[1] = left_product(y_high[...], y_low[...], flat(peer_first[1]))

    def span_flux(at, lanes, u, w, v, t, density, viscosity, yv, yw):
        s1 = viscosity * dz[0, at, lanes]
        s2 = viscosity * (dz_more[0, at, lanes] + yw)
        s3 = viscosity * ((4.0 / 3.0) * dz[1, at, lanes] - (2.0 / 3.0) * yv)
        m = density * w
        total = m * (enthalpy * t + 0.5 * (u * u + v * v + w * w))
        flux[0, at, lanes] = m
        flux[1, at, lanes] = m * u - s1
        flux[2, at, lanes] = m * v - s2
        flux[3, at, lanes] = m * w + density * t - s3
        flux[4, at, lanes] = (
            total
            - (s1 * u + s2 * v + s3 * w)
            - conduction * viscosity * dz_more[1, at, lanes]
        )

    def plane(x, carry):
        at = pl.ds(pl.multiple_of(x * rows, rows), rows)
        here = slice(0, width)
        u, w, v, t = (own[f, x] for f in range(4))
        density = second[2, x]
        viscosity = mu[x]
        span_flux(at, here, u, w, v, t, density, viscosity, dy[V, x], dy[W, x])
        dil = dx[U, x] + dy[V, x] + dz[1, at, here]
        s1 = viscosity * (dy[U, x] + dx[V, x])
        s2 = viscosity * (2.0 * dy[V, x] - (2.0 / 3.0) * dil)
        s3 = viscosity * (dy[W, x] + dz_more[0, at, here])
        m = density * v
        total = m * (enthalpy * t + 0.5 * (u * u + v * v + w * w))
        flux_y[0, at, :] = m
        flux_y[1, at, :] = m * u - s1
        flux_y[2, at, :] = m * v + density * t - s2
        flux_y[3, at, :] = m * w - s3
        flux_y[4, at, :] = (
            total - (s1 * u + s2 * v + s3 * w) - conduction * viscosity * dy[T, x]
        )
        t = peer_second[1, x]
        viscosity = shear_resistance_reference * jnp.exp(sutherland_power_law * jnp.log(t))
        span_flux(
            at, slice(width, 2 * width), peer_first[0, x], peer_first[1, x],
            peer_second[0, x], t, peer_second[2, x], viscosity,
            dy_peer[0, at, :], dy_peer[1, at, :],
        )
        return carry

    lax.fori_loop(0, CX, plane, 0)
    shape = own.shape[1:]
    for f in range(5):
        spread = right_product(flux[f], f_high[odd], f_low[odd])
        local = left_product(y_high[...], y_low[...], flux_y[f])
        part[f] = (spread[:, :width] + local).reshape(shape)
        part_mate[f] = spread[:, width:].reshape(shape)


def kernel_corrections(
    parity, own, peer_first, third, peer_third, part, part_mate, f_high, f_low,
    total, for_mate,
):
    width = own.shape[-1]
    odd = parity[0]
    shape = own.shape[1:]
    for f in (0, 2):
        total[f] = part[f]
        for_mate[f] = part_mate[f]
    pairs = ((own, third), (peer_first, peer_third))
    for f in (1, 3, 4):
        sides = []
        for speeds, shared in pairs:
            if f == 1:
                value = -shared[1]
            elif f == 3:
                value = shared[0]
            else:
                value = shared[0] * speeds[W] - shared[1] * speeds[U]
            sides.append(flat(value))
        spread = right_product(jnp.concatenate(sides, axis=1), f_high[odd], f_low[odd])
        total[f] = part[f] + spread[:, :width].reshape(shape)
        for_mate[f] = part_mate[f] + spread[:, width:].reshape(shape)


def kernel_flux_x_gradient(flux, before, after, result):
    def field(f, carry):
        for rows in row_chunks(flux.shape[2]):
            derived = compact_x(extended(before, flux, after, f, rows))
            for x in range(CX):
                result[f, x, rows, :] = derived[x]
        return carry

    lax.fori_loop(0, 5, field, 0)


def kernel_finish(rho, mom, ene, total, from_mate, stream, tendency, advanced):
    def plane(x, carry):
        for f in range(5):
            value = -(total[f, x] + from_mate[f, x] + stream[f, x])
            old = rho[x] if f == 0 else ene[x] if f == 4 else mom[f - 1, x]
            tendency[f, x] = value
            advanced[f, x] = old + section_step * value
        return carry

    lax.fori_loop(0, CX, plane, 0)


def call(kernel, outputs, operands, scratch=(), scalar=False, outside=False, cost=1.0):
    space = pl.ANY if outside else pltpu.VMEM
    in_specs = [pl.BlockSpec(memory_space=space) for _ in operands]
    if scalar:
        in_specs[0] = pl.BlockSpec(memory_space=pltpu.SMEM)
    work = int(cost * 1e9)
    return pl.pallas_call(
        kernel,
        out_shape=[jax.ShapeDtypeStruct(shape, F32) for shape in outputs],
        in_specs=in_specs,
        out_specs=[pl.BlockSpec(memory_space=pltpu.VMEM) for _ in outputs],
        scratch_shapes=list(scratch),
        cost_estimate=pl.CostEstimate(flops=work, bytes_accessed=work // 300, transcendentals=0),
        compiler_params=pltpu.CompilerParams(vmem_limit_bytes=24 * 1024 * 1024),
    )(*operands)


def fast_device(mass_per_volume, momentum, energy):
    rho = jnp.transpose(mass_per_volume, (0, 2, 1))
    mom = jnp.transpose(momentum, (0, 1, 3, 2))
    ene = jnp.transpose(energy, (0, 2, 1))
    _, rows, width = rho.shape
    length = 4 * width
    parity = lax.rem(lax.axis_index("gy").astype(jnp.int32), 2).reshape(1)
    z_high, z_low = span_blocks(length, PLACES, PLACES[:2])
    f_high, f_low = span_blocks(length, PLACES[:2], (0, 1))
    y_high, y_low = halves(np.kron(np.eye(CX, dtype=np.float32), pitch_matrix(rows, CY)))
    block = (CX, rows, width)
    sums = (2, rows, width)
    points = CX * rows
    devices = lax.axis_size("gx")
    ring_up = [(i, (i + 1) % devices) for i in range(devices)]
    ring_down = [(j, i) for i, j in ring_up]
    to_mate = [(i, i ^ 1) for i in range(4)]
    to_peer = [(i, i ^ 2) for i in range(4)]

    own, first, second, up, down = call(
        kernel_primitives,
        [(4,) + block, (2,) + block, (3,) + block, (4,) + sums, (4,) + sums],
        (rho, mom, ene),
        scratch=(
            pltpu.VMEM(block, F32),
            pltpu.VMEM((3,) + block, F32),
            pltpu.VMEM(block, F32),
            pltpu.SemaphoreType.DMA((3,)),
        ),
        outside=True,
    )
    peer_first = lax.ppermute(first, "gy", to_peer)
    before = lax.ppermute(up, "gx", ring_up)
    after = lax.ppermute(down, "gx", ring_down)
    mate = lax.ppermute(own, "gy", to_mate)
    peer_second = lax.ppermute(second, "gy", to_peer)
    dy, mu = call(kernel_pitch_gradients, [(4,) + block, block], (own, y_high, y_low))
    across_first = lax.ppermute(peer_first, "gy", to_mate)
    dx, third = call(
        kernel_stream_gradients, [(4,) + block, (2,) + block], (own, before, after, mu)
    )
    peer_third = lax.ppermute(third, "gy", to_peer)
    dz, flux, flux_up, flux_down = call(
        kernel_flux_x,
        [(2, points, 2 * width), (5,) + block, (5,) + sums, (5,) + sums],
        (parity, own, second, peer_first, mate, across_first, dx, dy, mu, z_high, z_low),
        scalar=True,
    )
    flux_before = lax.ppermute(flux_up, "gx", ring_up)
    flux_after = lax.ppermute(flux_down, "gx", ring_down)
    across_second = lax.ppermute(peer_second, "gy", to_mate)
    part, part_mate = call(
        kernel_flux_yz,
        [(5,) + block, (5,) + block],
        (
            parity, own, second, peer_first, peer_second, mate, across_second, dz, dx, dy, mu,
            y_high, y_low, z_high, z_low, f_high, f_low,
        ),
        scratch=(
            pltpu.VMEM((2, points, 2 * width), F32),
            pltpu.VMEM((2, points, width), F32),
            pltpu.VMEM((5, points, 2 * width), F32),
            pltpu.VMEM((5, points, width), F32),
        ),
        scalar=True,
        cost=3.0,
    )
    (stream,) = call(
        kernel_flux_x_gradient, [(5,) + block], (flux, flux_before, flux_after)
    )
    total, for_mate = call(
        kernel_corrections,
        [(5,) + block, (5,) + block],
        (parity, own, peer_first, third, peer_third, part, part_mate, f_high, f_low),
        scalar=True,
    )
    from_mate = lax.ppermute(for_mate, "gy", to_mate)
    tendency, advanced = call(
        kernel_finish,
        [(5,) + block, (5,) + block],
        (rho, mom, ene, total, from_mate, stream),
    )
    return (
        jnp.transpose(tendency, (0, 1, 3, 2)),
        jnp.transpose(advanced, (0, 1, 3, 2)),
    )


def padded(array, sides, width):
    for axis, dim in sides:
        devices, length = (lax.axis_size(axis), array.shape[dim])
        up = [(i, (i + 1) % devices) for i in range(devices)]
        down = [(j, i) for i, j in up]
        last = lax.slice_in_dim(array, length - width, length, axis=dim)
        initial = lax.slice_in_dim(array, 0, width, axis=dim)
        before = lax.ppermute(last, axis, up)
        after = lax.ppermute(initial, axis, down)
        array = jnp.concatenate([before, array, after], axis=dim)
    return array


def right_side(conserved, gradients_of, derive_x, derive_y, derive_z):
    mass_per_volume = conserved[0]
    momentum = conserved[1:4]
    energy = conserved[4]
    local_speed_vector = momentum / mass_per_volume
    kinetic = 0.5 * jnp.sum(momentum * local_speed_vector, axis=0)
    normal_force_per_area = (heat_ratio - 1.0) * (energy - kinetic)
    thermal_state = normal_force_per_area / mass_per_volume
    basic_quantities = jnp.concatenate([local_speed_vector, thermal_state[None]], 0)
    gradients = gradients_of(basic_quantities)
    shear_resistance = shear_resistance_reference * jnp.power(thermal_state, sutherland_power_law)
    conductivity = shear_resistance * heat_ratio / ((heat_ratio - 1.0) * prandtl)
    dilatation = gradients[0][0] + gradients[1][1] + gradients[2][2]
    derivers = (derive_x, derive_y, derive_z)
    accumulated = None
    for direction in range(3):
        stress_column = [
            shear_resistance * (gradients[direction][component] + gradients[component][direction])
            for component in range(3)
        ]
        stress_column[direction] = (
            stress_column[direction] - 2.0 / 3.0 * shear_resistance * dilatation
        )
        fluxes = [momentum[direction]]
        for component in range(3):
            moment_flux = (
                momentum[component] * local_speed_vector[direction] - stress_column[component]
            )
            if component == direction:
                moment_flux = moment_flux + normal_force_per_area
            fluxes.append(moment_flux)
        work_term = (
            stress_column[0] * local_speed_vector[0]
            + stress_column[1] * local_speed_vector[1]
            + stress_column[2] * local_speed_vector[2]
        )
        fluxes.append(
            (energy + normal_force_per_area) * local_speed_vector[direction]
            - work_term
            - conductivity * gradients[direction][3]
        )
        divergence_part = derivers[direction](jnp.stack(fluxes))
        accumulated = divergence_part if accumulated is None else accumulated + divergence_part
    return -accumulated


def plain_device(mass_per_volume, momentum, energy):
    conserved = jnp.concatenate([mass_per_volume[None], momentum, energy[None]], 0)
    highest = lax.Precision.HIGHEST
    x_matrix = jnp.asarray(compact_matrix(CX, HALO))
    z_matrix = jnp.asarray(span_matrix(NZ))

    def apply_x(extended):
        return jnp.einsum("il,flab->fiab", x_matrix, extended, precision=highest)

    def flux_x(values):
        return apply_x(padded(values, (("gx", 1),), HALO))

    y_matrix = jnp.asarray(pitch_matrix(conserved.shape[3], CY))

    def apply_y(values):
        return jnp.einsum("fabk,jk->fabj", values, y_matrix, precision=highest)

    def derive_span(values):
        lines = jnp.transpose(
            lax.all_to_all(values, "gy", split_axis=3, concat_axis=2, tiled=True), (0, 1, 3, 2)
        )
        derived = jnp.einsum("fack,jk->facj", lines, z_matrix, precision=highest)
        returned = lax.all_to_all(derived, "gy", split_axis=3, concat_axis=2, tiled=True)
        return jnp.transpose(returned, (0, 1, 3, 2))

    def gradients_of(basic_quantities):
        extended = padded(basic_quantities, (("gx", 1),), HALO)
        return (apply_x(extended), apply_y(basic_quantities), derive_span(basic_quantities))

    tendency = right_side(conserved, gradients_of, flux_x, apply_y, derive_span)
    advanced = conserved + section_step * tendency
    return (tendency, advanced)


def per_device(mass_per_volume, momentum, energy):
    planes, width, rows = mass_per_volume.shape
    fits = planes == CX and width % 128 == 0 and rows <= 32 and rows % CY == 0
    if fits and lax.axis_size("gy") == 4:
        return fast_device(mass_per_volume, momentum, energy)
    return plain_device(mass_per_volume, momentum, energy)


def solution(mesh):
    in_specs = (P("gx", "gy", None), P(None, "gx", "gy", None), P("gx", "gy", None))
    out_specs = (P(None, "gx", "gy", None), P(None, "gx", "gy", None))
    return jax.shard_map(
        per_device, mesh=mesh, in_specs=in_specs, out_specs=out_specs, check_vma=False
    )
```

```python
import functools

import jax
import jax.numpy as jnp
import numpy as np
from jax import lax
from jax.experimental import pallas as pl
from jax.experimental.pallas import tpu as pltpu
from jax.sharding import PartitionSpec as P

CX = 8
CY = 8
NZ = 512
HALO = 4


heat_ratio = 1.4
shear_resistance_reference = 0.08
sutherland_power_law = 0.7
prandtl = 0.72
section_step = 0.05
compact_alpha = 1.0 / 3.0
compact_near = 14.0 / 9.0
compact_far = 1.0 / 9.0

conduction = heat_ratio / ((heat_ratio - 1.0) * prandtl)
enthalpy = heat_ratio / (heat_ratio - 1.0)


def tridiagonal_inverse_product(length, stencil):
    solved = np.array(stencil)
    upper_ratio = np.zeros(length)
    for row_index in range(length):
        if row_index == 0:
            pivot_value = 1.0
            solved[row_index] = solved[row_index] / pivot_value
        else:
            pivot_value = 1.0 - compact_alpha * upper_ratio[row_index - 1]
            solved[row_index] = (
                solved[row_index] - compact_alpha * solved[row_index - 1]
            ) / pivot_value
        upper_ratio[row_index] = compact_alpha / pivot_value
    for row_index in range(length - 2, -1, -1):
        solved[row_index] = solved[row_index] - upper_ratio[row_index] * solved[row_index + 1]
    return solved


def exact_compact_matrix(block_size, margin):
    length = block_size + 2 * margin
    stencil = compact_near / 2.0 * (np.eye(length, k=1) - np.eye(length, k=-1))
    stencil = stencil + compact_far / 4.0 * (np.eye(length, k=2) - np.eye(length, k=-2))
    inverse_product = tridiagonal_inverse_product(length, stencil)
    return inverse_product[margin : margin + block_size]


def compact_matrix(block_size, margin):
    return exact_compact_matrix(block_size, margin).astype(np.float32)


def pitch_matrix(total, block_size):
    matrix = compact_matrix(block_size, HALO)
    result = np.zeros((total, total), np.float32)
    rows_all = np.arange(total)
    block_start = rows_all // block_size * block_size
    for offset in range(block_size + 2 * HALO):
        columns = (block_start - HALO + offset) % total
        result[rows_all, columns] += matrix[rows_all % block_size, offset]
    return result


def span_matrix(total):
    offsets = np.arange(total)[:, None] - np.arange(total)[None, :]
    angles = np.pi * offsets / total
    signs = np.where(offsets % 2 == 0, 1.0, -1.0)
    sines = np.where(offsets == 0, 1.0, np.sin(angles))
    result = np.where(offsets == 0, 0.0, np.pi / total * signs * np.cos(angles) / sines)
    return result.astype(np.float32)


F32 = jnp.float32
BF16 = jnp.bfloat16
U, W, V, T, R = range(5)
PLACES = (0, 2, 1, 3)
HALF = CX // 2


def halves(matrix):
    high = np.asarray(matrix, np.float32).astype(BF16)
    low = (matrix - high.astype(np.float32)).astype(BF16)
    return jnp.asarray(high), jnp.asarray(low)


def span_blocks(length, sources, targets):
    width = length // 4
    matrix = span_matrix(length).T
    both = []
    for core in range(2):
        columns = []
        for target in targets:
            to = core ^ target
            columns.append(
                np.concatenate(
                    [
                        matrix[
                            (core ^ source) * width : (core ^ source) * width + width,
                            to * width : to * width + width,
                        ]
                        for source in sources
                    ],
                    axis=0,
                )
            )
        both.append(np.concatenate(columns, axis=1))
    return halves(np.stack(both))


def halo_basis():
    matrix = exact_compact_matrix(CX, HALO)
    left = matrix[:, :HALO]
    basis = np.linalg.svd(left)[2][:2]
    inner = left @ basis.T
    outer = -inner[::-1]
    return basis, np.concatenate(
        [inner, matrix[:, HALO : HALO + CX], outer[:, ::-1]], axis=1
    )


def split(values):
    high = values.astype(BF16)
    low = (values - high.astype(F32)).astype(BF16)
    return high, low


def dot(a, b):
    return jnp.dot(a, b, preferred_element_type=F32)


def right_product(values, matrix_high, matrix_low):
    high, low = split(values)
    return dot(high, matrix_high) + dot(low, matrix_high) + dot(high, matrix_low)


def left_product(matrix_high, matrix_low, values):
    high, low = split(values)
    return dot(matrix_high, high) + dot(matrix_high, low) + dot(matrix_low, high)


def compact_x(planes):
    matrix = halo_basis()[1]
    length = CX + 4
    half = length // 2
    odd = [planes[l] - planes[length - 1 - l] for l in range(half)]
    even = [planes[l] + planes[length - 1 - l] for l in range(half)]
    result = [None] * CX
    for i in range(HALF):
        first = None
        second = None
        for l in range(half):
            a = float(0.5 * (matrix[i, l] - matrix[i, length - 1 - l]))
            b = float(0.5 * (matrix[i, l] + matrix[i, length - 1 - l]))
            first = a * odd[l] if first is None else first + a * odd[l]
            second = b * even[l] if second is None else second + b * even[l]
        result[i] = first + second
        result[CX - 1 - i] = first - second
    return result


def extended(before, own, after, f, rows):
    return (
        [before[f, 0, rows, :], before[f, 1, rows, :]]
        + [own[f, l, rows, :] for l in range(CX)]
        + [after[f, 1, rows, :], after[f, 0, rows, :]]
    )


def halo_sums(values, f, rows, up, down):
    basis = halo_basis()[0]
    for k in range(2):
        top = None
        bottom = None
        for l in range(HALO):
            a = float(basis[k, l]) * values[f, CX - HALO + l, rows, :]
            b = float(basis[k, l]) * values[f, HALO - 1 - l, rows, :]
            top = a if top is None else top + a
            bottom = b if bottom is None else bottom + b
        up[f, k, rows, :] = top
        down[f, k, rows, :] = bottom


def row_chunks(rows):
    return [slice(start, start + 8) for start in range(0, rows, 8)]


def flat(values):
    return values.reshape(-1, values.shape[-1])


def kernel_primitives(
    rho_in, mom_in, ene_in, conserved, own, first, up, down, arrived
):
    rho = conserved.at[0]
    mom = conserved.at[1:4]
    ene = conserved.at[4]
    copies = [
        pltpu.make_async_copy(source, target, arrived.at[k])
        for k, (source, target) in enumerate(((rho_in, rho), (mom_in, mom), (ene_in, ene)))
    ]
    for copy in copies:
        copy.start()
    for copy in copies:
        copy.wait()

    def plane(x, carry):
        density = rho[x]
        inverse = 1.0 / density
        u = mom[0, x] * inverse
        v = mom[1, x] * inverse
        w = mom[2, x] * inverse
        kinetic = 0.5 * (mom[0, x] * u + mom[1, x] * v + mom[2, x] * w)
        temperature = (heat_ratio - 1.0) * (ene[x] - kinetic) * inverse
        own[U, x] = u
        own[W, x] = w
        own[V, x] = v
        own[T, x] = temperature
        first[0, x] = u
        first[1, x] = w
        return carry

    lax.fori_loop(0, CX, plane, 0)

    def sums(f, carry):
        for rows in row_chunks(rho.shape[1]):
            halo_sums(own, f, rows, up, down)
        return carry

    lax.fori_loop(0, 4, sums, 0)


def kernel_pitch_gradients(own, conserved, y_high, y_low, dy, mu, second):
    for f in range(4):
        dy[f] = left_product(y_high[...], y_low[...], flat(own[f])).reshape(own.shape[1:])

    def plane(x, carry):
        mu[x] = shear_resistance_reference * jnp.exp(
            sutherland_power_law * jnp.log(own[T, x])
        )
        second[0, x] = own[V, x]
        second[1, x] = own[T, x]
        second[2, x] = conserved[0, x]
        return carry

    lax.fori_loop(0, CX, plane, 0)


def kernel_stream_gradients(own, before, after, mu, dx, third):
    def field(f, carry):
        for rows in row_chunks(own.shape[2]):
            derived = compact_x(extended(before, own, after, f, rows))
            for x in range(CX):
                dx[f, x, rows, :] = derived[x]
        return carry

    lax.fori_loop(0, 4, field, 0)

    def plane(x, carry):
        third[0, x] = (2.0 / 3.0) * mu[x] * dx[U, x]
        third[1, x] = mu[x] * dx[W, x]
        return carry

    lax.fori_loop(0, CX, plane, 0)


def kernel_flux_x(
    parity, own, second, peer_first, mate, across_first, dx, dy, mu, z_high, z_low,
    dz, flux, up, down,
):
    width = own.shape[-1]
    odd = parity[0]
    for f in range(2):
        values = jnp.concatenate(
            [flat(own[f]), flat(peer_first[f]), flat(mate[f]), flat(across_first[f])], axis=1
        )
        dz[f] = right_product(values, z_high[odd], z_low[odd])

    rows = own.shape[2]

    def plane(x, carry):
        at = pl.ds(pl.multiple_of(x * rows, rows), rows)
        u, w, v, t = (own[f, x] for f in range(4))
        density = second[2, x]
        viscosity = mu[x]
        dil = dx[U, x] + dy[V, x] + dz[1, at, :width]
        s1 = viscosity * (2.0 * dx[U, x] - (2.0 / 3.0) * dil)
        s2 = viscosity * (dx[V, x] + dy[U, x])
        s3 = viscosity * (dx[W, x] + dz[0, at, :width])
        m = density * u
        total = m * (enthalpy * t + 0.5 * (u * u + v * v + w * w))
        flux[0, x] = m
        flux[1, x] = m * u + density * t - s1
        flux[2, x] = m * v - s2
        flux[3, x] = m * w - s3
        flux[4, x] = total - (s1 * u + s2 * v + s3 * w) - conduction * viscosity * dx[T, x]
        return carry

    lax.fori_loop(0, CX, plane, 0)

    def sums(f, carry):
        for chunk in row_chunks(rows):
            halo_sums(flux, f, chunk, up, down)
        return carry

    lax.fori_loop(0, 5, sums, 0)


def kernel_peer(peer_first, peer_second, flux, y_high, y_low, for_v, for_t, dy_peer):
    for_v[...] = peer_second[0]
    for_t[...] = peer_second[1]
    dy_peer[0] = left_product(y_high[...], y_low[...], flat(peer_second[0]))
    dy_peer[1] = left_product(y_high[...], y_low[...], flat(peer_first[1]))


def kernel_flux_yz(
    parity, own, second, peer_first, peer_second, mate, across_v, across_t, dy_peer,
    dz, dx, dy, mu, y_high, y_low, z_high, z_low, f_high, f_low, part, part_mate,
    dz_more, flux, flux_y,
):
    rows, width = own.shape[2:]
    odd = parity[0]
    for f, across in enumerate((across_v, across_t)):
        values = jnp.concatenate(
            [flat(own[V + f]), flat(peer_second[f]), flat(mate[V + f]), flat(across[...])],
            axis=1,
        )
        dz_more[f] = right_product(values, z_high[odd], z_low[odd])

    def span_flux(at, lanes, u, w, v, t, density, viscosity, yv, yw):
        s1 = viscosity * dz[0, at, lanes]
        s2 = viscosity * (dz_more[0, at, lanes] + yw)
        s3 = viscosity * ((4.0 / 3.0) * dz[1, at, lanes] - (2.0 / 3.0) * yv)
        m = density * w
        total = m * (enthalpy * t + 0.5 * (u * u + v * v + w * w))
        flux[0, at, lanes] = m
        flux[1, at, lanes] = m * u - s1
        flux[2, at, lanes] = m * v - s2
        flux[3, at, lanes] = m * w + density * t - s3
        flux[4, at, lanes] = (
            total
            - (s1 * u + s2 * v + s3 * w)
            - conduction * viscosity * dz_more[1, at, lanes]
        )

    def plane(x, carry):
        at = pl.ds(pl.multiple_of(x * rows, rows), rows)
        here = slice(0, width)
        u, w, v, t = (own[f, x] for f in range(4))
        density = second[2, x]
        viscosity = mu[x]
        span_flux(at, here, u, w, v, t, density, viscosity, dy[V, x], dy[W, x])
        dil = dx[U, x] + dy[V, x] + dz[1, at, here]
        s1 = viscosity * (dy[U, x] + dx[V, x])
        s2 = viscosity * (2.0 * dy[V, x] - (2.0 / 3.0) * dil)
        s3 = viscosity * (dy[W, x] + dz_more[0, at, here])
        m = density * v
        total = m * (enthalpy * t + 0.5 * (u * u + v * v + w * w))
        flux_y[0, at, :] = m
        flux_y[1, at, :] = m * u - s1
        flux_y[2, at, :] = m * v + density * t - s2
        flux_y[3, at, :] = m * w - s3
        flux_y[4, at, :] = (
            total - (s1 * u + s2 * v + s3 * w) - conduction * viscosity * dy[T, x]
        )
        t = peer_second[1, x]
        viscosity = shear_resistance_reference * jnp.exp(sutherland_power_law * jnp.log(t))
        span_flux(
            at, slice(width, 2 * width), peer_first[0, x], peer_first[1, x],
            peer_second[0, x], t, peer_second[2, x], viscosity,
            dy_peer[0, at, :], dy_peer[1, at, :],
        )
        return carry

    lax.fori_loop(0, CX, plane, 0)
    shape = own.shape[1:]
    for f in range(5):
        spread = right_product(flux[f], f_high[odd], f_low[odd])
        local = left_product(y_high[...], y_low[...], flux_y[f])
        part[f] = (spread[:, :width] + local).reshape(shape)
        part_mate[f] = spread[:, width:].reshape(shape)


def kernel_corrections(
    parity, own, peer_first, third, peer_third, part, part_mate, stream, f_high, f_low,
    total, for_mate,
):
    width = own.shape[-1]
    odd = parity[0]
    shape = own.shape[1:]
    for f in (0, 2):
        total[f] = part[f] + stream[f]
        for_mate[f] = part_mate[f]
    pairs = ((own, third), (peer_first, peer_third))
    for f in (1, 3, 4):
        sides = []
        for speeds, shared in pairs:
            if f == 1:
                value = -shared[1]
            elif f == 3:
                value = shared[0]
            else:
                value = shared[0] * speeds[W] - shared[1] * speeds[U]
            sides.append(flat(value))
        spread = right_product(jnp.concatenate(sides, axis=1), f_high[odd], f_low[odd])
        total[f] = part[f] + stream[f] + spread[:, :width].reshape(shape)
        for_mate[f] = part_mate[f] + spread[:, width:].reshape(shape)


def kernel_flux_x_gradient(flux, before, after, result):
    def field(f, carry):
        for rows in row_chunks(flux.shape[2]):
            derived = compact_x(extended(before, flux, after, f, rows))
            for x in range(CX):
                result[f, x, rows, :] = derived[x]
        return carry

    lax.fori_loop(0, 5, field, 0)


def kernel_finish(conserved, total, from_mate, tendency, advanced):
    def plane(x, carry):
        for f in range(5):
            value = -(total[f, x] + from_mate[f, x])
            tendency[f, x] = value
            advanced[f, x] = conserved[f, x] + section_step * value
        return carry

    lax.fori_loop(0, CX, plane, 0)


def call(kernel, outputs, operands, scratch=(), scalar=False, outside=False, cost=0.02):
    space = pltpu.HBM if outside else pltpu.VMEM
    in_specs = [pl.BlockSpec(memory_space=space) for _ in operands]
    if scalar:
        in_specs[0] = pl.BlockSpec(memory_space=pltpu.SMEM)
    work = int(cost * 1e9)
    return pl.pallas_call(
        kernel,
        out_shape=[jax.ShapeDtypeStruct(shape, F32) for shape in outputs],
        in_specs=in_specs,
        out_specs=[pl.BlockSpec(memory_space=pltpu.VMEM) for _ in outputs],
        scratch_shapes=list(scratch),
        cost_estimate=pl.CostEstimate(flops=work, bytes_accessed=work // 300, transcendentals=0),
        compiler_params=pltpu.CompilerParams(vmem_limit_bytes=24 * 1024 * 1024),
    )(*operands)


def fast_device(mass_per_volume, momentum, energy):
    rho = jnp.transpose(mass_per_volume, (0, 2, 1))
    mom = jnp.transpose(momentum, (0, 1, 3, 2))
    ene = jnp.transpose(energy, (0, 2, 1))
    _, rows, width = rho.shape
    length = 4 * width
    parity = lax.rem(lax.axis_index("gy").astype(jnp.int32), 2).reshape(1)
    z_high, z_low = span_blocks(length, PLACES, PLACES[:2])
    f_high, f_low = span_blocks(length, PLACES[:2], (0, 1))
    y_high, y_low = halves(np.kron(np.eye(CX, dtype=np.float32), pitch_matrix(rows, CY)))
    block = (CX, rows, width)
    sums = (2, rows, width)
    points = CX * rows
    devices = lax.axis_size("gx")
    ring_up = [(i, (i + 1) % devices) for i in range(devices)]
    ring_down = [(j, i) for i, j in ring_up]
    to_mate = [(i, i ^ 1) for i in range(4)]
    to_peer = [(i, i ^ 2) for i in range(4)]

    conserved, own, first, up, down = call(
        kernel_primitives,
        [(5,) + block, (4,) + block, (2,) + block, (4,) + sums, (4,) + sums],
        (rho, mom, ene),
        scratch=(pltpu.SemaphoreType.DMA((3,)),),
        outside=True,
    )
    peer_first = lax.ppermute(first, "gy", to_peer)
    before = lax.ppermute(up, "gx", ring_up)
    after = lax.ppermute(down, "gx", ring_down)
    mate = lax.ppermute(own, "gy", to_mate)
    dy, mu, second = call(
        kernel_pitch_gradients,
        [(4,) + block, block, (3,) + block],
        (own, conserved, y_high, y_low),
    )
    peer_second = lax.ppermute(second, "gy", to_peer)
    peer_first, before, after = lax.optimization_barrier((peer_first, before, after))
    across_first = lax.ppermute(peer_first, "gy", to_mate)
    dx, third = call(
        kernel_stream_gradients, [(4,) + block, (2,) + block], (own, before, after, mu)
    )
    peer_third = lax.ppermute(third, "gy", to_peer)
    dz, flux, flux_up, flux_down = call(
        kernel_flux_x,
        [(2, points, 2 * width), (5,) + block, (5,) + sums, (5,) + sums],
        (parity, own, second, peer_first, mate, across_first, dx, dy, mu, z_high, z_low),
        scalar=True,
    )
    flux_before = lax.ppermute(flux_up, "gx", ring_up)
    flux_after = lax.ppermute(flux_down, "gx", ring_down)
    for_v, for_t, dy_peer = call(
        kernel_peer,
        [block, block, (2, points, width)],
        (peer_first, peer_second, flux, y_high, y_low),
    )
    across_v = lax.ppermute(for_v, "gy", to_mate)
    across_t = lax.ppermute(for_t, "gy", to_mate)
    part, part_mate = call(
        kernel_flux_yz,
        [(5,) + block, (5,) + block],
        (
            parity, own, second, peer_first, peer_second, mate, across_v, across_t, dy_peer,
            dz, dx, dy, mu, y_high, y_low, z_high, z_low, f_high, f_low,
        ),
        scratch=(
            pltpu.VMEM((2, points, 2 * width), F32),
            pltpu.VMEM((5, points, 2 * width), F32),
            pltpu.VMEM((5, points, width), F32),
        ),
        scalar=True,
        cost=0.02,
    )
    (stream,) = call(
        kernel_flux_x_gradient, [(5,) + block], (flux, flux_before, flux_after)
    )
    total, for_mate = call(
        kernel_corrections,
        [(5,) + block, (5,) + block],
        (parity, own, peer_first, third, peer_third, part, part_mate, stream, f_high, f_low),
        scalar=True,
    )
    from_mate = lax.ppermute(for_mate, "gy", to_mate)
    tendency, advanced = call(
        kernel_finish,
        [(5,) + block, (5,) + block],
        (conserved, total, from_mate),
    )
    return (
        jnp.transpose(tendency, (0, 1, 3, 2)),
        jnp.transpose(advanced, (0, 1, 3, 2)),
    )


def padded(array, sides, width):
    for axis, dim in sides:
        devices, length = (lax.axis_size(axis), array.shape[dim])
        up = [(i, (i + 1) % devices) for i in range(devices)]
        down = [(j, i) for i, j in up]
        last = lax.slice_in_dim(array, length - width, length, axis=dim)
        initial = lax.slice_in_dim(array, 0, width, axis=dim)
        before = lax.ppermute(last, axis, up)
        after = lax.ppermute(initial, axis, down)
        array = jnp.concatenate([before, array, after], axis=dim)
    return array


def right_side(conserved, gradients_of, derive_x, derive_y, derive_z):
    mass_per_volume = conserved[0]
    momentum = conserved[1:4]
    energy = conserved[4]
    local_speed_vector = momentum / mass_per_volume
    kinetic = 0.5 * jnp.sum(momentum * local_speed_vector, axis=0)
    normal_force_per_area = (heat_ratio - 1.0) * (energy - kinetic)
    thermal_state = normal_force_per_area / mass_per_volume
    basic_quantities = jnp.concatenate([local_speed_vector, thermal_state[None]], 0)
    gradients = gradients_of(basic_quantities)
    shear_resistance = shear_resistance_reference * jnp.power(thermal_state, sutherland_power_law)
    conductivity = shear_resistance * heat_ratio / ((heat_ratio - 1.0) * prandtl)
    dilatation = gradients[0][0] + gradients[1][1] + gradients[2][2]
    derivers = (derive_x, derive_y, derive_z)
    accumulated = None
    for direction in range(3):
        stress_column = [
            shear_resistance * (gradients[direction][component] + gradients[component][direction])
            for component in range(3)
        ]
        stress_column[direction] = (
            stress_column[direction] - 2.0 / 3.0 * shear_resistance * dilatation
        )
        fluxes = [momentum[direction]]
        for component in range(3):
            moment_flux = (
                momentum[component] * local_speed_vector[direction] - stress_column[component]
            )
            if component == direction:
                moment_flux = moment_flux + normal_force_per_area
            fluxes.append(moment_flux)
        work_term = (
            stress_column[0] * local_speed_vector[0]
            + stress_column[1] * local_speed_vector[1]
            + stress_column[2] * local_speed_vector[2]
        )
        fluxes.append(
            (energy + normal_force_per_area) * local_speed_vector[direction]
            - work_term
            - conductivity * gradients[direction][3]
        )
        divergence_part = derivers[direction](jnp.stack(fluxes))
        accumulated = divergence_part if accumulated is None else accumulated + divergence_part
    return -accumulated


def plain_device(mass_per_volume, momentum, energy):
    conserved = jnp.concatenate([mass_per_volume[None], momentum, energy[None]], 0)
    highest = lax.Precision.HIGHEST
    x_matrix = jnp.asarray(compact_matrix(CX, HALO))
    z_matrix = jnp.asarray(span_matrix(NZ))

    def apply_x(extended):
        return jnp.einsum("il,flab->fiab", x_matrix, extended, precision=highest)

    def flux_x(values):
        return apply_x(padded(values, (("gx", 1),), HALO))

    y_matrix = jnp.asarray(pitch_matrix(conserved.shape[3], CY))

    def apply_y(values):
        return jnp.einsum("fabk,jk->fabj", values, y_matrix, precision=highest)

    def derive_span(values):
        lines = jnp.transpose(
            lax.all_to_all(values, "gy", split_axis=3, concat_axis=2, tiled=True), (0, 1, 3, 2)
        )
        derived = jnp.einsum("fack,jk->facj", lines, z_matrix, precision=highest)
        returned = lax.all_to_all(derived, "gy", split_axis=3, concat_axis=2, tiled=True)
        return jnp.transpose(returned, (0, 1, 3, 2))

    def gradients_of(basic_quantities):
        extended = padded(basic_quantities, (("gx", 1),), HALO)
        return (apply_x(extended), apply_y(basic_quantities), derive_span(basic_quantities))

    tendency = right_side(conserved, gradients_of, flux_x, apply_y, derive_span)
    advanced = conserved + section_step * tendency
    return (tendency, advanced)


def per_device(mass_per_volume, momentum, energy):
    planes, width, rows = mass_per_volume.shape
    fits = planes == CX and width % 128 == 0 and rows <= 32 and rows % CY == 0
    if fits and lax.axis_size("gy") == 4:
        return fast_device(mass_per_volume, momentum, energy)
    return plain_device(mass_per_volume, momentum, energy)


def solution(mesh):
    in_specs = (P("gx", "gy", None), P(None, "gx", "gy", None), P("gx", "gy", None))
    out_specs = (P(None, "gx", "gy", None), P(None, "gx", "gy", None))
    return jax.shard_map(
        per_device, mesh=mesh, in_specs=in_specs, out_specs=out_specs, check_vma=False
    )
```

```python
import functools

import jax
import jax.numpy as jnp
import numpy as np
from jax import lax
from jax.experimental import pallas as pl
from jax.experimental.pallas import tpu as pltpu
from jax.sharding import PartitionSpec as P

CX = 8
CY = 8
NZ = 512
HALO = 4


heat_ratio = 1.4
shear_resistance_reference = 0.08
sutherland_power_law = 0.7
prandtl = 0.72
section_step = 0.05
compact_alpha = 1.0 / 3.0
compact_near = 14.0 / 9.0
compact_far = 1.0 / 9.0

conduction = heat_ratio / ((heat_ratio - 1.0) * prandtl)
enthalpy = heat_ratio / (heat_ratio - 1.0)


def tridiagonal_inverse_product(length, stencil):
    solved = np.array(stencil)
    upper_ratio = np.zeros(length)
    for row_index in range(length):
        if row_index == 0:
            pivot_value = 1.0
            solved[row_index] = solved[row_index] / pivot_value
        else:
            pivot_value = 1.0 - compact_alpha * upper_ratio[row_index - 1]
            solved[row_index] = (
                solved[row_index] - compact_alpha * solved[row_index - 1]
            ) / pivot_value
        upper_ratio[row_index] = compact_alpha / pivot_value
    for row_index in range(length - 2, -1, -1):
        solved[row_index] = solved[row_index] - upper_ratio[row_index] * solved[row_index + 1]
    return solved


def exact_compact_matrix(block_size, margin):
    length = block_size + 2 * margin
    stencil = compact_near / 2.0 * (np.eye(length, k=1) - np.eye(length, k=-1))
    stencil = stencil + compact_far / 4.0 * (np.eye(length, k=2) - np.eye(length, k=-2))
    inverse_product = tridiagonal_inverse_product(length, stencil)
    return inverse_product[margin : margin + block_size]


def compact_matrix(block_size, margin):
    return exact_compact_matrix(block_size, margin).astype(np.float32)


def pitch_matrix(total, block_size):
    matrix = compact_matrix(block_size, HALO)
    result = np.zeros((total, total), np.float32)
    rows_all = np.arange(total)
    block_start = rows_all // block_size * block_size
    for offset in range(block_size + 2 * HALO):
        columns = (block_start - HALO + offset) % total
        result[rows_all, columns] += matrix[rows_all % block_size, offset]
    return result


def span_matrix(total):
    offsets = np.arange(total)[:, None] - np.arange(total)[None, :]
    angles = np.pi * offsets / total
    signs = np.where(offsets % 2 == 0, 1.0, -1.0)
    sines = np.where(offsets == 0, 1.0, np.sin(angles))
    result = np.where(offsets == 0, 0.0, np.pi / total * signs * np.cos(angles) / sines)
    return result.astype(np.float32)


F32 = jnp.float32
BF16 = jnp.bfloat16
U, W, V, T, R = range(5)
PLACES = (0, 2, 1, 3)
HALF = CX // 2


def halves(matrix):
    high = np.asarray(matrix, np.float32).astype(BF16)
    low = (matrix - high.astype(np.float32)).astype(BF16)
    return jnp.asarray(high), jnp.asarray(low)


def span_blocks(length, sources, targets):
    width = length // 4
    matrix = span_matrix(length).T
    both = []
    for core in range(2):
        columns = []
        for target in targets:
            to = core ^ target
            columns.append(
                np.concatenate(
                    [
                        matrix[
                            (core ^ source) * width : (core ^ source) * width + width,
                            to * width : to * width + width,
                        ]
                        for source in sources
                    ],
                    axis=0,
                )
            )
        both.append(np.concatenate(columns, axis=1))
    return halves(np.stack(both))


def halo_basis():
    matrix = exact_compact_matrix(CX, HALO)
    left = matrix[:, :HALO]
    basis = np.linalg.svd(left)[2][:2]
    inner = left @ basis.T
    outer = -inner[::-1]
    return basis, np.concatenate(
        [inner, matrix[:, HALO : HALO + CX], outer[:, ::-1]], axis=1
    )


def split(values):
    high = values.astype(BF16)
    low = (values - high.astype(F32)).astype(BF16)
    return high, low


def dot(a, b):
    return jnp.dot(a, b, preferred_element_type=F32)


def right_product(values, matrix_high, matrix_low):
    high, low = split(values)
    return dot(high, matrix_high) + dot(low, matrix_high) + dot(high, matrix_low)


def left_product(matrix_high, matrix_low, values):
    high, low = split(values)
    return dot(matrix_high, high) + dot(matrix_high, low) + dot(matrix_low, high)


def compact_x(planes):
    matrix = halo_basis()[1]
    length = CX + 4
    half = length // 2
    odd = [planes[l] - planes[length - 1 - l] for l in range(half)]
    even = [planes[l] + planes[length - 1 - l] for l in range(half)]
    result = [None] * CX
    for i in range(HALF):
        first = None
        second = None
        for l in range(half):
            a = float(0.5 * (matrix[i, l] - matrix[i, length - 1 - l]))
            b = float(0.5 * (matrix[i, l] + matrix[i, length - 1 - l]))
            first = a * odd[l] if first is None else first + a * odd[l]
            second = b * even[l] if second is None else second + b * even[l]
        result[i] = first + second
        result[CX - 1 - i] = first - second
    return result


def extended(before, own, after, f, rows):
    return (
        [before[f, 0, rows, :], before[f, 1, rows, :]]
        + [own[f, l, rows, :] for l in range(CX)]
        + [after[f, 1, rows, :], after[f, 0, rows, :]]
    )


def halo_sums(values, f, rows, up, down):
    basis = halo_basis()[0]
    for k in range(2):
        top = None
        bottom = None
        for l in range(HALO):
            a = float(basis[k, l]) * values[f, CX - HALO + l, rows, :]
            b = float(basis[k, l]) * values[f, HALO - 1 - l, rows, :]
            top = a if top is None else top + a
            bottom = b if bottom is None else bottom + b
        up[f, k, rows, :] = top
        down[f, k, rows, :] = bottom


def row_chunks(rows):
    return [slice(start, start + 8) for start in range(0, rows, 8)]


def flat(values):
    return values.reshape(-1, values.shape[-1])


def kernel_primitives(
    rho_in, mom_in, ene_in, conserved, own, first, up, down, arrived
):
    rho = conserved.at[0]
    mom = conserved.at[1:4]
    ene = conserved.at[4]
    copies = [
        pltpu.make_async_copy(source, target, arrived.at[k])
        for k, (source, target) in enumerate(((rho_in, rho), (mom_in, mom), (ene_in, ene)))
    ]
    for copy in copies:
        copy.start()
    for copy in copies:
        copy.wait()

    def plane(x, carry):
        density = rho[x]
        inverse = 1.0 / density
        u = mom[0, x] * inverse
        v = mom[1, x] * inverse
        w = mom[2, x] * inverse
        kinetic = 0.5 * (mom[0, x] * u + mom[1, x] * v + mom[2, x] * w)
        temperature = (heat_ratio - 1.0) * (ene[x] - kinetic) * inverse
        own[U, x] = u
        own[W, x] = w
        own[V, x] = v
        own[T, x] = temperature
        first[0, x] = u
        first[1, x] = w
        return carry

    lax.fori_loop(0, CX, plane, 0)

    def sums(f, carry):
        for rows in row_chunks(rho.shape[1]):
            halo_sums(own, f, rows, up, down)
        return carry

    lax.fori_loop(0, 4, sums, 0)


def kernel_pitch_gradients(own, conserved, y_high, y_low, dy, mu, second):
    for f in range(4):
        dy[f] = left_product(y_high[...], y_low[...], flat(own[f])).reshape(own.shape[1:])

    def plane(x, carry):
        mu[x] = shear_resistance_reference * jnp.exp(
            sutherland_power_law * jnp.log(own[T, x])
        )
        second[0, x] = own[V, x]
        second[1, x] = own[T, x]
        second[2, x] = conserved[0, x]
        return carry

    lax.fori_loop(0, CX, plane, 0)


def kernel_stream_gradients(own, before, after, mu, dx, third):
    def field(f, carry):
        for rows in row_chunks(own.shape[2]):
            derived = compact_x(extended(before, own, after, f, rows))
            for x in range(CX):
                dx[f, x, rows, :] = derived[x]
        return carry

    lax.fori_loop(0, 4, field, 0)

    def plane(x, carry):
        third[0, x] = (2.0 / 3.0) * mu[x] * dx[U, x]
        third[1, x] = mu[x] * dx[W, x]
        return carry

    lax.fori_loop(0, CX, plane, 0)


def kernel_flux_x(
    parity, own, second, peer_first, mate, across_first, dx, dy, mu, z_high, z_low,
    dz, flux, up, down,
):
    width = own.shape[-1]
    odd = parity[0]
    for f in range(2):
        values = jnp.concatenate(
            [flat(own[f]), flat(peer_first[f]), flat(mate[f]), flat(across_first[f])], axis=1
        )
        dz[f] = right_product(values, z_high[odd], z_low[odd])

    rows = own.shape[2]

    def plane(x, carry):
        at = pl.ds(pl.multiple_of(x * rows, rows), rows)
        u, w, v, t = (own[f, x] for f in range(4))
        density = second[2, x]
        viscosity = mu[x]
        dil = dx[U, x] + dy[V, x] + dz[1, at, :width]
        s1 = viscosity * (2.0 * dx[U, x] - (2.0 / 3.0) * dil)
        s2 = viscosity * (dx[V, x] + dy[U, x])
        s3 = viscosity * (dx[W, x] + dz[0, at, :width])
        m = density * u
        total = m * (enthalpy * t + 0.5 * (u * u + v * v + w * w))
        flux[0, x] = m
        flux[1, x] = m * u + density * t - s1
        flux[2, x] = m * v - s2
        flux[3, x] = m * w - s3
        flux[4, x] = total - (s1 * u + s2 * v + s3 * w) - conduction * viscosity * dx[T, x]
        return carry

    lax.fori_loop(0, CX, plane, 0)

    def sums(f, carry):
        for chunk in row_chunks(rows):
            halo_sums(flux, f, chunk, up, down)
        return carry

    lax.fori_loop(0, 5, sums, 0)


def kernel_peer(peer_first, peer_second, flux, y_high, y_low, for_v, for_t, dy_peer):
    for_v[...] = peer_second[0]
    for_t[...] = peer_second[1]
    dy_peer[0] = left_product(y_high[...], y_low[...], flat(peer_second[0]))
    dy_peer[1] = left_product(y_high[...], y_low[...], flat(peer_first[1]))


def kernel_flux_yz(
    parity, own, second, peer_first, peer_second, mate, across_v, across_t, dy_peer,
    dz, dx, dy, mu, y_high, y_low, z_high, z_low, f_high, f_low, part, part_mate,
    dz_more, flux, flux_y,
):
    rows, width = own.shape[2:]
    odd = parity[0]
    for f, across in enumerate((across_v, across_t)):
        values = jnp.concatenate(
            [flat(own[V + f]), flat(peer_second[f]), flat(mate[V + f]), flat(across[...])],
            axis=1,
        )
        dz_more[f] = right_product(values, z_high[odd], z_low[odd])

    def span_flux(at, lanes, u, w, v, t, density, viscosity, yv, yw):
        s1 = viscosity * dz[0, at, lanes]
        s2 = viscosity * (dz_more[0, at, lanes] + yw)
        s3 = viscosity * ((4.0 / 3.0) * dz[1, at, lanes] - (2.0 / 3.0) * yv)
        m = density * w
        total = m * (enthalpy * t + 0.5 * (u * u + v * v + w * w))
        flux[0, at, lanes] = m
        flux[1, at, lanes] = m * u - s1
        flux[2, at, lanes] = m * v - s2
        flux[3, at, lanes] = m * w + density * t - s3
        flux[4, at, lanes] = (
            total
            - (s1 * u + s2 * v + s3 * w)
            - conduction * viscosity * dz_more[1, at, lanes]
        )

    def plane(x, carry):
        at = pl.ds(pl.multiple_of(x * rows, rows), rows)
        here = slice(0, width)
        u, w, v, t = (own[f, x] for f in range(4))
        density = second[2, x]
        viscosity = mu[x]
        span_flux(at, here, u, w, v, t, density, viscosity, dy[V, x], dy[W, x])
        dil = dx[U, x] + dy[V, x] + dz[1, at, here]
        s1 = viscosity * (dy[U, x] + dx[V, x])
        s2 = viscosity * (2.0 * dy[V, x] - (2.0 / 3.0) * dil)
        s3 = viscosity * (dy[W, x] + dz_more[0, at, here])
        m = density * v
        total = m * (enthalpy * t + 0.5 * (u * u + v * v + w * w))
        flux_y[0, at, :] = m
        flux_y[1, at, :] = m * u - s1
        flux_y[2, at, :] = m * v + density * t - s2
        flux_y[3, at, :] = m * w - s3
        flux_y[4, at, :] = (
            total - (s1 * u + s2 * v + s3 * w) - conduction * viscosity * dy[T, x]
        )
        t = peer_second[1, x]
        viscosity = shear_resistance_reference * jnp.exp(sutherland_power_law * jnp.log(t))
        span_flux(
            at, slice(width, 2 * width), peer_first[0, x], peer_first[1, x],
            peer_second[0, x], t, peer_second[2, x], viscosity,
            dy_peer[0, at, :], dy_peer[1, at, :],
        )
        return carry

    lax.fori_loop(0, CX, plane, 0)
    shape = own.shape[1:]
    for f in range(5):
        spread = right_product(flux[f], f_high[odd], f_low[odd])
        local = left_product(y_high[...], y_low[...], flux_y[f])
        part[f] = (spread[:, :width] + local).reshape(shape)
        part_mate[f] = spread[:, width:].reshape(shape)


def kernel_corrections(
    parity, own, peer_first, third, peer_third, part, part_mate, stream, f_high, f_low,
    total, for_mate,
):
    width = own.shape[-1]
    odd = parity[0]
    shape = own.shape[1:]
    for f in (0, 2):
        total[f] = part[f] + stream[f]
        for_mate[f] = part_mate[f]
    pairs = ((own, third), (peer_first, peer_third))
    for f in (1, 3, 4):
        sides = []
        for speeds, shared in pairs:
            if f == 1:
                value = -shared[1]
            elif f == 3:
                value = shared[0]
            else:
                value = shared[0] * speeds[W] - shared[1] * speeds[U]
            sides.append(flat(value))
        spread = right_product(jnp.concatenate(sides, axis=1), f_high[odd], f_low[odd])
        total[f] = part[f] + stream[f] + spread[:, :width].reshape(shape)
        for_mate[f] = part_mate[f] + spread[:, width:].reshape(shape)


def kernel_flux_x_gradient(flux, before, after, result):
    def field(f, carry):
        for rows in row_chunks(flux.shape[2]):
            derived = compact_x(extended(before, flux, after, f, rows))
            for x in range(CX):
                result[f, x, rows, :] = derived[x]
        return carry

    lax.fori_loop(0, 5, field, 0)


def kernel_finish(conserved, total, from_mate, tendency, advanced):
    def plane(x, carry):
        for f in range(5):
            value = -(total[f, x] + from_mate[f, x])
            tendency[f, x] = value
            advanced[f, x] = conserved[f, x] + section_step * value
        return carry

    lax.fori_loop(0, CX, plane, 0)


def call(kernel, outputs, operands, scratch=(), scalar=False, outside=False, inside=True, cost=0.02):
    space = pltpu.HBM if outside else pltpu.VMEM
    in_specs = [pl.BlockSpec(memory_space=space) for _ in operands]
    if scalar:
        in_specs[0] = pl.BlockSpec(memory_space=pltpu.SMEM)
    if outside:
        operands = [pltpu.with_memory_space_constraint(value, pltpu.HBM) for value in operands]
    work = int(cost * 1e9)
    held = pltpu.VMEM if inside else jax.ShapeDtypeStruct
    return pl.pallas_call(
        kernel,
        out_shape=[held(shape, F32) for shape in outputs],
        in_specs=in_specs,
        out_specs=[pl.BlockSpec(memory_space=pltpu.VMEM) for _ in outputs],
        scratch_shapes=list(scratch),
        cost_estimate=pl.CostEstimate(flops=work, bytes_accessed=work // 300, transcendentals=0),
        compiler_params=pltpu.CompilerParams(vmem_limit_bytes=24 * 1024 * 1024),
    )(*operands)


def fast_device(mass_per_volume, momentum, energy):
    rho = jnp.transpose(mass_per_volume, (0, 2, 1))
    mom = jnp.transpose(momentum, (0, 1, 3, 2))
    ene = jnp.transpose(energy, (0, 2, 1))
    _, rows, width = rho.shape
    length = 4 * width
    parity = lax.rem(lax.axis_index("gy").astype(jnp.int32), 2).reshape(1)
    z_high, z_low = span_blocks(length, PLACES, PLACES[:2])
    f_high, f_low = span_blocks(length, PLACES[:2], (0, 1))
    y_high, y_low = halves(np.kron(np.eye(CX, dtype=np.float32), pitch_matrix(rows, CY)))
    block = (CX, rows, width)
    sums = (2, rows, width)
    points = CX * rows
    devices = lax.axis_size("gx")
    ring_up = [(i, (i + 1) % devices) for i in range(devices)]
    ring_down = [(j, i) for i, j in ring_up]
    to_mate = [(i, i ^ 1) for i in range(4)]
    to_peer = [(i, i ^ 2) for i in range(4)]

    conserved, own, first, up, down = call(
        kernel_primitives,
        [(5,) + block, (4,) + block, (2,) + block, (4,) + sums, (4,) + sums],
        (rho, mom, ene),
        scratch=(pltpu.SemaphoreType.DMA((3,)),),
        outside=True,
    )
    peer_first = lax.ppermute(first, "gy", to_peer)
    before = lax.ppermute(up, "gx", ring_up)
    after = lax.ppermute(down, "gx", ring_down)
    mate = lax.ppermute(own, "gy", to_mate)
    dy, mu, second = call(
        kernel_pitch_gradients,
        [(4,) + block, block, (3,) + block],
        (own, conserved, y_high, y_low),
    )
    peer_second = lax.ppermute(second, "gy", to_peer)
    peer_first, before, after = lax.optimization_barrier((peer_first, before, after))
    across_first = lax.ppermute(peer_first, "gy", to_mate)
    dx, third = call(
        kernel_stream_gradients, [(4,) + block, (2,) + block], (own, before, after, mu)
    )
    peer_third = lax.ppermute(third, "gy", to_peer)
    dz, flux, flux_up, flux_down = call(
        kernel_flux_x,
        [(2, points, 2 * width), (5,) + block, (5,) + sums, (5,) + sums],
        (parity, own, second, peer_first, mate, across_first, dx, dy, mu, z_high, z_low),
        scalar=True,
    )
    flux_before = lax.ppermute(flux_up, "gx", ring_up)
    flux_after = lax.ppermute(flux_down, "gx", ring_down)
    for_v, for_t, dy_peer = call(
        kernel_peer,
        [block, block, (2, points, width)],
        (peer_first, peer_second, flux, y_high, y_low),
    )
    across_v = lax.ppermute(for_v, "gy", to_mate)
    across_t = lax.ppermute(for_t, "gy", to_mate)
    part, part_mate = call(
        kernel_flux_yz,
        [(5,) + block, (5,) + block],
        (
            parity, own, second, peer_first, peer_second, mate, across_v, across_t, dy_peer,
            dz, dx, dy, mu, y_high, y_low, z_high, z_low, f_high, f_low,
        ),
        scratch=(
            pltpu.VMEM((2, points, 2 * width), F32),
            pltpu.VMEM((5, points, 2 * width), F32),
            pltpu.VMEM((5, points, width), F32),
        ),
        scalar=True,
        cost=0.02,
    )
    (stream,) = call(
        kernel_flux_x_gradient, [(5,) + block], (flux, flux_before, flux_after)
    )
    total, for_mate = call(
        kernel_corrections,
        [(5,) + block, (5,) + block],
        (parity, own, peer_first, third, peer_third, part, part_mate, stream, f_high, f_low),
        scalar=True,
    )
    from_mate = lax.ppermute(for_mate, "gy", to_mate)
    tendency, advanced = call(
        kernel_finish,
        [(5,) + block, (5,) + block],
        (conserved, total, from_mate),
        inside=False,
    )
    return (
        jnp.transpose(tendency, (0, 1, 3, 2)),
        jnp.transpose(advanced, (0, 1, 3, 2)),
    )


def padded(array, sides, width):
    for axis, dim in sides:
        devices, length = (lax.axis_size(axis), array.shape[dim])
        up = [(i, (i + 1) % devices) for i in range(devices)]
        down = [(j, i) for i, j in up]
        last = lax.slice_in_dim(array, length - width, length, axis=dim)
        initial = lax.slice_in_dim(array, 0, width, axis=dim)
        before = lax.ppermute(last, axis, up)
        after = lax.ppermute(initial, axis, down)
        array = jnp.concatenate([before, array, after], axis=dim)
    return array


def right_side(conserved, gradients_of, derive_x, derive_y, derive_z):
    mass_per_volume = conserved[0]
    momentum = conserved[1:4]
    energy = conserved[4]
    local_speed_vector = momentum / mass_per_volume
    kinetic = 0.5 * jnp.sum(momentum * local_speed_vector, axis=0)
    normal_force_per_area = (heat_ratio - 1.0) * (energy - kinetic)
    thermal_state = normal_force_per_area / mass_per_volume
    basic_quantities = jnp.concatenate([local_speed_vector, thermal_state[None]], 0)
    gradients = gradients_of(basic_quantities)
    shear_resistance = shear_resistance_reference * jnp.power(thermal_state, sutherland_power_law)
    conductivity = shear_resistance * heat_ratio / ((heat_ratio - 1.0) * prandtl)
    dilatation = gradients[0][0] + gradients[1][1] + gradients[2][2]
    derivers = (derive_x, derive_y, derive_z)
    accumulated = None
    for direction in range(3):
        stress_column = [
            shear_resistance * (gradients[direction][component] + gradients[component][direction])
            for component in range(3)
        ]
        stress_column[direction] = (
            stress_column[direction] - 2.0 / 3.0 * shear_resistance * dilatation
        )
        fluxes = [momentum[direction]]
        for component in range(3):
            moment_flux = (
                momentum[component] * local_speed_vector[direction] - stress_column[component]
            )
            if component == direction:
                moment_flux = moment_flux + normal_force_per_area
            fluxes.append(moment_flux)
        work_term = (
            stress_column[0] * local_speed_vector[0]
            + stress_column[1] * local_speed_vector[1]
            + stress_column[2] * local_speed_vector[2]
        )
        fluxes.append(
            (energy + normal_force_per_area) * local_speed_vector[direction]
            - work_term
            - conductivity * gradients[direction][3]
        )
        divergence_part = derivers[direction](jnp.stack(fluxes))
        accumulated = divergence_part if accumulated is None else accumulated + divergence_part
    return -accumulated


def plain_device(mass_per_volume, momentum, energy):
    conserved = jnp.concatenate([mass_per_volume[None], momentum, energy[None]], 0)
    highest = lax.Precision.HIGHEST
    x_matrix = jnp.asarray(compact_matrix(CX, HALO))
    z_matrix = jnp.asarray(span_matrix(NZ))

    def apply_x(extended):
        return jnp.einsum("il,flab->fiab", x_matrix, extended, precision=highest)

    def flux_x(values):
        return apply_x(padded(values, (("gx", 1),), HALO))

    y_matrix = jnp.asarray(pitch_matrix(conserved.shape[3], CY))

    def apply_y(values):
        return jnp.einsum("fabk,jk->fabj", values, y_matrix, precision=highest)

    def derive_span(values):
        lines = jnp.transpose(
            lax.all_to_all(values, "gy", split_axis=3, concat_axis=2, tiled=True), (0, 1, 3, 2)
        )
        derived = jnp.einsum("fack,jk->facj", lines, z_matrix, precision=highest)
        returned = lax.all_to_all(derived, "gy", split_axis=3, concat_axis=2, tiled=True)
        return jnp.transpose(returned, (0, 1, 3, 2))

    def gradients_of(basic_quantities):
        extended = padded(basic_quantities, (("gx", 1),), HALO)
        return (apply_x(extended), apply_y(basic_quantities), derive_span(basic_quantities))

    tendency = right_side(conserved, gradients_of, flux_x, apply_y, derive_span)
    advanced = conserved + section_step * tendency
    return (tendency, advanced)


def per_device(mass_per_volume, momentum, energy):
    planes, width, rows = mass_per_volume.shape
    fits = planes == CX and width % 128 == 0 and rows <= 32 and rows % CY == 0
    if fits and lax.axis_size("gy") == 4:
        return fast_device(mass_per_volume, momentum, energy)
    return plain_device(mass_per_volume, momentum, energy)


def solution(mesh):
    in_specs = (P("gx", "gy", None), P(None, "gx", "gy", None), P("gx", "gy", None))
    out_specs = (P(None, "gx", "gy", None), P(None, "gx", "gy", None))
    return jax.shard_map(
        per_device, mesh=mesh, in_specs=in_specs, out_specs=out_specs, check_vma=False
    )
```

```python
import functools

import jax
import jax.numpy as jnp
import numpy as np
from jax import lax
from jax.experimental import pallas as pl
from jax.experimental.pallas import tpu as pltpu
from jax.sharding import PartitionSpec as P

CX = 8
CY = 8
NZ = 512
HALO = 4


heat_ratio = 1.4
shear_resistance_reference = 0.08
sutherland_power_law = 0.7
prandtl = 0.72
section_step = 0.05
compact_alpha = 1.0 / 3.0
compact_near = 14.0 / 9.0
compact_far = 1.0 / 9.0

conduction = heat_ratio / ((heat_ratio - 1.0) * prandtl)
enthalpy = heat_ratio / (heat_ratio - 1.0)


def tridiagonal_inverse_product(length, stencil):
    solved = np.array(stencil)
    upper_ratio = np.zeros(length)
    for row_index in range(length):
        if row_index == 0:
            pivot_value = 1.0
            solved[row_index] = solved[row_index] / pivot_value
        else:
            pivot_value = 1.0 - compact_alpha * upper_ratio[row_index - 1]
            solved[row_index] = (
                solved[row_index] - compact_alpha * solved[row_index - 1]
            ) / pivot_value
        upper_ratio[row_index] = compact_alpha / pivot_value
    for row_index in range(length - 2, -1, -1):
        solved[row_index] = solved[row_index] - upper_ratio[row_index] * solved[row_index + 1]
    return solved


def exact_compact_matrix(block_size, margin):
    length = block_size + 2 * margin
    stencil = compact_near / 2.0 * (np.eye(length, k=1) - np.eye(length, k=-1))
    stencil = stencil + compact_far / 4.0 * (np.eye(length, k=2) - np.eye(length, k=-2))
    inverse_product = tridiagonal_inverse_product(length, stencil)
    return inverse_product[margin : margin + block_size]


def compact_matrix(block_size, margin):
    return exact_compact_matrix(block_size, margin).astype(np.float32)


def pitch_matrix(total, block_size):
    matrix = compact_matrix(block_size, HALO)
    result = np.zeros((total, total), np.float32)
    rows_all = np.arange(total)
    block_start = rows_all // block_size * block_size
    for offset in range(block_size + 2 * HALO):
        columns = (block_start - HALO + offset) % total
        result[rows_all, columns] += matrix[rows_all % block_size, offset]
    return result


def span_matrix(total):
    offsets = np.arange(total)[:, None] - np.arange(total)[None, :]
    angles = np.pi * offsets / total
    signs = np.where(offsets % 2 == 0, 1.0, -1.0)
    sines = np.where(offsets == 0, 1.0, np.sin(angles))
    result = np.where(offsets == 0, 0.0, np.pi / total * signs * np.cos(angles) / sines)
    return result.astype(np.float32)


F32 = jnp.float32
BF16 = jnp.bfloat16
U, W, V, T, R = range(5)
PLACES = (0, 2, 1, 3)
HALF = CX // 2


def halves(matrix):
    high = np.asarray(matrix, np.float32).astype(BF16)
    low = (matrix - high.astype(np.float32)).astype(BF16)
    return jnp.asarray(high), jnp.asarray(low)


def span_blocks(length, sources, targets):
    width = length // 4
    matrix = span_matrix(length).T
    both = []
    for core in range(2):
        columns = []
        for target in targets:
            to = core ^ target
            columns.append(
                np.concatenate(
                    [
                        matrix[
                            (core ^ source) * width : (core ^ source) * width + width,
                            to * width : to * width + width,
                        ]
                        for source in sources
                    ],
                    axis=0,
                )
            )
        both.append(np.concatenate(columns, axis=1))
    return halves(np.stack(both))


def halo_basis():
    matrix = exact_compact_matrix(CX, HALO)
    left = matrix[:, :HALO]
    basis = np.linalg.svd(left)[2][:2]
    inner = left @ basis.T
    outer = -inner[::-1]
    return basis, np.concatenate(
        [inner, matrix[:, HALO : HALO + CX], outer[:, ::-1]], axis=1
    )


def split(values):
    high = values.astype(BF16)
    low = (values - high.astype(F32)).astype(BF16)
    return high, low


def dot(a, b):
    return jnp.dot(a, b, preferred_element_type=F32)


def right_product(values, matrix_high, matrix_low):
    high, low = split(values)
    return dot(high, matrix_high) + dot(low, matrix_high) + dot(high, matrix_low)


def left_product(matrix_high, matrix_low, values):
    high, low = split(values)
    return dot(matrix_high, high) + dot(matrix_high, low) + dot(matrix_low, high)


def compact_x(planes):
    matrix = halo_basis()[1]
    length = CX + 4
    half = length // 2
    odd = [planes[l] - planes[length - 1 - l] for l in range(half)]
    even = [planes[l] + planes[length - 1 - l] for l in range(half)]
    result = [None] * CX
    for i in range(HALF):
        first = None
        second = None
        for l in range(half):
            a = float(0.5 * (matrix[i, l] - matrix[i, length - 1 - l]))
            b = float(0.5 * (matrix[i, l] + matrix[i, length - 1 - l]))
            first = a * odd[l] if first is None else first + a * odd[l]
            second = b * even[l] if second is None else second + b * even[l]
        result[i] = first + second
        result[CX - 1 - i] = first - second
    return result


def extended(before, own, after, f, rows):
    return (
        [before[f, 0, rows, :], before[f, 1, rows, :]]
        + [own[f, l, rows, :] for l in range(CX)]
        + [after[f, 1, rows, :], after[f, 0, rows, :]]
    )


def halo_sums(values, f, rows, up, down):
    basis = halo_basis()[0]
    for k in range(2):
        top = None
        bottom = None
        for l in range(HALO):
            a = float(basis[k, l]) * values[f, CX - HALO + l, rows, :]
            b = float(basis[k, l]) * values[f, HALO - 1 - l, rows, :]
            top = a if top is None else top + a
            bottom = b if bottom is None else bottom + b
        up[f, k, rows, :] = top
        down[f, k, rows, :] = bottom


def row_chunks(rows):
    return [slice(start, start + 8) for start in range(0, rows, 8)]


def flat(values):
    return values.reshape(-1, values.shape[-1])


def kernel_primitives(
    rho_in, mom_in, ene_in, conserved, own, first, up, down, arrived
):
    rho = conserved.at[0]
    mom = conserved.at[1:4]
    ene = conserved.at[4]
    copies = [
        pltpu.make_async_copy(source, target, arrived.at[k])
        for k, (source, target) in enumerate(((rho_in, rho), (mom_in, mom), (ene_in, ene)))
    ]
    for copy in copies:
        copy.start()
    for copy in copies:
        copy.wait()

    def plane(x, carry):
        density = rho[x]
        inverse = 1.0 / density
        u = mom[0, x] * inverse
        v = mom[1, x] * inverse
        w = mom[2, x] * inverse
        kinetic = 0.5 * (mom[0, x] * u + mom[1, x] * v + mom[2, x] * w)
        temperature = (heat_ratio - 1.0) * (ene[x] - kinetic) * inverse
        own[U, x] = u
        own[W, x] = w
        own[V, x] = v
        own[T, x] = temperature
        first[0, x] = u
        first[1, x] = w
        return carry

    lax.fori_loop(0, CX, plane, 0)

    def sums(f, carry):
        for rows in row_chunks(rho.shape[1]):
            halo_sums(own, f, rows, up, down)
        return carry

    lax.fori_loop(0, 4, sums, 0)


def kernel_pitch_gradients(own, conserved, y_high, y_low, dy, mu, second):
    for f in range(4):
        dy[f] = left_product(y_high[...], y_low[...], flat(own[f])).reshape(own.shape[1:])

    def plane(x, carry):
        mu[x] = shear_resistance_reference * jnp.exp(
            sutherland_power_law * jnp.log(own[T, x])
        )
        second[0, x] = own[V, x]
        second[1, x] = own[T, x]
        second[2, x] = conserved[0, x]
        return carry

    lax.fori_loop(0, CX, plane, 0)


def kernel_stream_gradients(own, before, after, mu, dx, third):
    def field(f, carry):
        for rows in row_chunks(own.shape[2]):
            derived = compact_x(extended(before, own, after, f, rows))
            for x in range(CX):
                dx[f, x, rows, :] = derived[x]
        return carry

    lax.fori_loop(0, 4, field, 0)

    def plane(x, carry):
        third[0, x] = (2.0 / 3.0) * mu[x] * dx[U, x]
        third[1, x] = mu[x] * dx[W, x]
        return carry

    lax.fori_loop(0, CX, plane, 0)


def kernel_flux_x(
    parity, own, second, peer_first, mate, across_first, dx, dy, mu, z_high, z_low,
    dz, flux, up, down,
):
    width = own.shape[-1]
    odd = parity[0]
    for f in range(2):
        values = jnp.concatenate(
            [flat(own[f]), flat(peer_first[f]), flat(mate[f]), flat(across_first[f])], axis=1
        )
        dz[f] = right_product(values, z_high[odd], z_low[odd])

    rows = own.shape[2]

    def plane(x, carry):
        at = pl.ds(pl.multiple_of(x * rows, rows), rows)
        u, w, v, t = (own[f, x] for f in range(4))
        density = second[2, x]
        viscosity = mu[x]
        dil = dx[U, x] + dy[V, x] + dz[1, at, :width]
        s1 = viscosity * (2.0 * dx[U, x] - (2.0 / 3.0) * dil)
        s2 = viscosity * (dx[V, x] + dy[U, x])
        s3 = viscosity * (dx[W, x] + dz[0, at, :width])
        m = density * u
        total = m * (enthalpy * t + 0.5 * (u * u + v * v + w * w))
        flux[0, x] = m
        flux[1, x] = m * u + density * t - s1
        flux[2, x] = m * v - s2
        flux[3, x] = m * w - s3
        flux[4, x] = total - (s1 * u + s2 * v + s3 * w) - conduction * viscosity * dx[T, x]
        return carry

    lax.fori_loop(0, CX, plane, 0)

    def sums(f, carry):
        for chunk in row_chunks(rows):
            halo_sums(flux, f, chunk, up, down)
        return carry

    lax.fori_loop(0, 5, sums, 0)


def kernel_peer(peer_first, peer_second, flux, y_high, y_low, for_v, for_t, dy_peer):
    for_v[...] = peer_second[0]
    for_t[...] = peer_second[1]
    dy_peer[0] = left_product(y_high[...], y_low[...], flat(peer_second[0]))
    dy_peer[1] = left_product(y_high[...], y_low[...], flat(peer_first[1]))


def kernel_flux_yz(
    parity, own, second, peer_first, peer_second, mate, across_v, across_t, dy_peer,
    dz, dx, dy, mu, y_high, y_low, z_high, z_low, f_high, f_low, part, part_mate,
    dz_more, flux, flux_y,
):
    rows, width = own.shape[2:]
    odd = parity[0]
    for f, across in enumerate((across_v, across_t)):
        values = jnp.concatenate(
            [flat(own[V + f]), flat(peer_second[f]), flat(mate[V + f]), flat(across[...])],
            axis=1,
        )
        dz_more[f] = right_product(values, z_high[odd], z_low[odd])

    def span_flux(at, lanes, u, w, v, t, density, viscosity, yv, yw):
        s1 = viscosity * dz[0, at, lanes]
        s2 = viscosity * (dz_more[0, at, lanes] + yw)
        s3 = viscosity * ((4.0 / 3.0) * dz[1, at, lanes] - (2.0 / 3.0) * yv)
        m = density * w
        total = m * (enthalpy * t + 0.5 * (u * u + v * v + w * w))
        flux[0, at, lanes] = m
        flux[1, at, lanes] = m * u - s1
        flux[2, at, lanes] = m * v - s2
        flux[3, at, lanes] = m * w + density * t - s3
        flux[4, at, lanes] = (
            total
            - (s1 * u + s2 * v + s3 * w)
            - conduction * viscosity * dz_more[1, at, lanes]
        )

    def plane(x, carry):
        at = pl.ds(pl.multiple_of(x * rows, rows), rows)
        here = slice(0, width)
        u, w, v, t = (own[f, x] for f in range(4))
        density = second[2, x]
        viscosity = mu[x]
        span_flux(at, here, u, w, v, t, density, viscosity, dy[V, x], dy[W, x])
        dil = dx[U, x] + dy[V, x] + dz[1, at, here]
        s1 = viscosity * (dy[U, x] + dx[V, x])
        s2 = viscosity * (2.0 * dy[V, x] - (2.0 / 3.0) * dil)
        s3 = viscosity * (dy[W, x] + dz_more[0, at, here])
        m = density * v
        total = m * (enthalpy * t + 0.5 * (u * u + v * v + w * w))
        flux_y[0, at, :] = m
        flux_y[1, at, :] = m * u - s1
        flux_y[2, at, :] = m * v + density * t - s2
        flux_y[3, at, :] = m * w - s3
        flux_y[4, at, :] = (
            total - (s1 * u + s2 * v + s3 * w) - conduction * viscosity * dy[T, x]
        )
        t = peer_second[1, x]
        viscosity = shear_resistance_reference * jnp.exp(sutherland_power_law * jnp.log(t))
        span_flux(
            at, slice(width, 2 * width), peer_first[0, x], peer_first[1, x],
            peer_second[0, x], t, peer_second[2, x], viscosity,
            dy_peer[0, at, :], dy_peer[1, at, :],
        )
        return carry

    lax.fori_loop(0, CX, plane, 0)
    shape = own.shape[1:]
    for f in range(5):
        spread = right_product(flux[f], f_high[odd], f_low[odd])
        local = left_product(y_high[...], y_low[...], flux_y[f])
        part[f] = (spread[:, :width] + local).reshape(shape)
        part_mate[f] = spread[:, width:].reshape(shape)


def kernel_corrections(
    parity, own, peer_first, third, peer_third, part, part_mate, stream, f_high, f_low,
    total, for_mate,
):
    width = own.shape[-1]
    odd = parity[0]
    shape = own.shape[1:]
    for f in (0, 2):
        total[f] = part[f] + stream[f]
        for_mate[f] = part_mate[f]
    pairs = ((own, third), (peer_first, peer_third))
    for f in (1, 3, 4):
        sides = []
        for speeds, shared in pairs:
            if f == 1:
                value = -shared[1]
            elif f == 3:
                value = shared[0]
            else:
                value = shared[0] * speeds[W] - shared[1] * speeds[U]
            sides.append(flat(value))
        spread = right_product(jnp.concatenate(sides, axis=1), f_high[odd], f_low[odd])
        total[f] = part[f] + stream[f] + spread[:, :width].reshape(shape)
        for_mate[f] = part_mate[f] + spread[:, width:].reshape(shape)


def kernel_flux_x_gradient(flux, before, after, result):
    def field(f, carry):
        for rows in row_chunks(flux.shape[2]):
            derived = compact_x(extended(before, flux, after, f, rows))
            for x in range(CX):
                result[f, x, rows, :] = derived[x]
        return carry

    lax.fori_loop(0, 5, field, 0)


def kernel_finish(conserved, total, from_mate, tendency, advanced):
    def plane(x, carry):
        for f in range(5):
            value = -(total[f, x] + from_mate[f, x])
            tendency[f, x] = value
            advanced[f, x] = conserved[f, x] + section_step * value
        return carry

    lax.fori_loop(0, CX, plane, 0)


def call(kernel, outputs, operands, scratch=(), scalar=False, outside=False, inside=True):
    space = pltpu.HBM if outside else pltpu.VMEM
    in_specs = [pl.BlockSpec(memory_space=space) for _ in operands]
    if scalar:
        in_specs[0] = pl.BlockSpec(memory_space=pltpu.SMEM)
    if outside:
        operands = [pltpu.with_memory_space_constraint(value, pltpu.HBM) for value in operands]
    touched = sum(value.size * value.dtype.itemsize for value in operands)
    touched += 4 * sum(int(np.prod(shape)) for shape in outputs)
    held = pltpu.VMEM if inside else jax.ShapeDtypeStruct
    return pl.pallas_call(
        kernel,
        out_shape=[held(shape, F32) for shape in outputs],
        in_specs=in_specs,
        out_specs=[pl.BlockSpec(memory_space=pltpu.VMEM) for _ in outputs],
        scratch_shapes=list(scratch),
        cost_estimate=pl.CostEstimate(flops=0, bytes_accessed=touched, transcendentals=0),
        compiler_params=pltpu.CompilerParams(vmem_limit_bytes=24 * 1024 * 1024),
    )(*operands)


def fast_device(mass_per_volume, momentum, energy):
    rho = jnp.transpose(mass_per_volume, (0, 2, 1))
    mom = jnp.transpose(momentum, (0, 1, 3, 2))
    ene = jnp.transpose(energy, (0, 2, 1))
    _, rows, width = rho.shape
    length = 4 * width
    parity = lax.rem(lax.axis_index("gy").astype(jnp.int32), 2).reshape(1)
    z_high, z_low = span_blocks(length, PLACES, PLACES[:2])
    f_high, f_low = span_blocks(length, PLACES[:2], (0, 1))
    y_high, y_low = halves(np.kron(np.eye(CX, dtype=np.float32), pitch_matrix(rows, CY)))
    block = (CX, rows, width)
    sums = (2, rows, width)
    points = CX * rows
    devices = lax.axis_size("gx")
    ring_up = [(i, (i + 1) % devices) for i in range(devices)]
    ring_down = [(j, i) for i, j in ring_up]
    to_mate = [(i, i ^ 1) for i in range(4)]
    to_peer = [(i, i ^ 2) for i in range(4)]

    conserved, own, first, up, down = call(
        kernel_primitives,
        [(5,) + block, (4,) + block, (2,) + block, (4,) + sums, (4,) + sums],
        (rho, mom, ene),
        scratch=(pltpu.SemaphoreType.DMA((3,)),),
        outside=True,
    )
    peer_first = lax.ppermute(first, "gy", to_peer)
    before = lax.ppermute(up, "gx", ring_up)
    after = lax.ppermute(down, "gx", ring_down)
    mate = lax.ppermute(own, "gy", to_mate)
    dy, mu, second = call(
        kernel_pitch_gradients,
        [(4,) + block, block, (3,) + block],
        (own, conserved, y_high, y_low),
    )
    peer_second = lax.ppermute(second, "gy", to_peer)
    peer_first, before, after = lax.optimization_barrier((peer_first, before, after))
    across_first = lax.ppermute(peer_first, "gy", to_mate)
    dx, third = call(
        kernel_stream_gradients, [(4,) + block, (2,) + block], (own, before, after, mu)
    )
    peer_third = lax.ppermute(third, "gy", to_peer)
    dz, flux, flux_up, flux_down = call(
        kernel_flux_x,
        [(2, points, 2 * width), (5,) + block, (5,) + sums, (5,) + sums],
        (parity, own, second, peer_first, mate, across_first, dx, dy, mu, z_high, z_low),
        scalar=True,
    )
    flux_before = lax.ppermute(flux_up, "gx", ring_up)
    flux_after = lax.ppermute(flux_down, "gx", ring_down)
    for_v, for_t, dy_peer = call(
        kernel_peer,
        [block, block, (2, points, width)],
        (peer_first, peer_second, flux, y_high, y_low),
    )
    across_v = lax.ppermute(for_v, "gy", to_mate)
    across_t = lax.ppermute(for_t, "gy", to_mate)
    part, part_mate = call(
        kernel_flux_yz,
        [(5,) + block, (5,) + block],
        (
            parity, own, second, peer_first, peer_second, mate, across_v, across_t, dy_peer,
            dz, dx, dy, mu, y_high, y_low, z_high, z_low, f_high, f_low,
        ),
        scratch=(
            pltpu.VMEM((2, points, 2 * width), F32),
            pltpu.VMEM((5, points, 2 * width), F32),
            pltpu.VMEM((5, points, width), F32),
        ),
        scalar=True,
    )
    (stream,) = call(
        kernel_flux_x_gradient, [(5,) + block], (flux, flux_before, flux_after)
    )
    total, for_mate = call(
        kernel_corrections,
        [(5,) + block, (5,) + block],
        (parity, own, peer_first, third, peer_third, part, part_mate, stream, f_high, f_low),
        scalar=True,
    )
    from_mate = lax.ppermute(for_mate, "gy", to_mate)
    tendency, advanced = call(
        kernel_finish,
        [(5,) + block, (5,) + block],
        (conserved, total, from_mate),
        inside=False,
    )
    return (
        jnp.transpose(tendency, (0, 1, 3, 2)),
        jnp.transpose(advanced, (0, 1, 3, 2)),
    )


def padded(array, sides, width):
    for axis, dim in sides:
        devices, length = (lax.axis_size(axis), array.shape[dim])
        up = [(i, (i + 1) % devices) for i in range(devices)]
        down = [(j, i) for i, j in up]
        last = lax.slice_in_dim(array, length - width, length, axis=dim)
        initial = lax.slice_in_dim(array, 0, width, axis=dim)
        before = lax.ppermute(last, axis, up)
        after = lax.ppermute(initial, axis, down)
        array = jnp.concatenate([before, array, after], axis=dim)
    return array


def right_side(conserved, gradients_of, derive_x, derive_y, derive_z):
    mass_per_volume = conserved[0]
    momentum = conserved[1:4]
    energy = conserved[4]
    local_speed_vector = momentum / mass_per_volume
    kinetic = 0.5 * jnp.sum(momentum * local_speed_vector, axis=0)
    normal_force_per_area = (heat_ratio - 1.0) * (energy - kinetic)
    thermal_state = normal_force_per_area / mass_per_volume
    basic_quantities = jnp.concatenate([local_speed_vector, thermal_state[None]], 0)
    gradients = gradients_of(basic_quantities)
    shear_resistance = shear_resistance_reference * jnp.power(thermal_state, sutherland_power_law)
    conductivity = shear_resistance * heat_ratio / ((heat_ratio - 1.0) * prandtl)
    dilatation = gradients[0][0] + gradients[1][1] + gradients[2][2]
    derivers = (derive_x, derive_y, derive_z)
    accumulated = None
    for direction in range(3):
        stress_column = [
            shear_resistance * (gradients[direction][component] + gradients[component][direction])
            for component in range(3)
        ]
        stress_column[direction] = (
            stress_column[direction] - 2.0 / 3.0 * shear_resistance * dilatation
        )
        fluxes = [momentum[direction]]
        for component in range(3):
            moment_flux = (
                momentum[component] * local_speed_vector[direction] - stress_column[component]
            )
            if component == direction:
                moment_flux = moment_flux + normal_force_per_area
            fluxes.append(moment_flux)
        work_term = (
            stress_column[0] * local_speed_vector[0]
            + stress_column[1] * local_speed_vector[1]
            + stress_column[2] * local_speed_vector[2]
        )
        fluxes.append(
            (energy + normal_force_per_area) * local_speed_vector[direction]
            - work_term
            - conductivity * gradients[direction][3]
        )
        divergence_part = derivers[direction](jnp.stack(fluxes))
        accumulated = divergence_part if accumulated is None else accumulated + divergence_part
    return -accumulated


def plain_device(mass_per_volume, momentum, energy):
    conserved = jnp.concatenate([mass_per_volume[None], momentum, energy[None]], 0)
    highest = lax.Precision.HIGHEST
    x_matrix = jnp.asarray(compact_matrix(CX, HALO))
    z_matrix = jnp.asarray(span_matrix(NZ))

    def apply_x(extended):
        return jnp.einsum("il,flab->fiab", x_matrix, extended, precision=highest)

    def flux_x(values):
        return apply_x(padded(values, (("gx", 1),), HALO))

    y_matrix = jnp.asarray(pitch_matrix(conserved.shape[3], CY))

    def apply_y(values):
        return jnp.einsum("fabk,jk->fabj", values, y_matrix, precision=highest)

    def derive_span(values):
        lines = jnp.transpose(
            lax.all_to_all(values, "gy", split_axis=3, concat_axis=2, tiled=True), (0, 1, 3, 2)
        )
        derived = jnp.einsum("fack,jk->facj", lines, z_matrix, precision=highest)
        returned = lax.all_to_all(derived, "gy", split_axis=3, concat_axis=2, tiled=True)
        return jnp.transpose(returned, (0, 1, 3, 2))

    def gradients_of(basic_quantities):
        extended = padded(basic_quantities, (("gx", 1),), HALO)
        return (apply_x(extended), apply_y(basic_quantities), derive_span(basic_quantities))

    tendency = right_side(conserved, gradients_of, flux_x, apply_y, derive_span)
    advanced = conserved + section_step * tendency
    return (tendency, advanced)


def per_device(mass_per_volume, momentum, energy):
    planes, width, rows = mass_per_volume.shape
    fits = planes == CX and width % 128 == 0 and rows <= 32 and rows % CY == 0
    if fits and lax.axis_size("gy") == 4:
        return fast_device(mass_per_volume, momentum, energy)
    return plain_device(mass_per_volume, momentum, energy)


def solution(mesh):
    in_specs = (P("gx", "gy", None), P(None, "gx", "gy", None), P("gx", "gy", None))
    out_specs = (P(None, "gx", "gy", None), P(None, "gx", "gy", None))
    return jax.shard_map(
        per_device, mesh=mesh, in_specs=in_specs, out_specs=out_specs, check_vma=False
    )
```

```python
import functools

import jax
import jax.numpy as jnp
import numpy as np
from jax import lax
from jax.experimental import pallas as pl
from jax.experimental.pallas import tpu as pltpu
from jax.sharding import PartitionSpec as P

CX = 8
CY = 8
NZ = 512
HALO = 4


heat_ratio = 1.4
shear_resistance_reference = 0.08
sutherland_power_law = 0.7
prandtl = 0.72
section_step = 0.05
compact_alpha = 1.0 / 3.0
compact_near = 14.0 / 9.0
compact_far = 1.0 / 9.0

conduction = heat_ratio / ((heat_ratio - 1.0) * prandtl)
enthalpy = heat_ratio / (heat_ratio - 1.0)


def tridiagonal_inverse_product(length, stencil):
    solved = np.array(stencil)
    upper_ratio = np.zeros(length)
    for row_index in range(length):
        if row_index == 0:
            pivot_value = 1.0
            solved[row_index] = solved[row_index] / pivot_value
        else:
            pivot_value = 1.0 - compact_alpha * upper_ratio[row_index - 1]
            solved[row_index] = (
                solved[row_index] - compact_alpha * solved[row_index - 1]
            ) / pivot_value
        upper_ratio[row_index] = compact_alpha / pivot_value
    for row_index in range(length - 2, -1, -1):
        solved[row_index] = solved[row_index] - upper_ratio[row_index] * solved[row_index + 1]
    return solved


def exact_compact_matrix(block_size, margin):
    length = block_size + 2 * margin
    stencil = compact_near / 2.0 * (np.eye(length, k=1) - np.eye(length, k=-1))
    stencil = stencil + compact_far / 4.0 * (np.eye(length, k=2) - np.eye(length, k=-2))
    inverse_product = tridiagonal_inverse_product(length, stencil)
    return inverse_product[margin : margin + block_size]


def compact_matrix(block_size, margin):
    return exact_compact_matrix(block_size, margin).astype(np.float32)


def pitch_matrix(total, block_size):
    matrix = compact_matrix(block_size, HALO)
    result = np.zeros((total, total), np.float32)
    rows_all = np.arange(total)
    block_start = rows_all // block_size * block_size
    for offset in range(block_size + 2 * HALO):
        columns = (block_start - HALO + offset) % total
        result[rows_all, columns] += matrix[rows_all % block_size, offset]
    return result


def span_matrix(total):
    offsets = np.arange(total)[:, None] - np.arange(total)[None, :]
    angles = np.pi * offsets / total
    signs = np.where(offsets % 2 == 0, 1.0, -1.0)
    sines = np.where(offsets == 0, 1.0, np.sin(angles))
    result = np.where(offsets == 0, 0.0, np.pi / total * signs * np.cos(angles) / sines)
    return result.astype(np.float32)


F32 = jnp.float32
BF16 = jnp.bfloat16
U, W, V, T, R = range(5)
PLACES = (0, 2, 1, 3)
HALF = CX // 2


def halves(matrix):
    high = np.asarray(matrix, np.float32).astype(BF16)
    low = (matrix - high.astype(np.float32)).astype(BF16)
    return jnp.asarray(high), jnp.asarray(low)


def span_blocks(length, sources, targets):
    width = length // 4
    matrix = span_matrix(length).T
    both = []
    for core in range(2):
        columns = []
        for target in targets:
            to = core ^ target
            columns.append(
                np.concatenate(
                    [
                        matrix[
                            (core ^ source) * width : (core ^ source) * width + width,
                            to * width : to * width + width,
                        ]
                        for source in sources
                    ],
                    axis=0,
                )
            )
        both.append(np.concatenate(columns, axis=1))
    return halves(np.stack(both))


def halo_basis():
    matrix = exact_compact_matrix(CX, HALO)
    left = matrix[:, :HALO]
    basis = np.linalg.svd(left)[2][:2]
    inner = left @ basis.T
    outer = -inner[::-1]
    return basis, np.concatenate(
        [inner, matrix[:, HALO : HALO + CX], outer[:, ::-1]], axis=1
    )


def split(values):
    high = values.astype(BF16)
    low = (values - high.astype(F32)).astype(BF16)
    return high, low


def dot(a, b):
    return jnp.dot(a, b, preferred_element_type=F32)


def right_product(values, matrix_high, matrix_low):
    high, low = split(values)
    return dot(high, matrix_high) + dot(low, matrix_high) + dot(high, matrix_low)


def left_product(matrix_high, matrix_low, values):
    high, low = split(values)
    return dot(matrix_high, high) + dot(matrix_high, low) + dot(matrix_low, high)


def compact_x(planes):
    matrix = halo_basis()[1]
    length = CX + 4
    half = length // 2
    odd = [planes[l] - planes[length - 1 - l] for l in range(half)]
    even = [planes[l] + planes[length - 1 - l] for l in range(half)]
    result = [None] * CX
    for i in range(HALF):
        first = None
        second = None
        for l in range(half):
            a = float(0.5 * (matrix[i, l] - matrix[i, length - 1 - l]))
            b = float(0.5 * (matrix[i, l] + matrix[i, length - 1 - l]))
            first = a * odd[l] if first is None else first + a * odd[l]
            second = b * even[l] if second is None else second + b * even[l]
        result[i] = first + second
        result[CX - 1 - i] = first - second
    return result


def extended(before, own, after, f, rows):
    return (
        [before[f, 0, rows, :], before[f, 1, rows, :]]
        + [own[f, l, rows, :] for l in range(CX)]
        + [after[f, 1, rows, :], after[f, 0, rows, :]]
    )


def halo_sums(values, f, rows, up, down):
    basis = halo_basis()[0]
    for k in range(2):
        top = None
        bottom = None
        for l in range(HALO):
            a = float(basis[k, l]) * values[f, CX - HALO + l, rows, :]
            b = float(basis[k, l]) * values[f, HALO - 1 - l, rows, :]
            top = a if top is None else top + a
            bottom = b if bottom is None else bottom + b
        up[f, k, rows, :] = top
        down[f, k, rows, :] = bottom


def row_chunks(rows):
    return [slice(start, start + 8) for start in range(0, rows, 8)]


def flat(values):
    return values.reshape(-1, values.shape[-1])


def kernel_primitives(
    rho_in, mom_in, ene_in, conserved, own, first, up, down, arrived
):
    rho = conserved.at[0]
    mom = conserved.at[1:4]
    ene = conserved.at[4]
    copies = [
        pltpu.make_async_copy(source, target, arrived.at[k])
        for k, (source, target) in enumerate(((rho_in, rho), (mom_in, mom), (ene_in, ene)))
    ]
    for copy in copies:
        copy.start()
    for copy in copies:
        copy.wait()

    def plane(x, carry):
        density = rho[x]
        inverse = 1.0 / density
        u = mom[0, x] * inverse
        v = mom[1, x] * inverse
        w = mom[2, x] * inverse
        kinetic = 0.5 * (mom[0, x] * u + mom[1, x] * v + mom[2, x] * w)
        temperature = (heat_ratio - 1.0) * (ene[x] - kinetic) * inverse
        own[U, x] = u
        own[W, x] = w
        own[V, x] = v
        own[T, x] = temperature
        first[0, x] = u
        first[1, x] = w
        return carry

    lax.fori_loop(0, CX, plane, 0)

    def sums(f, carry):
        for rows in row_chunks(rho.shape[1]):
            halo_sums(own, f, rows, up, down)
        return carry

    lax.fori_loop(0, 4, sums, 0)


def kernel_pitch_gradients(own, conserved, y_high, y_low, dy, mu, second, for_mate):
    for f in range(4):
        dy[f] = left_product(y_high[...], y_low[...], flat(own[f])).reshape(own.shape[1:])

    def plane(x, carry):
        mu[x] = shear_resistance_reference * jnp.exp(
            sutherland_power_law * jnp.log(own[T, x])
        )
        for f in range(4):
            for_mate[f, x] = own[f, x]
        second[0, x] = own[V, x]
        second[1, x] = own[T, x]
        second[2, x] = conserved[0, x]
        return carry

    lax.fori_loop(0, CX, plane, 0)


def kernel_stream_gradients(own, before, after, mu, dx, third):
    def field(f, carry):
        for rows in row_chunks(own.shape[2]):
            derived = compact_x(extended(before, own, after, f, rows))
            for x in range(CX):
                dx[f, x, rows, :] = derived[x]
        return carry

    lax.fori_loop(0, 4, field, 0)

    def plane(x, carry):
        third[0, x] = (2.0 / 3.0) * mu[x] * dx[U, x]
        third[1, x] = mu[x] * dx[W, x]
        return carry

    lax.fori_loop(0, CX, plane, 0)


def kernel_flux_x(
    own, second, peer_first, mate, across_first, dx, dy, mu, z_high, z_low,
    dz, flux, up, down,
):
    width = own.shape[-1]
    odd = lax.rem(lax.axis_index("gy"), 2)
    for f in range(2):
        values = jnp.concatenate(
            [flat(own[f]), flat(peer_first[f]), flat(mate[f]), flat(across_first[f])], axis=1
        )
        dz[f] = right_product(values, z_high[odd], z_low[odd])

    rows = own.shape[2]

    def plane(x, carry):
        at = pl.ds(pl.multiple_of(x * rows, rows), rows)
        u, w, v, t = (own[f, x] for f in range(4))
        density = second[2, x]
        viscosity = mu[x]
        dil = dx[U, x] + dy[V, x] + dz[1, at, :width]
        s1 = viscosity * (2.0 * dx[U, x] - (2.0 / 3.0) * dil)
        s2 = viscosity * (dx[V, x] + dy[U, x])
        s3 = viscosity * (dx[W, x] + dz[0, at, :width])
        m = density * u
        total = m * (enthalpy * t + 0.5 * (u * u + v * v + w * w))
        flux[0, x] = m
        flux[1, x] = m * u + density * t - s1
        flux[2, x] = m * v - s2
        flux[3, x] = m * w - s3
        flux[4, x] = total - (s1 * u + s2 * v + s3 * w) - conduction * viscosity * dx[T, x]
        return carry

    lax.fori_loop(0, CX, plane, 0)

    def sums(f, carry):
        for chunk in row_chunks(rows):
            halo_sums(flux, f, chunk, up, down)
        return carry

    lax.fori_loop(0, 5, sums, 0)


def kernel_peer(peer_first, peer_second, flux, y_high, y_low, for_v, for_t, dy_peer):
    for_v[...] = peer_second[0]
    for_t[...] = peer_second[1]
    dy_peer[0] = left_product(y_high[...], y_low[...], flat(peer_second[0]))
    dy_peer[1] = left_product(y_high[...], y_low[...], flat(peer_first[1]))


def kernel_flux_yz(
    own, second, peer_first, peer_second, mate, across_v, across_t, dy_peer,
    dz, dx, dy, mu, y_high, y_low, z_high, z_low, f_high, f_low, part, part_mate,
    dz_more, flux, flux_y,
):
    rows, width = own.shape[2:]
    odd = lax.rem(lax.axis_index("gy"), 2)
    for f, across in enumerate((across_v, across_t)):
        values = jnp.concatenate(
            [flat(own[V + f]), flat(peer_second[f]), flat(mate[V + f]), flat(across[...])],
            axis=1,
        )
        dz_more[f] = right_product(values, z_high[odd], z_low[odd])

    def span_flux(at, lanes, u, w, v, t, density, viscosity, yv, yw):
        s1 = viscosity * dz[0, at, lanes]
        s2 = viscosity * (dz_more[0, at, lanes] + yw)
        s3 = viscosity * ((4.0 / 3.0) * dz[1, at, lanes] - (2.0 / 3.0) * yv)
        m = density * w
        total = m * (enthalpy * t + 0.5 * (u * u + v * v + w * w))
        flux[0, at, lanes] = m
        flux[1, at, lanes] = m * u - s1
        flux[2, at, lanes] = m * v - s2
        flux[3, at, lanes] = m * w + density * t - s3
        flux[4, at, lanes] = (
            total
            - (s1 * u + s2 * v + s3 * w)
            - conduction * viscosity * dz_more[1, at, lanes]
        )

    def plane(x, carry):
        at = pl.ds(pl.multiple_of(x * rows, rows), rows)
        here = slice(0, width)
        u, w, v, t = (own[f, x] for f in range(4))
        density = second[2, x]
        viscosity = mu[x]
        span_flux(at, here, u, w, v, t, density, viscosity, dy[V, x], dy[W, x])
        dil = dx[U, x] + dy[V, x] + dz[1, at, here]
        s1 = viscosity * (dy[U, x] + dx[V, x])
        s2 = viscosity * (2.0 * dy[V, x] - (2.0 / 3.0) * dil)
        s3 = viscosity * (dy[W, x] + dz_more[0, at, here])
        m = density * v
        total = m * (enthalpy * t + 0.5 * (u * u + v * v + w * w))
        flux_y[0, at, :] = m
        flux_y[1, at, :] = m * u - s1
        flux_y[2, at, :] = m * v + density * t - s2
        flux_y[3, at, :] = m * w - s3
        flux_y[4, at, :] = (
            total - (s1 * u + s2 * v + s3 * w) - conduction * viscosity * dy[T, x]
        )
        t = peer_second[1, x]
        viscosity = shear_resistance_reference * jnp.exp(sutherland_power_law * jnp.log(t))
        span_flux(
            at, slice(width, 2 * width), peer_first[0, x], peer_first[1, x],
            peer_second[0, x], t, peer_second[2, x], viscosity,
            dy_peer[0, at, :], dy_peer[1, at, :],
        )
        return carry

    lax.fori_loop(0, CX, plane, 0)
    shape = own.shape[1:]
    for f in range(5):
        spread = right_product(flux[f], f_high[odd], f_low[odd])
        local = left_product(y_high[...], y_low[...], flux_y[f])
        part[f] = (spread[:, :width] + local).reshape(shape)
        part_mate[f] = spread[:, width:].reshape(shape)


def kernel_corrections(
    own, peer_first, third, peer_third, part, part_mate, stream, f_high, f_low,
    total, for_mate,
):
    width = own.shape[-1]
    odd = lax.rem(lax.axis_index("gy"), 2)
    shape = own.shape[1:]
    for f in (0, 2):
        total[f] = part[f] + stream[f]
        for_mate[f] = part_mate[f]
    pairs = ((own, third), (peer_first, peer_third))
    for f in (1, 3, 4):
        sides = []
        for speeds, shared in pairs:
            if f == 1:
                value = -shared[1]
            elif f == 3:
                value = shared[0]
            else:
                value = shared[0] * speeds[W] - shared[1] * speeds[U]
            sides.append(flat(value))
        spread = right_product(jnp.concatenate(sides, axis=1), f_high[odd], f_low[odd])
        total[f] = part[f] + stream[f] + spread[:, :width].reshape(shape)
        for_mate[f] = part_mate[f] + spread[:, width:].reshape(shape)


def kernel_flux_x_gradient(flux, before, after, result):
    def field(f, carry):
        for rows in row_chunks(flux.shape[2]):
            derived = compact_x(extended(before, flux, after, f, rows))
            for x in range(CX):
                result[f, x, rows, :] = derived[x]
        return carry

    lax.fori_loop(0, 5, field, 0)


def kernel_finish(conserved, total, from_mate, tendency, advanced):
    def plane(x, carry):
        for f in range(5):
            value = -(total[f, x] + from_mate[f, x])
            tendency[f, x] = value
            advanced[f, x] = conserved[f, x] + section_step * value
        return carry

    lax.fori_loop(0, CX, plane, 0)


def call(kernel, outputs, operands, scratch=(), outside=False):
    space = pltpu.HBM if outside else pltpu.VMEM
    in_specs = [pl.BlockSpec(memory_space=space) for _ in operands]
    if outside:
        operands = [pltpu.with_memory_space_constraint(value, pltpu.HBM) for value in operands]
    touched = sum(value.size * value.dtype.itemsize for value in operands)
    touched += 4 * sum(int(np.prod(shape)) for shape in outputs)
    return pl.pallas_call(
        kernel,
        out_shape=[jax.ShapeDtypeStruct(shape, F32) for shape in outputs],
        in_specs=in_specs,
        out_specs=[pl.BlockSpec(memory_space=pltpu.VMEM) for _ in outputs],
        scratch_shapes=list(scratch),
        cost_estimate=pl.CostEstimate(flops=0, bytes_accessed=touched, transcendentals=0),
        compiler_params=pltpu.CompilerParams(vmem_limit_bytes=24 * 1024 * 1024),
    )(*operands)


def fast_device(mass_per_volume, momentum, energy):
    rho = jnp.transpose(mass_per_volume, (0, 2, 1))
    mom = jnp.transpose(momentum, (0, 1, 3, 2))
    ene = jnp.transpose(energy, (0, 2, 1))
    _, rows, width = rho.shape
    length = 4 * width
    z_high, z_low = span_blocks(length, PLACES, PLACES[:2])
    f_high, f_low = span_blocks(length, PLACES[:2], (0, 1))
    y_high, y_low = halves(np.kron(np.eye(CX, dtype=np.float32), pitch_matrix(rows, CY)))
    block = (CX, rows, width)
    sums = (2, rows, width)
    points = CX * rows
    devices = lax.axis_size("gx")
    ring_up = [(i, (i + 1) % devices) for i in range(devices)]
    ring_down = [(j, i) for i, j in ring_up]
    to_mate = [(i, i ^ 1) for i in range(4)]
    to_peer = [(i, i ^ 2) for i in range(4)]

    conserved, own, first, up, down = call(
        kernel_primitives,
        [(5,) + block, (4,) + block, (2,) + block, (4,) + sums, (4,) + sums],
        (rho, mom, ene),
        scratch=(pltpu.SemaphoreType.DMA((3,)),),
        outside=True,
    )
    peer_first = lax.ppermute(first, "gy", to_peer)
    before = lax.ppermute(up, "gx", ring_up)
    after = lax.ppermute(down, "gx", ring_down)
    dy, mu, second, for_mate = call(
        kernel_pitch_gradients,
        [(4,) + block, block, (3,) + block, (4,) + block],
        (own, conserved, y_high, y_low),
    )
    mate = lax.ppermute(for_mate, "gy", to_mate)
    peer_second = lax.ppermute(second, "gy", to_peer)
    peer_first, before, after = lax.optimization_barrier((peer_first, before, after))
    across_first = lax.ppermute(peer_first, "gy", to_mate)
    dx, third = call(
        kernel_stream_gradients, [(4,) + block, (2,) + block], (own, before, after, mu)
    )
    peer_third = lax.ppermute(third, "gy", to_peer)
    dz, flux, flux_up, flux_down = call(
        kernel_flux_x,
        [(2, points, 2 * width), (5,) + block, (5,) + sums, (5,) + sums],
        (own, second, peer_first, mate, across_first, dx, dy, mu, z_high, z_low),
    )
    flux_before = lax.ppermute(flux_up, "gx", ring_up)
    flux_after = lax.ppermute(flux_down, "gx", ring_down)
    for_v, for_t, dy_peer = call(
        kernel_peer,
        [block, block, (2, points, width)],
        (peer_first, peer_second, flux, y_high, y_low),
    )
    across_v = lax.ppermute(for_v, "gy", to_mate)
    across_t = lax.ppermute(for_t, "gy", to_mate)
    part, part_mate = call(
        kernel_flux_yz,
        [(5,) + block, (5,) + block],
        (
            own, second, peer_first, peer_second, mate, across_v, across_t, dy_peer,
            dz, dx, dy, mu, y_high, y_low, z_high, z_low, f_high, f_low,
        ),
        scratch=(
            pltpu.VMEM((2, points, 2 * width), F32),
            pltpu.VMEM((5, points, 2 * width), F32),
            pltpu.VMEM((5, points, width), F32),
        ),
    )
    (stream,) = call(
        kernel_flux_x_gradient, [(5,) + block], (flux, flux_before, flux_after)
    )
    total, for_mate = call(
        kernel_corrections,
        [(5,) + block, (5,) + block],
        (own, peer_first, third, peer_third, part, part_mate, stream, f_high, f_low),
    )
    from_mate = lax.ppermute(for_mate, "gy", to_mate)
    tendency, advanced = call(
        kernel_finish,
        [(5,) + block, (5,) + block],
        (conserved, total, from_mate),
    )
    return (
        jnp.transpose(tendency, (0, 1, 3, 2)),
        jnp.transpose(advanced, (0, 1, 3, 2)),
    )


def padded(array, sides, width):
    for axis, dim in sides:
        devices, length = (lax.axis_size(axis), array.shape[dim])
        up = [(i, (i + 1) % devices) for i in range(devices)]
        down = [(j, i) for i, j in up]
        last = lax.slice_in_dim(array, length - width, length, axis=dim)
        initial = lax.slice_in_dim(array, 0, width, axis=dim)
        before = lax.ppermute(last, axis, up)
        after = lax.ppermute(initial, axis, down)
        array = jnp.concatenate([before, array, after], axis=dim)
    return array


def right_side(conserved, gradients_of, derive_x, derive_y, derive_z):
    mass_per_volume = conserved[0]
    momentum = conserved[1:4]
    energy = conserved[4]
    local_speed_vector = momentum / mass_per_volume
    kinetic = 0.5 * jnp.sum(momentum * local_speed_vector, axis=0)
    normal_force_per_area = (heat_ratio - 1.0) * (energy - kinetic)
    thermal_state = normal_force_per_area / mass_per_volume
    basic_quantities = jnp.concatenate([local_speed_vector, thermal_state[None]], 0)
    gradients = gradients_of(basic_quantities)
    shear_resistance = shear_resistance_reference * jnp.power(thermal_state, sutherland_power_law)
    conductivity = shear_resistance * heat_ratio / ((heat_ratio - 1.0) * prandtl)
    dilatation = gradients[0][0] + gradients[1][1] + gradients[2][2]
    derivers = (derive_x, derive_y, derive_z)
    accumulated = None
    for direction in range(3):
        stress_column = [
            shear_resistance * (gradients[direction][component] + gradients[component][direction])
            for component in range(3)
        ]
        stress_column[direction] = (
            stress_column[direction] - 2.0 / 3.0 * shear_resistance * dilatation
        )
        fluxes = [momentum[direction]]
        for component in range(3):
            moment_flux = (
                momentum[component] * local_speed_vector[direction] - stress_column[component]
            )
            if component == direction:
                moment_flux = moment_flux + normal_force_per_area
            fluxes.append(moment_flux)
        work_term = (
            stress_column[0] * local_speed_vector[0]
            + stress_column[1] * local_speed_vector[1]
            + stress_column[2] * local_speed_vector[2]
        )
        fluxes.append(
            (energy + normal_force_per_area) * local_speed_vector[direction]
            - work_term
            - conductivity * gradients[direction][3]
        )
        divergence_part = derivers[direction](jnp.stack(fluxes))
        accumulated = divergence_part if accumulated is None else accumulated + divergence_part
    return -accumulated


def plain_device(mass_per_volume, momentum, energy):
    conserved = jnp.concatenate([mass_per_volume[None], momentum, energy[None]], 0)
    highest = lax.Precision.HIGHEST
    x_matrix = jnp.asarray(compact_matrix(CX, HALO))
    z_matrix = jnp.asarray(span_matrix(NZ))

    def apply_x(extended):
        return jnp.einsum("il,flab->fiab", x_matrix, extended, precision=highest)

    def flux_x(values):
        return apply_x(padded(values, (("gx", 1),), HALO))

    y_matrix = jnp.asarray(pitch_matrix(conserved.shape[3], CY))

    def apply_y(values):
        return jnp.einsum("fabk,jk->fabj", values, y_matrix, precision=highest)

    def derive_span(values):
        lines = jnp.transpose(
            lax.all_to_all(values, "gy", split_axis=3, concat_axis=2, tiled=True), (0, 1, 3, 2)
        )
        derived = jnp.einsum("fack,jk->facj", lines, z_matrix, precision=highest)
        returned = lax.all_to_all(derived, "gy", split_axis=3, concat_axis=2, tiled=True)
        return jnp.transpose(returned, (0, 1, 3, 2))

    def gradients_of(basic_quantities):
        extended = padded(basic_quantities, (("gx", 1),), HALO)
        return (apply_x(extended), apply_y(basic_quantities), derive_span(basic_quantities))

    tendency = right_side(conserved, gradients_of, flux_x, apply_y, derive_span)
    advanced = conserved + section_step * tendency
    return (tendency, advanced)


def per_device(mass_per_volume, momentum, energy):
    planes, width, rows = mass_per_volume.shape
    fits = planes == CX and width % 128 == 0 and rows <= 32 and rows % CY == 0
    if fits and lax.axis_size("gy") == 4:
        return fast_device(mass_per_volume, momentum, energy)
    return plain_device(mass_per_volume, momentum, energy)


def solution(mesh):
    in_specs = (P("gx", "gy", None), P(None, "gx", "gy", None), P("gx", "gy", None))
    out_specs = (P(None, "gx", "gy", None), P(None, "gx", "gy", None))
    return jax.shard_map(
        per_device, mesh=mesh, in_specs=in_specs, out_specs=out_specs, check_vma=False
    )
```

```python
import functools

import jax
import jax.numpy as jnp
import numpy as np
from jax import lax
from jax.experimental import pallas as pl
from jax.experimental.pallas import tpu as pltpu
from jax.sharding import PartitionSpec as P

CX = 8
CY = 8
NZ = 512
HALO = 4


heat_ratio = 1.4
shear_resistance_reference = 0.08
sutherland_power_law = 0.7
prandtl = 0.72
section_step = 0.05
compact_alpha = 1.0 / 3.0
compact_near = 14.0 / 9.0
compact_far = 1.0 / 9.0

conduction = heat_ratio / ((heat_ratio - 1.0) * prandtl)
enthalpy = heat_ratio / (heat_ratio - 1.0)


def tridiagonal_inverse_product(length, stencil):
    solved = np.array(stencil)
    upper_ratio = np.zeros(length)
    for row_index in range(length):
        if row_index == 0:
            pivot_value = 1.0
            solved[row_index] = solved[row_index] / pivot_value
        else:
            pivot_value = 1.0 - compact_alpha * upper_ratio[row_index - 1]
            solved[row_index] = (
                solved[row_index] - compact_alpha * solved[row_index - 1]
            ) / pivot_value
        upper_ratio[row_index] = compact_alpha / pivot_value
    for row_index in range(length - 2, -1, -1):
        solved[row_index] = solved[row_index] - upper_ratio[row_index] * solved[row_index + 1]
    return solved


def exact_compact_matrix(block_size, margin):
    length = block_size + 2 * margin
    stencil = compact_near / 2.0 * (np.eye(length, k=1) - np.eye(length, k=-1))
    stencil = stencil + compact_far / 4.0 * (np.eye(length, k=2) - np.eye(length, k=-2))
    inverse_product = tridiagonal_inverse_product(length, stencil)
    return inverse_product[margin : margin + block_size]


def compact_matrix(block_size, margin):
    return exact_compact_matrix(block_size, margin).astype(np.float32)


def pitch_matrix(total, block_size):
    matrix = compact_matrix(block_size, HALO)
    result = np.zeros((total, total), np.float32)
    rows_all = np.arange(total)
    block_start = rows_all // block_size * block_size
    for offset in range(block_size + 2 * HALO):
        columns = (block_start - HALO + offset) % total
        result[rows_all, columns] += matrix[rows_all % block_size, offset]
    return result


def span_matrix(total):
    offsets = np.arange(total)[:, None] - np.arange(total)[None, :]
    angles = np.pi * offsets / total
    signs = np.where(offsets % 2 == 0, 1.0, -1.0)
    sines = np.where(offsets == 0, 1.0, np.sin(angles))
    result = np.where(offsets == 0, 0.0, np.pi / total * signs * np.cos(angles) / sines)
    return result.astype(np.float32)


F32 = jnp.float32
BF16 = jnp.bfloat16
U, W, V, T, R = range(5)
PLACES = (0, 1, 2, 3)
HALF = CX // 2


def halves(matrix):
    high = np.asarray(matrix, np.float32).astype(BF16)
    low = (matrix - high.astype(np.float32)).astype(BF16)
    return jnp.asarray(high), jnp.asarray(low)


def span_blocks(length, sources, targets):
    width = length // 4
    matrix = span_matrix(length).T
    both = []
    for core in range(2):
        columns = []
        for target in targets:
            to = core ^ target
            columns.append(
                np.concatenate(
                    [
                        matrix[
                            (core ^ source) * width : (core ^ source) * width + width,
                            to * width : to * width + width,
                        ]
                        for source in sources
                    ],
                    axis=0,
                )
            )
        both.append(np.concatenate(columns, axis=1))
    return halves(np.stack(both))


def halo_basis():
    matrix = exact_compact_matrix(CX, HALO)
    left = matrix[:, :HALO]
    basis = np.linalg.svd(left)[2][:2]
    inner = left @ basis.T
    outer = -inner[::-1]
    return basis, np.concatenate(
        [inner, matrix[:, HALO : HALO + CX], outer[:, ::-1]], axis=1
    )


def split(values):
    high = values.astype(BF16)
    low = (values - high.astype(F32)).astype(BF16)
    return high, low


def dot(a, b):
    return jnp.dot(a, b, preferred_element_type=F32)


def right_product(values, matrix_high, matrix_low):
    high, low = split(values)
    return dot(high, matrix_high) + dot(low, matrix_high) + dot(high, matrix_low)


def left_product(matrix_high, matrix_low, values):
    high, low = split(values)
    return dot(matrix_high, high) + dot(matrix_high, low) + dot(matrix_low, high)


def compact_x(planes):
    matrix = halo_basis()[1]
    length = CX + 4
    half = length // 2
    odd = [planes[l] - planes[length - 1 - l] for l in range(half)]
    even = [planes[l] + planes[length - 1 - l] for l in range(half)]
    result = [None] * CX
    for i in range(HALF):
        first = None
        second = None
        for l in range(half):
            a = float(0.5 * (matrix[i, l] - matrix[i, length - 1 - l]))
            b = float(0.5 * (matrix[i, l] + matrix[i, length - 1 - l]))
            first = a * odd[l] if first is None else first + a * odd[l]
            second = b * even[l] if second is None else second + b * even[l]
        result[i] = first + second
        result[CX - 1 - i] = first - second
    return result


def extended(before, own, after, f, rows):
    return (
        [before[f, 0, rows, :], before[f, 1, rows, :]]
        + [own[l, rows, :] for l in range(CX)]
        + [after[f, 1, rows, :], after[f, 0, rows, :]]
    )


def halo_sums(values, f, rows, up, down):
    basis = halo_basis()[0]
    for k in range(2):
        top = None
        bottom = None
        for l in range(HALO):
            a = float(basis[k, l]) * values[CX - HALO + l, rows, :]
            b = float(basis[k, l]) * values[HALO - 1 - l, rows, :]
            top = a if top is None else top + a
            bottom = b if bottom is None else bottom + b
        up[f, k, rows, :] = top
        down[f, k, rows, :] = bottom


def row_chunks(rows):
    return [slice(start, start + 8) for start in range(0, rows, 8)]


def flat(values):
    return values.reshape(-1, values.shape[-1])


def core():
    return lax.rem(lax.axis_index("gy"), 2)


def along(parts):
    return jnp.concatenate([flat(part) for part in parts], axis=1)


def kernel_primitives(
    rho_in, mom_in, ene_in, conserved, own, mine, other, for_mate, up, down, arrived
):
    rho = conserved.at[0]
    mom = conserved.at[1:4]
    ene = conserved.at[4]
    copies = [
        pltpu.make_async_copy(source, target, arrived.at[k])
        for k, (source, target) in enumerate(((rho_in, rho), (mom_in, mom), (ene_in, ene)))
    ]
    for copy in copies:
        copy.start()
    for copy in copies:
        copy.wait()

    def plane(x, carry):
        density = rho[x]
        inverse = 1.0 / density
        u = mom[0, x] * inverse
        v = mom[1, x] * inverse
        w = mom[2, x] * inverse
        kinetic = 0.5 * (mom[0, x] * u + mom[1, x] * v + mom[2, x] * w)
        own[U, x] = u
        own[W, x] = w
        own[V, x] = v
        own[T, x] = (heat_ratio - 1.0) * (ene[x] - kinetic) * inverse
        return carry

    lax.fori_loop(0, CX, plane, 0)
    start = HALF * core()
    for f in range(2):
        for i in range(HALF):
            mine[f, i] = own[f, start + i]
            other[f, i] = own[f, HALF - start + i]
            for_mate[f, i] = own[f, HALF - start + i]
    for i in range(HALF):
        mine[2, i] = conserved[0, start + i]
        other[2, i] = conserved[0, HALF - start + i]

    def sums(f, carry):
        for rows in row_chunks(rho.shape[1]):
            halo_sums(own.at[f], f, rows, up, down)
        return carry

    lax.fori_loop(0, 4, sums, 0)


def kernel_pitch_gradients(
    own, peer, y_high, y_low, dy, mu, second_mine, second_other
):
    start = HALF * core()
    for i in range(HALF):
        for f in range(2):
            second_mine[f, i] = own[V + f, start + i]
            second_other[f, i] = own[V + f, HALF - start + i]
    for k, f in enumerate((U, V)):
        dy[k] = left_product(y_high[...], y_low[...], flat(own[f])).reshape(own.shape[1:])

    def plane(x, carry):
        mu[x] = shear_resistance_reference * jnp.exp(
            sutherland_power_law * jnp.log(own[T, x])
        )
        return carry

    lax.fori_loop(0, CX, plane, 0)


def kernel_span_gradients(mine, mate, peer, across, z_high, z_low, dz, for_mate):
    width = mine.shape[-1]
    odd = core()
    for f in range(2):
        values = along([part[f] for part in (mine, mate, peer, across)])
        dz[f] = right_product(values, z_high[odd], z_low[odd])
        for_mate[f] = dz[f, :, width : 2 * width].reshape(mine.shape[1:])


def kernel_flux_x(
    own, conserved, before, after, dy, mu, dz, dz_mate, peer_2,
    dx, mine, other, for_mate, flux, up, down,
):
    rows, width = own.shape[2:]
    odd = core()

    def field(f, carry):
        for rows in row_chunks(own.shape[2]):
            derived = compact_x(extended(before, own.at[f], after, f, rows))
            for x in range(CX):
                dx[f, x, rows, :] = derived[x]
        return carry

    lax.fori_loop(0, 4, field, 0)
    start = HALF * core()
    for i in range(HALF):
        for f in range(2):
            mine[f, i] = dx[f, start + i]
            other[f, i] = dx[f, HALF - start + i]
            for_mate[f, i] = dx[f, HALF - start + i]
        for_mate[2, i] = dx[V, HALF - start + i]
        for_mate[3, i] = own[V, HALF - start + i]
        for_mate[4, i] = own[T, HALF - start + i]
        for_mate[5, i] = conserved[0, HALF - start + i]

    def plane(i, carry):
        at = pl.ds(pl.multiple_of(i * rows, rows), rows)
        for half in range(2):
            x = HALF * half + i
            is_mine = odd == half
            zu = jnp.where(is_mine, dz[0, at, :width], dz_mate[0, i])
            zw = jnp.where(is_mine, dz[1, at, :width], dz_mate[1, i])
            u, w, v, t = (own[f, x] for f in range(4))
            density = conserved[0, x]
            viscosity = mu[x]
            dil = dx[U, x] + dy[1, x] + zw
            s1 = viscosity * (2.0 * dx[U, x] - (2.0 / 3.0) * dil)
            s2 = viscosity * (dx[V, x] + dy[0, x])
            s3 = viscosity * (dx[W, x] + zu)
            m = density * u
            total = m * (enthalpy * t + 0.5 * (u * u + v * v + w * w))
            flux[0, x] = m
            flux[1, x] = m * u + density * t - s1
            flux[2, x] = m * v - s2
            flux[3, x] = m * w - s3
            flux[4, x] = (
                total - (s1 * u + s2 * v + s3 * w) - conduction * viscosity * dx[T, x]
            )
        return carry

    lax.fori_loop(0, HALF, plane, 0)

    def sums(f, carry):
        for chunk in row_chunks(rows):
            halo_sums(flux.at[f], f, chunk, up, down)
        return carry

    lax.fori_loop(0, 5, sums, 0)


def kernel_flux_yz(
    mine, mate, peer, across, mine_2, peer_2, across_2, dx, from_mate, dz,
    y_high, y_low, z_high, z_low, part, mu,
    dz_more, dy_all, dy_near, flux, flux_y,
):
    rows, width = mine.shape[2:]
    near = 2 * width
    odd = core()
    start = HALF * odd
    first = (mine, mate, peer, across)
    second = (mine_2, from_mate.at[3:6], peer_2, across_2)
    yh, yl = y_high[...], y_low[...]
    for f in range(2):
        values = along([place[f] for place in second])
        dz_more[f] = right_product(values, z_high[odd], z_low[odd])
    dy_all[0] = left_product(yh, yl, along([place[0] for place in second]))
    dy_all[1] = left_product(yh, yl, along([place[1] for place in first]))
    dy_near[0] = left_product(yh, yl, along([place[0] for place in first[:2]]))
    dy_near[1] = left_product(yh, yl, along([place[1] for place in second[:2]]))

    def plane(i, carry):
        at = pl.ds(pl.multiple_of(i * rows, rows), rows)
        for k in range(4):
            lanes = slice(k * width, (k + 1) * width)
            u, w = first[k][0, i], first[k][1, i]
            v, t = second[k][0, i], second[k][1, i]
            density = (from_mate[5, i] if k == 1 else first[k][2, i])
            viscosity = shear_resistance_reference * jnp.exp(
                sutherland_power_law * jnp.log(t)
            )
            mu[at, lanes] = viscosity
            zu, zw = dz[0, at, lanes], dz[1, at, lanes]
            zv, zt = dz_more[0, at, lanes], dz_more[1, at, lanes]
            yv, yw = dy_all[0, at, lanes], dy_all[1, at, lanes]
            s1 = zu
            s2 = viscosity * (zv + yw)
            s3 = (4.0 / 3.0) * zw - (2.0 / 3.0) * yv
            if k < 2:
                if k == 0:
                    xu, xw, xv = (dx[f, start + i] for f in range(3))
                else:
                    xu, xw, xv = (from_mate[f, i] for f in range(3))
                s1 = s1 + xw
                s3 = s3 - (2.0 / 3.0) * xu
            s1 = viscosity * s1
            s3 = viscosity * s3
            pressure = density * t
            total = enthalpy * t + 0.5 * (u * u + v * v + w * w)
            m = density * w
            flux[0, at, lanes] = m
            flux[1, at, lanes] = m * u - s1
            flux[2, at, lanes] = m * v - s2
            flux[3, at, lanes] = m * w + pressure - s3
            flux[4, at, lanes] = (
                m * total - (s1 * u + s2 * v + s3 * w) - conduction * viscosity * zt
            )
            if k < 2:
                yu, yt = dy_near[0, at, lanes], dy_near[1, at, lanes]
                dil = xu + yv + zw
                r1 = viscosity * (yu + xv)
                r2 = viscosity * (2.0 * yv - (2.0 / 3.0) * dil)
                m = density * v
                flux_y[0, at, lanes] = m
                flux_y[1, at, lanes] = m * u - r1
                flux_y[2, at, lanes] = m * v + pressure - r2
                flux_y[3, at, lanes] = m * w - s2
                flux_y[4, at, lanes] = (
                    m * total - (r1 * u + r2 * v + s2 * w) - conduction * viscosity * yt
                )
        return carry

    lax.fori_loop(0, HALF, plane, 0)
    for f in range(5):
        spread = right_product(flux[f], z_high[odd, :, :near], z_low[odd, :, :near])
        part[f] = spread + left_product(yh, yl, flux_y[f])


def kernel_corrections(
    peer, across, dx_peer, dx_across, part, mu, z_high, z_low, total, mate_a, mate_b, mate_c
):
    shape = peer.shape[1:]
    width = shape[-1]
    near = 2 * width
    odd = core()
    targets = (mate_a.at[0], mate_a.at[1], mate_b.at[0], mate_b.at[1], mate_c.at[0])
    normal = (2.0 / 3.0) * mu[:, near:] * along([dx_peer[0], dx_across[0]])
    shear = mu[:, near:] * along([dx_peer[1], dx_across[1]])
    energy = normal * along([peer[1], across[1]]) - shear * along([peer[0], across[0]])
    corrections = {1: -shear, 3: normal, 4: energy}
    for f in range(5):
        value = part[f]
        if f in corrections:
            value = value + right_product(
                corrections[f], z_high[odd, near:, :near], z_low[odd, near:, :near]
            )
        total[f] = value[:, :width].reshape(shape)
        targets[f][...] = value[:, width:].reshape(shape)


def kernel_finish(
    conserved, total, mate_a, mate_b, mate_c, flux, before, after, tendency, advanced
):
    odd = core()
    sources = (mate_a.at[0], mate_a.at[1], mate_b.at[0], mate_b.at[1], mate_c.at[0])
    for f in range(5):
        for rows in row_chunks(flux.shape[2]):
            derived = compact_x(extended(before, flux.at[f], after, f, rows))
            for x in range(CX):
                i = x % HALF
                rest = jnp.where(
                    odd == x // HALF, total[f, i, rows, :], sources[f][i, rows, :]
                )
                value = -(rest + derived[x])
                tendency[f, x, rows, :] = value
                advanced[f, x, rows, :] = conserved[f, x, rows, :] + section_step * value


def call(kernel, outputs, operands, scratch=(), outside=False, weight=1):
    space = pltpu.HBM if outside else pltpu.VMEM
    in_specs = [pl.BlockSpec(memory_space=space) for _ in operands]
    if outside:
        operands = [pltpu.with_memory_space_constraint(value, pltpu.HBM) for value in operands]
    touched = sum(value.size * value.dtype.itemsize for value in operands)
    touched += 4 * sum(int(np.prod(shape)) for shape in outputs)
    return pl.pallas_call(
        kernel,
        out_shape=[jax.ShapeDtypeStruct(shape, F32) for shape in outputs],
        in_specs=in_specs,
        out_specs=[pl.BlockSpec(memory_space=pltpu.VMEM) for _ in outputs],
        scratch_shapes=list(scratch),
        cost_estimate=pl.CostEstimate(flops=0, bytes_accessed=weight * touched, transcendentals=0),
        compiler_params=pltpu.CompilerParams(vmem_limit_bytes=24 * 1024 * 1024),
    )(*operands)


def fast_device(mass_per_volume, momentum, energy):
    rho = jnp.transpose(mass_per_volume, (0, 2, 1))
    mom = jnp.transpose(momentum, (0, 1, 3, 2))
    ene = jnp.transpose(energy, (0, 2, 1))
    _, rows, width = rho.shape
    length = 4 * width
    pitch = pitch_matrix(rows, CY)
    z_high, z_low = span_blocks(length, PLACES, PLACES)
    y_high, y_low = halves(np.kron(np.eye(CX, dtype=np.float32), pitch))
    h_high, h_low = halves(np.kron(np.eye(HALF, dtype=np.float32), pitch))
    block = (CX, rows, width)
    half = (HALF, rows, width)
    sums = (2, rows, width)
    points = HALF * rows
    devices = lax.axis_size("gx")
    ring_up = [(i, (i + 1) % devices) for i in range(devices)]
    ring_down = [(j, i) for i, j in ring_up]
    to_mate, to_peer, to_across = ([(i, i ^ k) for i in range(4)] for k in (1, 2, 3))

    conserved, own, mine, other, for_mate, up, down = call(
        kernel_primitives,
        [(5,) + block, (4,) + block, (3,) + half, (3,) + half, (2,) + half, (4,) + sums, (4,) + sums],
        (rho, mom, ene),
        scratch=(pltpu.SemaphoreType.DMA((3,)),),
        outside=True,
    )
    peer = lax.ppermute(mine, "gy", to_peer)
    across = lax.ppermute(other, "gy", to_across)
    before = lax.ppermute(up, "gx", ring_up)
    after = lax.ppermute(down, "gx", ring_down)
    mate = lax.ppermute(for_mate, "gy", to_mate)
    dy, mu, mine_2, other_2 = call(
        kernel_pitch_gradients,
        [(2,) + block, block, (2,) + half, (2,) + half],
        (own, peer, y_high, y_low),
    )
    peer_2 = lax.ppermute(mine_2, "gy", to_peer)
    across_2 = lax.ppermute(other_2, "gy", to_across)
    dz, dz_sent = call(
        kernel_span_gradients,
        [(2, points, length), (2,) + half],
        (mine, mate, peer, across, z_high, z_low),
    )
    dz_mate = lax.ppermute(dz_sent, "gy", to_mate)
    dx, dx_mine, dx_other, sent, flux, flux_up, flux_down = call(
        kernel_flux_x,
        [(4,) + block, (2,) + half, (2,) + half, (6,) + half]
        + [(5,) + block, (5,) + sums, (5,) + sums],
        (own, conserved, before, after, dy, mu, dz, dz_mate, peer_2),
    )
    dx_peer = lax.ppermute(dx_mine, "gy", to_peer)
    dx_across = lax.ppermute(dx_other, "gy", to_across)
    mate_2 = lax.ppermute(sent, "gy", to_mate)
    flux_before = lax.ppermute(flux_up, "gx", ring_up)
    flux_after = lax.ppermute(flux_down, "gx", ring_down)
    part, mu_lines = call(
        kernel_flux_yz,
        [(5, points, 2 * width), (points, length)],
        (
            mine, mate, peer, across, mine_2, peer_2, across_2, dx, mate_2, dz,
            h_high, h_low, z_high, z_low,
        ),
        weight=1,
        scratch=(
            pltpu.VMEM((2, points, length), F32),
            pltpu.VMEM((2, points, length), F32),
            pltpu.VMEM((2, points, 2 * width), F32),
            pltpu.VMEM((5, points, length), F32),
            pltpu.VMEM((5, points, 2 * width), F32),
        ),
    )
    total, *for_mate = call(
        kernel_corrections,
        [(5,) + half, (2,) + half, (2,) + half, (1,) + half],
        (peer, across, dx_peer, dx_across, part, mu_lines, z_high, z_low),
    )
    from_mate = [lax.ppermute(value, "gy", to_mate) for value in for_mate]
    tendency, advanced = call(
        kernel_finish,
        [(5,) + block, (5,) + block],
        (conserved, total, *from_mate, flux, flux_before, flux_after),
    )
    return (
        jnp.transpose(tendency, (0, 1, 3, 2)),
        jnp.transpose(advanced, (0, 1, 3, 2)),
    )


def padded(array, sides, width):
    for axis, dim in sides:
        devices, length = (lax.axis_size(axis), array.shape[dim])
        up = [(i, (i + 1) % devices) for i in range(devices)]
        down = [(j, i) for i, j in up]
        last = lax.slice_in_dim(array, length - width, length, axis=dim)
        initial = lax.slice_in_dim(array, 0, width, axis=dim)
        before = lax.ppermute(last, axis, up)
        after = lax.ppermute(initial, axis, down)
        array = jnp.concatenate([before, array, after], axis=dim)
    return array


def right_side(conserved, gradients_of, derive_x, derive_y, derive_z):
    mass_per_volume = conserved[0]
    momentum = conserved[1:4]
    energy = conserved[4]
    local_speed_vector = momentum / mass_per_volume
    kinetic = 0.5 * jnp.sum(momentum * local_speed_vector, axis=0)
    normal_force_per_area = (heat_ratio - 1.0) * (energy - kinetic)
    thermal_state = normal_force_per_area / mass_per_volume
    basic_quantities = jnp.concatenate([local_speed_vector, thermal_state[None]], 0)
    gradients = gradients_of(basic_quantities)
    shear_resistance = shear_resistance_reference * jnp.power(thermal_state, sutherland_power_law)
    conductivity = shear_resistance * heat_ratio / ((heat_ratio - 1.0) * prandtl)
    dilatation = gradients[0][0] + gradients[1][1] + gradients[2][2]
    derivers = (derive_x, derive_y, derive_z)
    accumulated = None
    for direction in range(3):
        stress_column = [
            shear_resistance * (gradients[direction][component] + gradients[component][direction])
            for component in range(3)
        ]
        stress_column[direction] = (
            stress_column[direction] - 2.0 / 3.0 * shear_resistance * dilatation
        )
        fluxes = [momentum[direction]]
        for component in range(3):
            moment_flux = (
                momentum[component] * local_speed_vector[direction] - stress_column[component]
            )
            if component == direction:
                moment_flux = moment_flux + normal_force_per_area
            fluxes.append(moment_flux)
        work_term = (
            stress_column[0] * local_speed_vector[0]
            + stress_column[1] * local_speed_vector[1]
            + stress_column[2] * local_speed_vector[2]
        )
        fluxes.append(
            (energy + normal_force_per_area) * local_speed_vector[direction]
            - work_term
            - conductivity * gradients[direction][3]
        )
        divergence_part = derivers[direction](jnp.stack(fluxes))
        accumulated = divergence_part if accumulated is None else accumulated + divergence_part
    return -accumulated


def plain_device(mass_per_volume, momentum, energy):
    conserved = jnp.concatenate([mass_per_volume[None], momentum, energy[None]], 0)
    highest = lax.Precision.HIGHEST
    x_matrix = jnp.asarray(compact_matrix(CX, HALO))
    z_matrix = jnp.asarray(span_matrix(NZ))

    def apply_x(extended):
        return jnp.einsum("il,flab->fiab", x_matrix, extended, precision=highest)

    def flux_x(values):
        return apply_x(padded(values, (("gx", 1),), HALO))

    y_matrix = jnp.asarray(pitch_matrix(conserved.shape[3], CY))

    def apply_y(values):
        return jnp.einsum("fabk,jk->fabj", values, y_matrix, precision=highest)

    def derive_span(values):
        lines = jnp.transpose(
            lax.all_to_all(values, "gy", split_axis=3, concat_axis=2, tiled=True), (0, 1, 3, 2)
        )
        derived = jnp.einsum("fack,jk->facj", lines, z_matrix, precision=highest)
        returned = lax.all_to_all(derived, "gy", split_axis=3, concat_axis=2, tiled=True)
        return jnp.transpose(returned, (0, 1, 3, 2))

    def gradients_of(basic_quantities):
        extended = padded(basic_quantities, (("gx", 1),), HALO)
        return (apply_x(extended), apply_y(basic_quantities), derive_span(basic_quantities))

    tendency = right_side(conserved, gradients_of, flux_x, apply_y, derive_span)
    advanced = conserved + section_step * tendency
    return (tendency, advanced)


def per_device(mass_per_volume, momentum, energy):
    planes, width, rows = mass_per_volume.shape
    fits = planes == CX and width % 128 == 0 and rows <= 32 and rows % CY == 0
    if fits and lax.axis_size("gy") == 4:
        return fast_device(mass_per_volume, momentum, energy)
    return plain_device(mass_per_volume, momentum, energy)


def solution(mesh):
    in_specs = (P("gx", "gy", None), P(None, "gx", "gy", None), P("gx", "gy", None))
    out_specs = (P(None, "gx", "gy", None), P(None, "gx", "gy", None))
    return jax.shard_map(
        per_device, mesh=mesh, in_specs=in_specs, out_specs=out_specs, check_vma=False
    )
```

```python
import functools

import jax
import jax.numpy as jnp
import numpy as np
from jax import lax
from jax.experimental import pallas as pl
from jax.experimental.pallas import tpu as pltpu
from jax.sharding import PartitionSpec as P

CX = 8
CY = 8
NZ = 512
HALO = 4


heat_ratio = 1.4
shear_resistance_reference = 0.08
sutherland_power_law = 0.7
prandtl = 0.72
section_step = 0.05
compact_alpha = 1.0 / 3.0
compact_near = 14.0 / 9.0
compact_far = 1.0 / 9.0

conduction = heat_ratio / ((heat_ratio - 1.0) * prandtl)
enthalpy = heat_ratio / (heat_ratio - 1.0)


def tridiagonal_inverse_product(length, stencil):
    solved = np.array(stencil)
    upper_ratio = np.zeros(length)
    for row_index in range(length):
        if row_index == 0:
            pivot_value = 1.0
            solved[row_index] = solved[row_index] / pivot_value
        else:
            pivot_value = 1.0 - compact_alpha * upper_ratio[row_index - 1]
            solved[row_index] = (
                solved[row_index] - compact_alpha * solved[row_index - 1]
            ) / pivot_value
        upper_ratio[row_index] = compact_alpha / pivot_value
    for row_index in range(length - 2, -1, -1):
        solved[row_index] = solved[row_index] - upper_ratio[row_index] * solved[row_index + 1]
    return solved


def exact_compact_matrix(block_size, margin):
    length = block_size + 2 * margin
    stencil = compact_near / 2.0 * (np.eye(length, k=1) - np.eye(length, k=-1))
    stencil = stencil + compact_far / 4.0 * (np.eye(length, k=2) - np.eye(length, k=-2))
    inverse_product = tridiagonal_inverse_product(length, stencil)
    return inverse_product[margin : margin + block_size]


def compact_matrix(block_size, margin):
    return exact_compact_matrix(block_size, margin).astype(np.float32)


def pitch_matrix(total, block_size):
    matrix = compact_matrix(block_size, HALO)
    result = np.zeros((total, total), np.float32)
    rows_all = np.arange(total)
    block_start = rows_all // block_size * block_size
    for offset in range(block_size + 2 * HALO):
        columns = (block_start - HALO + offset) % total
        result[rows_all, columns] += matrix[rows_all % block_size, offset]
    return result


def span_matrix(total):
    offsets = np.arange(total)[:, None] - np.arange(total)[None, :]
    angles = np.pi * offsets / total
    signs = np.where(offsets % 2 == 0, 1.0, -1.0)
    sines = np.where(offsets == 0, 1.0, np.sin(angles))
    result = np.where(offsets == 0, 0.0, np.pi / total * signs * np.cos(angles) / sines)
    return result.astype(np.float32)


F32 = jnp.float32
BF16 = jnp.bfloat16
U, W, V, T, R = range(5)
PLACES = (0, 2, 1, 3)
HALF = CX // 2


def halves(matrix):
    high = np.asarray(matrix, np.float32).astype(BF16)
    low = (matrix - high.astype(np.float32)).astype(BF16)
    return jnp.asarray(high), jnp.asarray(low)


def span_blocks(length, sources, targets):
    width = length // 4
    matrix = span_matrix(length).T
    both = []
    for core in range(2):
        columns = []
        for target in targets:
            to = core ^ target
            columns.append(
                np.concatenate(
                    [
                        matrix[
                            (core ^ source) * width : (core ^ source) * width + width,
                            to * width : to * width + width,
                        ]
                        for source in sources
                    ],
                    axis=0,
                )
            )
        both.append(np.concatenate(columns, axis=1))
    return halves(np.stack(both))


def halo_basis():
    matrix = exact_compact_matrix(CX, HALO)
    left = matrix[:, :HALO]
    basis = np.linalg.svd(left)[2][:2]
    inner = left @ basis.T
    outer = -inner[::-1]
    return basis, np.concatenate(
        [inner, matrix[:, HALO : HALO + CX], outer[:, ::-1]], axis=1
    )


def split(values):
    high = values.astype(BF16)
    low = (values - high.astype(F32)).astype(BF16)
    return high, low


def dot(a, b):
    return jnp.dot(a, b, preferred_element_type=F32)


def right_product(values, matrix_high, matrix_low):
    high, low = split(values)
    return dot(high, matrix_high) + dot(low, matrix_high) + dot(high, matrix_low)


def left_product(matrix_high, matrix_low, values):
    high, low = split(values)
    return dot(matrix_high, high) + dot(matrix_high, low) + dot(matrix_low, high)


def compact_x(planes):
    matrix = halo_basis()[1]
    length = CX + 4
    half = length // 2
    odd = [planes[l] - planes[length - 1 - l] for l in range(half)]
    even = [planes[l] + planes[length - 1 - l] for l in range(half)]
    result = [None] * CX
    for i in range(HALF):
        first = None
        second = None
        for l in range(half):
            a = float(0.5 * (matrix[i, l] - matrix[i, length - 1 - l]))
            b = float(0.5 * (matrix[i, l] + matrix[i, length - 1 - l]))
            first = a * odd[l] if first is None else first + a * odd[l]
            second = b * even[l] if second is None else second + b * even[l]
        result[i] = first + second
        result[CX - 1 - i] = first - second
    return result


def extended(before, own, after, f, rows):
    return (
        [before[f, 0, rows, :], before[f, 1, rows, :]]
        + [own[f, l, rows, :] for l in range(CX)]
        + [after[f, 1, rows, :], after[f, 0, rows, :]]
    )


def halo_sums(values, f, rows, up, down):
    basis = halo_basis()[0]
    for k in range(2):
        top = None
        bottom = None
        for l in range(HALO):
            a = float(basis[k, l]) * values[f, CX - HALO + l, rows, :]
            b = float(basis[k, l]) * values[f, HALO - 1 - l, rows, :]
            top = a if top is None else top + a
            bottom = b if bottom is None else bottom + b
        up[f, k, rows, :] = top
        down[f, k, rows, :] = bottom


def row_chunks(rows):
    return [slice(start, start + 8) for start in range(0, rows, 8)]


def flat(values):
    return values.reshape(-1, values.shape[-1])


def kernel_primitives(
    rho_in, mom_in, ene_in, conserved, own, first, up, down, arrived
):
    rho = conserved.at[0]
    mom = conserved.at[1:4]
    ene = conserved.at[4]
    copies = [
        pltpu.make_async_copy(source, target, arrived.at[k])
        for k, (source, target) in enumerate(((rho_in, rho), (mom_in, mom), (ene_in, ene)))
    ]
    for copy in copies:
        copy.start()
    for copy in copies:
        copy.wait()

    def plane(x, carry):
        density = rho[x]
        inverse = 1.0 / density
        u = mom[0, x] * inverse
        v = mom[1, x] * inverse
        w = mom[2, x] * inverse
        kinetic = 0.5 * (mom[0, x] * u + mom[1, x] * v + mom[2, x] * w)
        temperature = (heat_ratio - 1.0) * (ene[x] - kinetic) * inverse
        own[U, x] = u
        own[W, x] = w
        own[V, x] = v
        own[T, x] = temperature
        first[0, x] = u
        first[1, x] = w
        return carry

    lax.fori_loop(0, CX, plane, 0)

    def sums(f, carry):
        for rows in row_chunks(rho.shape[1]):
            halo_sums(own, f, rows, up, down)
        return carry

    lax.fori_loop(0, 4, sums, 0)


def kernel_pitch_gradients(
    own, conserved, y_high, y_low, dy, mu, second, mate_a, mate_b
):
    for f in range(4):
        dy[f] = left_product(y_high[...], y_low[...], flat(own[f])).reshape(own.shape[1:])

    def plane(x, carry):
        mu[x] = shear_resistance_reference * jnp.exp(
            sutherland_power_law * jnp.log(own[T, x])
        )
        for f in range(2):
            mate_a[f, x] = own[f, x]
            mate_b[f, x] = own[V + f, x]
        second[0, x] = own[V, x]
        second[1, x] = own[T, x]
        second[2, x] = conserved[0, x]
        return carry

    lax.fori_loop(0, CX, plane, 0)


def kernel_stream_gradients(own, before, after, mu, dx, third):
    def field(f, carry):
        for rows in row_chunks(own.shape[2]):
            derived = compact_x(extended(before, own, after, f, rows))
            for x in range(CX):
                dx[f, x, rows, :] = derived[x]
        return carry

    lax.fori_loop(0, 4, field, 0)

    def plane(x, carry):
        third[0, x] = (2.0 / 3.0) * mu[x] * dx[U, x]
        third[1, x] = mu[x] * dx[W, x]
        return carry

    lax.fori_loop(0, CX, plane, 0)


def kernel_flux_x(
    own, second, peer_first, first_mate, across_first, dx, dy, mu, z_high, z_low,
    dz, flux, up, down,
):
    width = own.shape[-1]
    odd = lax.rem(lax.axis_index("gy"), 2)
    for f in range(2):
        values = jnp.concatenate(
            [flat(own[f]), flat(peer_first[f]), flat(first_mate[f]), flat(across_first[f])], axis=1
        )
        dz[f] = right_product(values, z_high[odd], z_low[odd])

    rows = own.shape[2]

    def plane(x, carry):
        at = pl.ds(pl.multiple_of(x * rows, rows), rows)
        u, w, v, t = (own[f, x] for f in range(4))
        density = second[2, x]
        viscosity = mu[x]
        dil = dx[U, x] + dy[V, x] + dz[1, at, :width]
        s1 = viscosity * (2.0 * dx[U, x] - (2.0 / 3.0) * dil)
        s2 = viscosity * (dx[V, x] + dy[U, x])
        s3 = viscosity * (dx[W, x] + dz[0, at, :width])
        m = density * u
        total = m * (enthalpy * t + 0.5 * (u * u + v * v + w * w))
        flux[0, x] = m
        flux[1, x] = m * u + density * t - s1
        flux[2, x] = m * v - s2
        flux[3, x] = m * w - s3
        flux[4, x] = total - (s1 * u + s2 * v + s3 * w) - conduction * viscosity * dx[T, x]
        return carry

    lax.fori_loop(0, CX, plane, 0)

    def sums(f, carry):
        for chunk in row_chunks(rows):
            halo_sums(flux, f, chunk, up, down)
        return carry

    lax.fori_loop(0, 5, sums, 0)


def kernel_peer(peer_first, peer_second, flux, y_high, y_low, for_v, for_t, dy_peer):
    for_v[...] = peer_second[0]
    for_t[...] = peer_second[1]
    dy_peer[0] = left_product(y_high[...], y_low[...], flat(peer_second[0]))
    dy_peer[1] = left_product(y_high[...], y_low[...], flat(peer_first[1]))


def kernel_flux_yz(
    own, second, peer_first, peer_second, second_mate, across_v, across_t, dy_peer,
    dz, dx, dy, mu, y_high, y_low, z_high, z_low, f_high, f_low, part, part_mate,
    dz_more, flux, flux_y,
):
    rows, width = own.shape[2:]
    odd = lax.rem(lax.axis_index("gy"), 2)
    for f, across in enumerate((across_v, across_t)):
        values = jnp.concatenate(
            [flat(own[V + f]), flat(peer_second[f]), flat(second_mate[f]), flat(across[...])],
            axis=1,
        )
        dz_more[f] = right_product(values, z_high[odd], z_low[odd])

    def span_flux(at, lanes, u, w, v, t, density, viscosity, yv, yw):
        s1 = viscosity * dz[0, at, lanes]
        s2 = viscosity * (dz_more[0, at, lanes] + yw)
        s3 = viscosity * ((4.0 / 3.0) * dz[1, at, lanes] - (2.0 / 3.0) * yv)
        m = density * w
        total = m * (enthalpy * t + 0.5 * (u * u + v * v + w * w))
        flux[0, at, lanes] = m
        flux[1, at, lanes] = m * u - s1
        flux[2, at, lanes] = m * v - s2
        flux[3, at, lanes] = m * w + density * t - s3
        flux[4, at, lanes] = (
            total
            - (s1 * u + s2 * v + s3 * w)
            - conduction * viscosity * dz_more[1, at, lanes]
        )

    def plane(x, carry):
        at = pl.ds(pl.multiple_of(x * rows, rows), rows)
        here = slice(0, width)
        u, w, v, t = (own[f, x] for f in range(4))
        density = second[2, x]
        viscosity = mu[x]
        span_flux(at, here, u, w, v, t, density, viscosity, dy[V, x], dy[W, x])
        dil = dx[U, x] + dy[V, x] + dz[1, at, here]
        s1 = viscosity * (dy[U, x] + dx[V, x])
        s2 = viscosity * (2.0 * dy[V, x] - (2.0 / 3.0) * dil)
        s3 = viscosity * (dy[W, x] + dz_more[0, at, here])
        m = density * v
        total = m * (enthalpy * t + 0.5 * (u * u + v * v + w * w))
        flux_y[0, at, :] = m
        flux_y[1, at, :] = m * u - s1
        flux_y[2, at, :] = m * v + density * t - s2
        flux_y[3, at, :] = m * w - s3
        flux_y[4, at, :] = (
            total - (s1 * u + s2 * v + s3 * w) - conduction * viscosity * dy[T, x]
        )
        t = peer_second[1, x]
        viscosity = shear_resistance_reference * jnp.exp(sutherland_power_law * jnp.log(t))
        span_flux(
            at, slice(width, 2 * width), peer_first[0, x], peer_first[1, x],
            peer_second[0, x], t, peer_second[2, x], viscosity,
            dy_peer[0, at, :], dy_peer[1, at, :],
        )
        return carry

    lax.fori_loop(0, CX, plane, 0)
    shape = own.shape[1:]
    for f in range(5):
        spread = right_product(flux[f], f_high[odd], f_low[odd])
        local = left_product(y_high[...], y_low[...], flux_y[f])
        part[f] = (spread[:, :width] + local).reshape(shape)
        part_mate[f] = spread[:, width:].reshape(shape)


def kernel_corrections(
    own, peer_first, third, peer_third, part, part_mate, f_high, f_low, total, *for_mate
):
    width = own.shape[-1]
    odd = lax.rem(lax.axis_index("gy"), 2)
    shape = own.shape[1:]
    for f in (0, 2):
        total[f] = part[f]
        for_mate[f][...] = part_mate[f]
    pairs = ((own, third), (peer_first, peer_third))
    for f in (1, 3, 4):
        sides = []
        for speeds, shared in pairs:
            if f == 1:
                value = -shared[1]
            elif f == 3:
                value = shared[0]
            else:
                value = shared[0] * speeds[W] - shared[1] * speeds[U]
            sides.append(flat(value))
        spread = right_product(jnp.concatenate(sides, axis=1), f_high[odd], f_low[odd])
        total[f] = part[f] + spread[:, :width].reshape(shape)
        for_mate[f][...] = part_mate[f] + spread[:, width:].reshape(shape)


def kernel_finish(
    conserved, total, mate_0, mate_1, mate_2, mate_3, mate_4, flux, before, after,
    tendency, advanced,
):
    for f, from_mate in enumerate((mate_0, mate_1, mate_2, mate_3, mate_4)):
        for rows in row_chunks(flux.shape[2]):
            derived = compact_x(extended(before, flux, after, f, rows))
            for x in range(CX):
                value = -(total[f, x, rows, :] + from_mate[x, rows, :] + derived[x])
                tendency[f, x, rows, :] = value
                advanced[f, x, rows, :] = conserved[f, x, rows, :] + section_step * value


def call(kernel, outputs, operands, scratch=(), outside=False):
    space = pltpu.HBM if outside else pltpu.VMEM
    in_specs = [pl.BlockSpec(memory_space=space) for _ in operands]
    if outside:
        operands = [pltpu.with_memory_space_constraint(value, pltpu.HBM) for value in operands]
    touched = sum(value.size * value.dtype.itemsize for value in operands)
    touched += 4 * sum(int(np.prod(shape)) for shape in outputs)
    return pl.pallas_call(
        kernel,
        out_shape=[jax.ShapeDtypeStruct(shape, F32) for shape in outputs],
        in_specs=in_specs,
        out_specs=[pl.BlockSpec(memory_space=pltpu.VMEM) for _ in outputs],
        scratch_shapes=list(scratch),
        cost_estimate=pl.CostEstimate(flops=0, bytes_accessed=touched, transcendentals=0),
        compiler_params=pltpu.CompilerParams(vmem_limit_bytes=24 * 1024 * 1024),
    )(*operands)


def fast_device(mass_per_volume, momentum, energy):
    rho = jnp.transpose(mass_per_volume, (0, 2, 1))
    mom = jnp.transpose(momentum, (0, 1, 3, 2))
    ene = jnp.transpose(energy, (0, 2, 1))
    _, rows, width = rho.shape
    length = 4 * width
    z_high, z_low = span_blocks(length, PLACES, PLACES[:2])
    f_high, f_low = span_blocks(length, PLACES[:2], (0, 1))
    y_high, y_low = halves(np.kron(np.eye(CX, dtype=np.float32), pitch_matrix(rows, CY)))
    block = (CX, rows, width)
    sums = (2, rows, width)
    points = CX * rows
    devices = lax.axis_size("gx")
    ring_up = [(i, (i + 1) % devices) for i in range(devices)]
    ring_down = [(j, i) for i, j in ring_up]
    to_mate = [(i, i ^ 1) for i in range(4)]
    to_peer = [(i, i ^ 2) for i in range(4)]

    conserved, own, first, up, down = call(
        kernel_primitives,
        [(5,) + block, (4,) + block, (2,) + block, (4,) + sums, (4,) + sums],
        (rho, mom, ene),
        scratch=(pltpu.SemaphoreType.DMA((3,)),),
        outside=True,
    )
    peer_first = lax.ppermute(first, "gy", to_peer)
    before = lax.ppermute(up, "gx", ring_up)
    after = lax.ppermute(down, "gx", ring_down)
    dy, mu, second, mate_a, mate_b = call(
        kernel_pitch_gradients,
        [(4,) + block, block, (3,) + block, (2,) + block, (2,) + block],
        (own, conserved, y_high, y_low),
    )
    first_mate = lax.ppermute(mate_a, "gy", to_mate)
    second_mate = lax.ppermute(mate_b, "gy", to_mate)
    peer_second = lax.ppermute(second, "gy", to_peer)
    peer_first, before, after = lax.optimization_barrier((peer_first, before, after))
    across_first = lax.ppermute(peer_first, "gy", to_mate)
    dx, third = call(
        kernel_stream_gradients, [(4,) + block, (2,) + block], (own, before, after, mu)
    )
    peer_third = lax.ppermute(third, "gy", to_peer)
    dz, flux, flux_up, flux_down = call(
        kernel_flux_x,
        [(2, points, 2 * width), (5,) + block, (5,) + sums, (5,) + sums],
        (own, second, peer_first, first_mate, across_first, dx, dy, mu, z_high, z_low),
    )
    flux_before = lax.ppermute(flux_up, "gx", ring_up)
    flux_after = lax.ppermute(flux_down, "gx", ring_down)
    for_v, for_t, dy_peer = call(
        kernel_peer,
        [block, block, (2, points, width)],
        (peer_first, peer_second, flux, y_high, y_low),
    )
    across_v = lax.ppermute(for_v, "gy", to_mate)
    across_t = lax.ppermute(for_t, "gy", to_mate)
    part, part_mate = call(
        kernel_flux_yz,
        [(5,) + block, (5,) + block],
        (
            own, second, peer_first, peer_second, second_mate, across_v, across_t, dy_peer,
            dz, dx, dy, mu, y_high, y_low, z_high, z_low, f_high, f_low,
        ),
        scratch=(
            pltpu.VMEM((2, points, 2 * width), F32),
            pltpu.VMEM((5, points, 2 * width), F32),
            pltpu.VMEM((5, points, width), F32),
        ),
    )
    total, *for_mate = call(
        kernel_corrections,
        [(5,) + block] + 5 * [block],
        (own, peer_first, third, peer_third, part, part_mate, f_high, f_low),
    )
    from_mate = [lax.ppermute(value, "gy", to_mate) for value in for_mate]
    tendency, advanced = call(
        kernel_finish,
        [(5,) + block, (5,) + block],
        (conserved, total, *from_mate, flux, flux_before, flux_after),
    )
    return (
        jnp.transpose(tendency, (0, 1, 3, 2)),
        jnp.transpose(advanced, (0, 1, 3, 2)),
    )


def padded(array, sides, width):
    for axis, dim in sides:
        devices, length = (lax.axis_size(axis), array.shape[dim])
        up = [(i, (i + 1) % devices) for i in range(devices)]
        down = [(j, i) for i, j in up]
        last = lax.slice_in_dim(array, length - width, length, axis=dim)
        initial = lax.slice_in_dim(array, 0, width, axis=dim)
        before = lax.ppermute(last, axis, up)
        after = lax.ppermute(initial, axis, down)
        array = jnp.concatenate([before, array, after], axis=dim)
    return array


def right_side(conserved, gradients_of, derive_x, derive_y, derive_z):
    mass_per_volume = conserved[0]
    momentum = conserved[1:4]
    energy = conserved[4]
    local_speed_vector = momentum / mass_per_volume
    kinetic = 0.5 * jnp.sum(momentum * local_speed_vector, axis=0)
    normal_force_per_area = (heat_ratio - 1.0) * (energy - kinetic)
    thermal_state = normal_force_per_area / mass_per_volume
    basic_quantities = jnp.concatenate([local_speed_vector, thermal_state[None]], 0)
    gradients = gradients_of(basic_quantities)
    shear_resistance = shear_resistance_reference * jnp.power(thermal_state, sutherland_power_law)
    conductivity = shear_resistance * heat_ratio / ((heat_ratio - 1.0) * prandtl)
    dilatation = gradients[0][0] + gradients[1][1] + gradients[2][2]
    derivers = (derive_x, derive_y, derive_z)
    accumulated = None
    for direction in range(3):
        stress_column = [
            shear_resistance * (gradients[direction][component] + gradients[component][direction])
            for component in range(3)
        ]
        stress_column[direction] = (
            stress_column[direction] - 2.0 / 3.0 * shear_resistance * dilatation
        )
        fluxes = [momentum[direction]]
        for component in range(3):
            moment_flux = (
                momentum[component] * local_speed_vector[direction] - stress_column[component]
            )
            if component == direction:
                moment_flux = moment_flux + normal_force_per_area
            fluxes.append(moment_flux)
        work_term = (
            stress_column[0] * local_speed_vector[0]
            + stress_column[1] * local_speed_vector[1]
            + stress_column[2] * local_speed_vector[2]
        )
        fluxes.append(
            (energy + normal_force_per_area) * local_speed_vector[direction]
            - work_term
            - conductivity * gradients[direction][3]
        )
        divergence_part = derivers[direction](jnp.stack(fluxes))
        accumulated = divergence_part if accumulated is None else accumulated + divergence_part
    return -accumulated


def plain_device(mass_per_volume, momentum, energy):
    conserved = jnp.concatenate([mass_per_volume[None], momentum, energy[None]], 0)
    highest = lax.Precision.HIGHEST
    x_matrix = jnp.asarray(compact_matrix(CX, HALO))
    z_matrix = jnp.asarray(span_matrix(NZ))

    def apply_x(extended):
        return jnp.einsum("il,flab->fiab", x_matrix, extended, precision=highest)

    def flux_x(values):
        return apply_x(padded(values, (("gx", 1),), HALO))

    y_matrix = jnp.asarray(pitch_matrix(conserved.shape[3], CY))

    def apply_y(values):
        return jnp.einsum("fabk,jk->fabj", values, y_matrix, precision=highest)

    def derive_span(values):
        lines = jnp.transpose(
            lax.all_to_all(values, "gy", split_axis=3, concat_axis=2, tiled=True), (0, 1, 3, 2)
        )
        derived = jnp.einsum("fack,jk->facj", lines, z_matrix, precision=highest)
        returned = lax.all_to_all(derived, "gy", split_axis=3, concat_axis=2, tiled=True)
        return jnp.transpose(returned, (0, 1, 3, 2))

    def gradients_of(basic_quantities):
        extended = padded(basic_quantities, (("gx", 1),), HALO)
        return (apply_x(extended), apply_y(basic_quantities), derive_span(basic_quantities))

    tendency = right_side(conserved, gradients_of, flux_x, apply_y, derive_span)
    advanced = conserved + section_step * tendency
    return (tendency, advanced)


def per_device(mass_per_volume, momentum, energy):
    planes, width, rows = mass_per_volume.shape
    fits = planes == CX and width % 128 == 0 and rows <= 32 and rows % CY == 0
    if fits and lax.axis_size("gy") == 4:
        return fast_device(mass_per_volume, momentum, energy)
    return plain_device(mass_per_volume, momentum, energy)


def solution(mesh):
    in_specs = (P("gx", "gy", None), P(None, "gx", "gy", None), P("gx", "gy", None))
    out_specs = (P(None, "gx", "gy", None), P(None, "gx", "gy", None))
    return jax.shard_map(
        per_device, mesh=mesh, in_specs=in_specs, out_specs=out_specs, check_vma=False
    )
```

```python
import functools

import jax
import jax.numpy as jnp
import numpy as np
from jax import lax
from jax.experimental import pallas as pl
from jax.experimental.pallas import tpu as pltpu
from jax.sharding import PartitionSpec as P

CX = 8
CY = 8
NZ = 512
HALO = 4


heat_ratio = 1.4
shear_resistance_reference = 0.08
sutherland_power_law = 0.7
prandtl = 0.72
section_step = 0.05
compact_alpha = 1.0 / 3.0
compact_near = 14.0 / 9.0
compact_far = 1.0 / 9.0

conduction = heat_ratio / ((heat_ratio - 1.0) * prandtl)
enthalpy = heat_ratio / (heat_ratio - 1.0)


def tridiagonal_inverse_product(length, stencil):
    solved = np.array(stencil)
    upper_ratio = np.zeros(length)
    for row_index in range(length):
        if row_index == 0:
            pivot_value = 1.0
            solved[row_index] = solved[row_index] / pivot_value
        else:
            pivot_value = 1.0 - compact_alpha * upper_ratio[row_index - 1]
            solved[row_index] = (
                solved[row_index] - compact_alpha * solved[row_index - 1]
            ) / pivot_value
        upper_ratio[row_index] = compact_alpha / pivot_value
    for row_index in range(length - 2, -1, -1):
        solved[row_index] = solved[row_index] - upper_ratio[row_index] * solved[row_index + 1]
    return solved


def exact_compact_matrix(block_size, margin):
    length = block_size + 2 * margin
    stencil = compact_near / 2.0 * (np.eye(length, k=1) - np.eye(length, k=-1))
    stencil = stencil + compact_far / 4.0 * (np.eye(length, k=2) - np.eye(length, k=-2))
    inverse_product = tridiagonal_inverse_product(length, stencil)
    return inverse_product[margin : margin + block_size]


def compact_matrix(block_size, margin):
    return exact_compact_matrix(block_size, margin).astype(np.float32)


def pitch_matrix(total, block_size):
    matrix = compact_matrix(block_size, HALO)
    result = np.zeros((total, total), np.float32)
    rows_all = np.arange(total)
    block_start = rows_all // block_size * block_size
    for offset in range(block_size + 2 * HALO):
        columns = (block_start - HALO + offset) % total
        result[rows_all, columns] += matrix[rows_all % block_size, offset]
    return result


def span_matrix(total):
    offsets = np.arange(total)[:, None] - np.arange(total)[None, :]
    angles = np.pi * offsets / total
    signs = np.where(offsets % 2 == 0, 1.0, -1.0)
    sines = np.where(offsets == 0, 1.0, np.sin(angles))
    result = np.where(offsets == 0, 0.0, np.pi / total * signs * np.cos(angles) / sines)
    return result.astype(np.float32)


F32 = jnp.float32
BF16 = jnp.bfloat16
U, W, V, T, R = range(5)
PLACES = (0, 2, 1, 3)
HALF = CX // 2


def halves(matrix):
    high = np.asarray(matrix, np.float32).astype(BF16)
    low = (matrix - high.astype(np.float32)).astype(BF16)
    return jnp.asarray(high), jnp.asarray(low)


def span_blocks(length, sources, targets):
    width = length // 4
    matrix = span_matrix(length).T
    both = []
    for core in range(2):
        columns = []
        for target in targets:
            to = core ^ target
            columns.append(
                np.concatenate(
                    [
                        matrix[
                            (core ^ source) * width : (core ^ source) * width + width,
                            to * width : to * width + width,
                        ]
                        for source in sources
                    ],
                    axis=0,
                )
            )
        both.append(np.concatenate(columns, axis=1))
    return halves(np.stack(both))


def halo_basis():
    matrix = exact_compact_matrix(CX, HALO)
    left = matrix[:, :HALO]
    basis = np.linalg.svd(left)[2][:2]
    inner = left @ basis.T
    outer = -inner[::-1]
    return basis, np.concatenate(
        [inner, matrix[:, HALO : HALO + CX], outer[:, ::-1]], axis=1
    )


def split(values):
    high = values.astype(BF16)
    low = (values - high.astype(F32)).astype(BF16)
    return high, low


def dot(a, b):
    return jnp.dot(a, b, preferred_element_type=F32)


def right_product(values, matrix_high, matrix_low):
    high, low = split(values)
    return dot(high, matrix_high) + dot(low, matrix_high) + dot(high, matrix_low)


def left_product(matrix_high, matrix_low, values):
    high, low = split(values)
    return dot(matrix_high, high) + dot(matrix_high, low) + dot(matrix_low, high)


def compact_x(planes):
    matrix = halo_basis()[1]
    length = CX + 4
    half = length // 2
    odd = [planes[l] - planes[length - 1 - l] for l in range(half)]
    even = [planes[l] + planes[length - 1 - l] for l in range(half)]
    result = [None] * CX
    for i in range(HALF):
        first = None
        second = None
        for l in range(half):
            a = float(0.5 * (matrix[i, l] - matrix[i, length - 1 - l]))
            b = float(0.5 * (matrix[i, l] + matrix[i, length - 1 - l]))
            first = a * odd[l] if first is None else first + a * odd[l]
            second = b * even[l] if second is None else second + b * even[l]
        result[i] = first + second
        result[CX - 1 - i] = first - second
    return result


def extended(before, own, after, f, rows):
    return (
        [before[f, 0, rows, :], before[f, 1, rows, :]]
        + [own[f, l, rows, :] for l in range(CX)]
        + [after[f, 1, rows, :], after[f, 0, rows, :]]
    )


def halo_sums(values, f, rows, up, down):
    basis = halo_basis()[0]
    for k in range(2):
        top = None
        bottom = None
        for l in range(HALO):
            a = float(basis[k, l]) * values[f, CX - HALO + l, rows, :]
            b = float(basis[k, l]) * values[f, HALO - 1 - l, rows, :]
            top = a if top is None else top + a
            bottom = b if bottom is None else bottom + b
        up[f, k, rows, :] = top
        down[f, k, rows, :] = bottom


def row_chunks(rows):
    return [slice(start, start + 8) for start in range(0, rows, 8)]


def flat(values):
    return values.reshape(-1, values.shape[-1])


def kernel_primitives(
    rho_in, mom_in, ene_in, conserved, own, first, second, up, down, arrived
):
    rho = conserved.at[0]
    mom = conserved.at[1:4]
    ene = conserved.at[4]
    copies = [
        pltpu.make_async_copy(source, target, arrived.at[k])
        for k, (source, target) in enumerate(((rho_in, rho), (mom_in, mom), (ene_in, ene)))
    ]
    for copy in copies:
        copy.start()
    for copy in copies:
        copy.wait()

    def plane(x, carry):
        density = rho[x]
        inverse = 1.0 / density
        u = mom[0, x] * inverse
        v = mom[1, x] * inverse
        w = mom[2, x] * inverse
        kinetic = 0.5 * (mom[0, x] * u + mom[1, x] * v + mom[2, x] * w)
        temperature = (heat_ratio - 1.0) * (ene[x] - kinetic) * inverse
        own[U, x] = u
        own[W, x] = w
        own[V, x] = v
        own[T, x] = temperature
        first[0, x] = u
        first[1, x] = w
        second[0, x] = v
        second[1, x] = temperature
        return carry

    lax.fori_loop(0, CX, plane, 0)

    def sums(f, carry):
        for rows in row_chunks(rho.shape[1]):
            halo_sums(own, f, rows, up, down)
        return carry

    lax.fori_loop(0, 4, sums, 0)


def kernel_pitch_gradients(
    own, y_high, y_low, dy, mu, mate_a, mate_b
):
    for f in range(4):
        dy[f] = left_product(y_high[...], y_low[...], flat(own[f])).reshape(own.shape[1:])

    def plane(x, carry):
        mu[x] = shear_resistance_reference * jnp.exp(
            sutherland_power_law * jnp.log(own[T, x])
        )
        for f in range(2):
            mate_a[f, x] = own[f, x]
            mate_b[f, x] = own[V + f, x]
        return carry

    lax.fori_loop(0, CX, plane, 0)


def kernel_stream_gradients(own, conserved, before, after, mu, peer_second, dx, third):
    def field(f, carry):
        for rows in row_chunks(own.shape[2]):
            derived = compact_x(extended(before, own, after, f, rows))
            for x in range(CX):
                dx[f, x, rows, :] = derived[x]
        return carry

    lax.fori_loop(0, 4, field, 0)

    def plane(x, carry):
        third[0, x] = (2.0 / 3.0) * mu[x] * dx[U, x]
        third[1, x] = mu[x] * dx[W, x]
        third[2, x] = conserved[0, x]
        return carry

    lax.fori_loop(0, CX, plane, 0)


def kernel_flux_x(
    own, conserved, peer_first, first_mate, across_first, dx, dy, mu, z_high, z_low,
    dz, flux, up, down,
):
    width = own.shape[-1]
    odd = lax.rem(lax.axis_index("gy"), 2)
    for f in range(2):
        values = jnp.concatenate(
            [flat(own[f]), flat(peer_first[f]), flat(first_mate[f]), flat(across_first[f])], axis=1
        )
        dz[f] = right_product(values, z_high[odd], z_low[odd])

    rows = own.shape[2]

    def plane(x, carry):
        at = pl.ds(pl.multiple_of(x * rows, rows), rows)
        u, w, v, t = (own[f, x] for f in range(4))
        density = conserved[0, x]
        viscosity = mu[x]
        dil = dx[U, x] + dy[V, x] + dz[1, at, :width]
        s1 = viscosity * (2.0 * dx[U, x] - (2.0 / 3.0) * dil)
        s2 = viscosity * (dx[V, x] + dy[U, x])
        s3 = viscosity * (dx[W, x] + dz[0, at, :width])
        m = density * u
        total = m * (enthalpy * t + 0.5 * (u * u + v * v + w * w))
        flux[0, x] = m
        flux[1, x] = m * u + density * t - s1
        flux[2, x] = m * v - s2
        flux[3, x] = m * w - s3
        flux[4, x] = total - (s1 * u + s2 * v + s3 * w) - conduction * viscosity * dx[T, x]
        return carry

    lax.fori_loop(0, CX, plane, 0)

    def sums(f, carry):
        for chunk in row_chunks(rows):
            halo_sums(flux, f, chunk, up, down)
        return carry

    lax.fori_loop(0, 5, sums, 0)


def kernel_peer(peer_first, peer_second, flux, y_high, y_low, for_v, for_t, dy_peer):
    for_v[...] = peer_second[0]
    for_t[...] = peer_second[1]
    dy_peer[0] = left_product(y_high[...], y_low[...], flat(peer_second[0]))
    dy_peer[1] = left_product(y_high[...], y_low[...], flat(peer_first[1]))


def kernel_flux_yz(
    own, third, peer_first, peer_second, second_mate, across_v, across_t, dy_peer,
    dz, dx, dy, mu, y_high, y_low, z_high, z_low, f_high, f_low, part, part_mate,
    dz_more, flux, flux_y,
):
    rows, width = own.shape[2:]
    odd = lax.rem(lax.axis_index("gy"), 2)
    for f, across in enumerate((across_v, across_t)):
        values = jnp.concatenate(
            [flat(own[V + f]), flat(peer_second[f]), flat(second_mate[f]), flat(across[...])],
            axis=1,
        )
        dz_more[f] = right_product(values, z_high[odd], z_low[odd])

    def viscous(at, lanes, u, w, v, viscosity, yv, yw):
        s1 = viscosity * dz[0, at, lanes]
        s2 = viscosity * (dz_more[0, at, lanes] + yw)
        s3 = viscosity * ((4.0 / 3.0) * dz[1, at, lanes] - (2.0 / 3.0) * yv)
        heat = conduction * viscosity * dz_more[1, at, lanes]
        return s1, s2, s3, s1 * u + s2 * v + s3 * w + heat

    def plane(x, carry):
        at = pl.ds(pl.multiple_of(x * rows, rows), rows)
        here = slice(0, width)
        u, w, v, t = (own[f, x] for f in range(4))
        density = third[2, x]
        viscosity = mu[x]
        energy = enthalpy * t + 0.5 * (u * u + v * v + w * w)
        s1, s2, s3, power = viscous(at, here, u, w, v, viscosity, dy[V, x], dy[W, x])
        normal, shear = third[0, x], third[1, x]
        m = density * w
        flux[0, at, here] = m
        flux[1, at, here] = m * u - s1 - shear
        flux[2, at, here] = m * v - s2
        flux[3, at, here] = m * w + density * t - s3 + normal
        flux[4, at, here] = m * energy - power - shear * u + normal * w
        dil = dx[U, x] + dy[V, x] + dz[1, at, here]
        s1 = viscosity * (dy[U, x] + dx[V, x])
        s2 = viscosity * (2.0 * dy[V, x] - (2.0 / 3.0) * dil)
        s3 = viscosity * (dy[W, x] + dz_more[0, at, here])
        m = density * v
        total = m * energy
        flux_y[0, at, :] = m
        flux_y[1, at, :] = m * u - s1
        flux_y[2, at, :] = m * v + density * t - s2
        flux_y[3, at, :] = m * w - s3
        flux_y[4, at, :] = (
            total - (s1 * u + s2 * v + s3 * w) - conduction * viscosity * dy[T, x]
        )
        t = peer_second[1, x]
        viscosity = shear_resistance_reference * jnp.exp(sutherland_power_law * jnp.log(t))
        there = slice(width, 2 * width)
        s1, s2, s3, power = viscous(
            at, there, peer_first[0, x], peer_first[1, x], peer_second[0, x], viscosity,
            dy_peer[0, at, :], dy_peer[1, at, :],
        )
        flux[0, at, there] = jnp.zeros_like(s1)
        flux[1, at, there] = -s1
        flux[2, at, there] = -s2
        flux[3, at, there] = -s3
        flux[4, at, there] = -power
        return carry

    lax.fori_loop(0, CX, plane, 0)
    shape = own.shape[1:]
    for f in range(5):
        spread = right_product(flux[f], f_high[odd], f_low[odd])
        local = left_product(y_high[...], y_low[...], flux_y[f])
        part[f] = (spread[:, :width] + local).reshape(shape)
        part_mate[f] = spread[:, width:].reshape(shape)


def kernel_corrections(
    peer_first, peer_second, peer_third, part, part_mate, f_high, f_low, total, *for_mate
):
    shape = peer_first.shape[1:]
    width = shape[-1]
    odd = lax.rem(lax.axis_index("gy"), 2)
    u, w = flat(peer_first[0]), flat(peer_first[1])
    v, t = flat(peer_second[0]), flat(peer_second[1])
    normal, shear, density = (flat(peer_third[k]) for k in range(3))
    m = density * w
    energy = enthalpy * t + 0.5 * (u * u + v * v + w * w)
    values = (
        m,
        m * u - shear,
        m * v,
        m * w + density * t + normal,
        m * energy - shear * u + normal * w,
    )
    for f in range(5):
        spread = right_product(values[f], f_high[odd, width:, :], f_low[odd, width:, :])
        total[f] = part[f] + spread[:, :width].reshape(shape)
        for_mate[f][...] = part_mate[f] + spread[:, width:].reshape(shape)


def kernel_finish(
    conserved, total, mate_0, mate_1, mate_2, mate_3, mate_4, flux, before, after,
    tendency, advanced,
):
    for f, from_mate in enumerate((mate_0, mate_1, mate_2, mate_3, mate_4)):
        for rows in row_chunks(flux.shape[2]):
            derived = compact_x(extended(before, flux, after, f, rows))
            for x in range(CX):
                value = -(total[f, x, rows, :] + from_mate[x, rows, :] + derived[x])
                tendency[f, x, rows, :] = value
                advanced[f, x, rows, :] = conserved[f, x, rows, :] + section_step * value


def call(kernel, outputs, operands, scratch=(), outside=False):
    space = pltpu.HBM if outside else pltpu.VMEM
    in_specs = [pl.BlockSpec(memory_space=space) for _ in operands]
    if outside:
        operands = [pltpu.with_memory_space_constraint(value, pltpu.HBM) for value in operands]
    touched = sum(value.size * value.dtype.itemsize for value in operands)
    touched += 4 * sum(int(np.prod(shape)) for shape in outputs)
    return pl.pallas_call(
        kernel,
        out_shape=[jax.ShapeDtypeStruct(shape, F32) for shape in outputs],
        in_specs=in_specs,
        out_specs=[pl.BlockSpec(memory_space=pltpu.VMEM) for _ in outputs],
        scratch_shapes=list(scratch),
        cost_estimate=pl.CostEstimate(flops=0, bytes_accessed=touched, transcendentals=0),
        compiler_params=pltpu.CompilerParams(vmem_limit_bytes=24 * 1024 * 1024),
    )(*operands)


def fast_device(mass_per_volume, momentum, energy):
    rho = jnp.transpose(mass_per_volume, (0, 2, 1))
    mom = jnp.transpose(momentum, (0, 1, 3, 2))
    ene = jnp.transpose(energy, (0, 2, 1))
    _, rows, width = rho.shape
    length = 4 * width
    z_high, z_low = span_blocks(length, PLACES, PLACES[:2])
    f_high, f_low = span_blocks(length, PLACES[:2], (0, 1))
    y_high, y_low = halves(np.kron(np.eye(CX, dtype=np.float32), pitch_matrix(rows, CY)))
    block = (CX, rows, width)
    sums = (2, rows, width)
    points = CX * rows
    devices = lax.axis_size("gx")
    ring_up = [(i, (i + 1) % devices) for i in range(devices)]
    ring_down = [(j, i) for i, j in ring_up]
    to_mate = [(i, i ^ 1) for i in range(4)]
    to_peer = [(i, i ^ 2) for i in range(4)]

    conserved, own, first, second, up, down = call(
        kernel_primitives,
        [(5,) + block, (4,) + block, (2,) + block, (2,) + block, (4,) + sums, (4,) + sums],
        (rho, mom, ene),
        scratch=(pltpu.SemaphoreType.DMA((3,)),),
        outside=True,
    )
    peer_first = lax.ppermute(first, "gy", to_peer)
    before = lax.ppermute(up, "gx", ring_up)
    after = lax.ppermute(down, "gx", ring_down)
    dy, mu, mate_a, mate_b = call(
        kernel_pitch_gradients,
        [(4,) + block, block, (2,) + block, (2,) + block],
        (own, y_high, y_low),
    )
    first_mate = lax.ppermute(mate_a, "gy", to_mate)
    second_mate = lax.ppermute(mate_b, "gy", to_mate)
    peer_second = lax.ppermute(second, "gy", to_peer)
    peer_first, before, after = lax.optimization_barrier((peer_first, before, after))
    across_first = lax.ppermute(peer_first, "gy", to_mate)
    dx, third = call(
        kernel_stream_gradients,
        [(4,) + block, (3,) + block],
        (own, conserved, before, after, mu, peer_second),
    )
    peer_third = lax.ppermute(third, "gy", to_peer)
    dz, flux, flux_up, flux_down = call(
        kernel_flux_x,
        [(2, points, 2 * width), (5,) + block, (5,) + sums, (5,) + sums],
        (own, conserved, peer_first, first_mate, across_first, dx, dy, mu, z_high, z_low),
    )
    flux_before = lax.ppermute(flux_up, "gx", ring_up)
    flux_after = lax.ppermute(flux_down, "gx", ring_down)
    for_v, for_t, dy_peer = call(
        kernel_peer,
        [block, block, (2, points, width)],
        (peer_first, peer_second, flux, y_high, y_low),
    )
    across_v = lax.ppermute(for_v, "gy", to_mate)
    across_t = lax.ppermute(for_t, "gy", to_mate)
    part, part_mate = call(
        kernel_flux_yz,
        [(5,) + block, (5,) + block],
        (
            own, third, peer_first, peer_second, second_mate, across_v, across_t, dy_peer,
            dz, dx, dy, mu, y_high, y_low, z_high, z_low, f_high, f_low,
        ),
        scratch=(
            pltpu.VMEM((2, points, 2 * width), F32),
            pltpu.VMEM((5, points, 2 * width), F32),
            pltpu.VMEM((5, points, width), F32),
        ),
    )
    total, *for_mate = call(
        kernel_corrections,
        [(5,) + block] + 5 * [block],
        (peer_first, peer_second, peer_third, part, part_mate, f_high, f_low),
    )
    from_mate = [lax.ppermute(value, "gy", to_mate) for value in for_mate]
    tendency, advanced = call(
        kernel_finish,
        [(5,) + block, (5,) + block],
        (conserved, total, *from_mate, flux, flux_before, flux_after),
    )
    return (
        jnp.transpose(tendency, (0, 1, 3, 2)),
        jnp.transpose(advanced, (0, 1, 3, 2)),
    )


def padded(array, sides, width):
    for axis, dim in sides:
        devices, length = (lax.axis_size(axis), array.shape[dim])
        up = [(i, (i + 1) % devices) for i in range(devices)]
        down = [(j, i) for i, j in up]
        last = lax.slice_in_dim(array, length - width, length, axis=dim)
        initial = lax.slice_in_dim(array, 0, width, axis=dim)
        before = lax.ppermute(last, axis, up)
        after = lax.ppermute(initial, axis, down)
        array = jnp.concatenate([before, array, after], axis=dim)
    return array


def right_side(conserved, gradients_of, derive_x, derive_y, derive_z):
    mass_per_volume = conserved[0]
    momentum = conserved[1:4]
    energy = conserved[4]
    local_speed_vector = momentum / mass_per_volume
    kinetic = 0.5 * jnp.sum(momentum * local_speed_vector, axis=0)
    normal_force_per_area = (heat_ratio - 1.0) * (energy - kinetic)
    thermal_state = normal_force_per_area / mass_per_volume
    basic_quantities = jnp.concatenate([local_speed_vector, thermal_state[None]], 0)
    gradients = gradients_of(basic_quantities)
    shear_resistance = shear_resistance_reference * jnp.power(thermal_state, sutherland_power_law)
    conductivity = shear_resistance * heat_ratio / ((heat_ratio - 1.0) * prandtl)
    dilatation = gradients[0][0] + gradients[1][1] + gradients[2][2]
    derivers = (derive_x, derive_y, derive_z)
    accumulated = None
    for direction in range(3):
        stress_column = [
            shear_resistance * (gradients[direction][component] + gradients[component][direction])
            for component in range(3)
        ]
        stress_column[direction] = (
            stress_column[direction] - 2.0 / 3.0 * shear_resistance * dilatation
        )
        fluxes = [momentum[direction]]
        for component in range(3):
            moment_flux = (
                momentum[component] * local_speed_vector[direction] - stress_column[component]
            )
            if component == direction:
                moment_flux = moment_flux + normal_force_per_area
            fluxes.append(moment_flux)
        work_term = (
            stress_column[0] * local_speed_vector[0]
            + stress_column[1] * local_speed_vector[1]
            + stress_column[2] * local_speed_vector[2]
        )
        fluxes.append(
            (energy + normal_force_per_area) * local_speed_vector[direction]
            - work_term
            - conductivity * gradients[direction][3]
        )
        divergence_part = derivers[direction](jnp.stack(fluxes))
        accumulated = divergence_part if accumulated is None else accumulated + divergence_part
    return -accumulated


def plain_device(mass_per_volume, momentum, energy):
    conserved = jnp.concatenate([mass_per_volume[None], momentum, energy[None]], 0)
    highest = lax.Precision.HIGHEST
    x_matrix = jnp.asarray(compact_matrix(CX, HALO))
    z_matrix = jnp.asarray(span_matrix(NZ))

    def apply_x(extended):
        return jnp.einsum("il,flab->fiab", x_matrix, extended, precision=highest)

    def flux_x(values):
        return apply_x(padded(values, (("gx", 1),), HALO))

    y_matrix = jnp.asarray(pitch_matrix(conserved.shape[3], CY))

    def apply_y(values):
        return jnp.einsum("fabk,jk->fabj", values, y_matrix, precision=highest)

    def derive_span(values):
        lines = jnp.transpose(
            lax.all_to_all(values, "gy", split_axis=3, concat_axis=2, tiled=True), (0, 1, 3, 2)
        )
        derived = jnp.einsum("fack,jk->facj", lines, z_matrix, precision=highest)
        returned = lax.all_to_all(derived, "gy", split_axis=3, concat_axis=2, tiled=True)
        return jnp.transpose(returned, (0, 1, 3, 2))

    def gradients_of(basic_quantities):
        extended = padded(basic_quantities, (("gx", 1),), HALO)
        return (apply_x(extended), apply_y(basic_quantities), derive_span(basic_quantities))

    tendency = right_side(conserved, gradients_of, flux_x, apply_y, derive_span)
    advanced = conserved + section_step * tendency
    return (tendency, advanced)


def per_device(mass_per_volume, momentum, energy):
    planes, width, rows = mass_per_volume.shape
    fits = planes == CX and width % 128 == 0 and rows <= 32 and rows % CY == 0
    if fits and lax.axis_size("gy") == 4:
        return fast_device(mass_per_volume, momentum, energy)
    return plain_device(mass_per_volume, momentum, energy)


def solution(mesh):
    in_specs = (P("gx", "gy", None), P(None, "gx", "gy", None), P("gx", "gy", None))
    out_specs = (P(None, "gx", "gy", None), P(None, "gx", "gy", None))
    return jax.shard_map(
        per_device, mesh=mesh, in_specs=in_specs, out_specs=out_specs, check_vma=False
    )
```

```python
import functools

import jax
import jax.numpy as jnp
import numpy as np
from jax import lax
from jax.experimental import pallas as pl
from jax.experimental.pallas import tpu as pltpu
from jax.sharding import PartitionSpec as P

CX = 8
CY = 8
NZ = 512
HALO = 4


heat_ratio = 1.4
shear_resistance_reference = 0.08
sutherland_power_law = 0.7
prandtl = 0.72
section_step = 0.05
compact_alpha = 1.0 / 3.0
compact_near = 14.0 / 9.0
compact_far = 1.0 / 9.0

conduction = heat_ratio / ((heat_ratio - 1.0) * prandtl)
enthalpy = heat_ratio / (heat_ratio - 1.0)


def tridiagonal_inverse_product(length, stencil):
    solved = np.array(stencil)
    upper_ratio = np.zeros(length)
    for row_index in range(length):
        if row_index == 0:
            pivot_value = 1.0
            solved[row_index] = solved[row_index] / pivot_value
        else:
            pivot_value = 1.0 - compact_alpha * upper_ratio[row_index - 1]
            solved[row_index] = (
                solved[row_index] - compact_alpha * solved[row_index - 1]
            ) / pivot_value
        upper_ratio[row_index] = compact_alpha / pivot_value
    for row_index in range(length - 2, -1, -1):
        solved[row_index] = solved[row_index] - upper_ratio[row_index] * solved[row_index + 1]
    return solved


def exact_compact_matrix(block_size, margin):
    length = block_size + 2 * margin
    stencil = compact_near / 2.0 * (np.eye(length, k=1) - np.eye(length, k=-1))
    stencil = stencil + compact_far / 4.0 * (np.eye(length, k=2) - np.eye(length, k=-2))
    inverse_product = tridiagonal_inverse_product(length, stencil)
    return inverse_product[margin : margin + block_size]


def compact_matrix(block_size, margin):
    return exact_compact_matrix(block_size, margin).astype(np.float32)


def pitch_matrix(total, block_size):
    matrix = compact_matrix(block_size, HALO)
    result = np.zeros((total, total), np.float32)
    rows_all = np.arange(total)
    block_start = rows_all // block_size * block_size
    for offset in range(block_size + 2 * HALO):
        columns = (block_start - HALO + offset) % total
        result[rows_all, columns] += matrix[rows_all % block_size, offset]
    return result


def span_matrix(total):
    offsets = np.arange(total)[:, None] - np.arange(total)[None, :]
    angles = np.pi * offsets / total
    signs = np.where(offsets % 2 == 0, 1.0, -1.0)
    sines = np.where(offsets == 0, 1.0, np.sin(angles))
    result = np.where(offsets == 0, 0.0, np.pi / total * signs * np.cos(angles) / sines)
    return result.astype(np.float32)


F32 = jnp.float32
BF16 = jnp.bfloat16
U, W, V, T, R = range(5)
PLACES = (0, 2, 1, 3)
HALF = CX // 2


def halves(matrix):
    high = np.asarray(matrix, np.float32).astype(BF16)
    low = (matrix - high.astype(np.float32)).astype(BF16)
    return jnp.asarray(high), jnp.asarray(low)


def span_blocks(length, sources, targets):
    width = length // 4
    matrix = span_matrix(length).T
    both = []
    for core in range(2):
        columns = []
        for target in targets:
            to = core ^ target
            columns.append(
                np.concatenate(
                    [
                        matrix[
                            (core ^ source) * width : (core ^ source) * width + width,
                            to * width : to * width + width,
                        ]
                        for source in sources
                    ],
                    axis=0,
                )
            )
        both.append(np.concatenate(columns, axis=1))
    return halves(np.stack(both))


def halo_basis():
    matrix = exact_compact_matrix(CX, HALO)
    left = matrix[:, :HALO]
    basis = np.linalg.svd(left)[2][:2]
    inner = left @ basis.T
    outer = -inner[::-1]
    return basis, np.concatenate(
        [inner, matrix[:, HALO : HALO + CX], outer[:, ::-1]], axis=1
    )


def split(values):
    high = values.astype(BF16)
    low = (values - high.astype(F32)).astype(BF16)
    return high, low


def dot(a, b):
    return jnp.dot(a, b, preferred_element_type=F32)


def right_product(values, matrix_high, matrix_low):
    high, low = split(values)
    return dot(high, matrix_high) + dot(low, matrix_high) + dot(high, matrix_low)


def left_product(matrix_high, matrix_low, values):
    high, low = split(values)
    return dot(matrix_high, high) + dot(matrix_high, low) + dot(matrix_low, high)


def compact_x(planes):
    matrix = halo_basis()[1]
    length = CX + 4
    half = length // 2
    odd = [planes[l] - planes[length - 1 - l] for l in range(half)]
    even = [planes[l] + planes[length - 1 - l] for l in range(half)]
    result = [None] * CX
    for i in range(HALF):
        first = None
        second = None
        for l in range(half):
            a = float(0.5 * (matrix[i, l] - matrix[i, length - 1 - l]))
            b = float(0.5 * (matrix[i, l] + matrix[i, length - 1 - l]))
            first = a * odd[l] if first is None else first + a * odd[l]
            second = b * even[l] if second is None else second + b * even[l]
        result[i] = first + second
        result[CX - 1 - i] = first - second
    return result


def extended(before, own, after, f, rows):
    return (
        [before[f, 0, rows, :], before[f, 1, rows, :]]
        + [own[f, l, rows, :] for l in range(CX)]
        + [after[f, 1, rows, :], after[f, 0, rows, :]]
    )


def halo_sums(values, f, rows, up, down):
    basis = halo_basis()[0]
    for k in range(2):
        top = None
        bottom = None
        for l in range(HALO):
            a = float(basis[k, l]) * values[f, CX - HALO + l, rows, :]
            b = float(basis[k, l]) * values[f, HALO - 1 - l, rows, :]
            top = a if top is None else top + a
            bottom = b if bottom is None else bottom + b
        up[f, k, rows, :] = top
        down[f, k, rows, :] = bottom


def row_chunks(rows):
    return [slice(start, start + 8) for start in range(0, rows, 8)]


def flat(values):
    return values.reshape(-1, values.shape[-1])


def kernel_primitives(
    rho_in, mom_in, ene_in, conserved, own, first, second, up, down, arrived
):
    rho = conserved.at[0]
    mom = conserved.at[1:4]
    ene = conserved.at[4]
    copies = [
        pltpu.make_async_copy(source, target, arrived.at[k])
        for k, (source, target) in enumerate(((rho_in, rho), (mom_in, mom), (ene_in, ene)))
    ]
    for copy in copies:
        copy.start()
    for copy in copies:
        copy.wait()

    def plane(x, carry):
        density = rho[x]
        inverse = 1.0 / density
        u = mom[0, x] * inverse
        v = mom[1, x] * inverse
        w = mom[2, x] * inverse
        kinetic = 0.5 * (mom[0, x] * u + mom[1, x] * v + mom[2, x] * w)
        temperature = (heat_ratio - 1.0) * (ene[x] - kinetic) * inverse
        own[U, x] = u
        own[W, x] = w
        own[V, x] = v
        own[T, x] = temperature
        first[0, x] = u
        first[1, x] = w
        second[0, x] = v
        second[1, x] = temperature
        second[2, x] = density
        return carry

    lax.fori_loop(0, CX, plane, 0)

    def sums(f, carry):
        for rows in row_chunks(rho.shape[1]):
            halo_sums(own, f, rows, up, down)
        return carry

    lax.fori_loop(0, 4, sums, 0)


def kernel_pitch_gradients(
    own, y_high, y_low, dy, mu, mate_u, mate_w, mate_b
):
    for f in range(4):
        dy[f] = left_product(y_high[...], y_low[...], flat(own[f])).reshape(own.shape[1:])

    def plane(x, carry):
        mu[x] = shear_resistance_reference * jnp.exp(
            sutherland_power_law * jnp.log(own[T, x])
        )
        mate_u[x] = own[U, x]
        mate_w[x] = own[W, x]
        for f in range(2):
            mate_b[f, x] = own[V + f, x]
        return carry

    lax.fori_loop(0, CX, plane, 0)


def kernel_stream_gradients(own, before, after, mu, peer_first, dx, third, for_u, for_w):
    for_u[...] = peer_first[0]
    for_w[...] = peer_first[1]

    def field(f, carry):
        for rows in row_chunks(own.shape[2]):
            derived = compact_x(extended(before, own, after, f, rows))
            for x in range(CX):
                dx[f, x, rows, :] = derived[x]
        return carry

    lax.fori_loop(0, 4, field, 0)

    def plane(x, carry):
        third[0, x] = (2.0 / 3.0) * mu[x] * dx[U, x]
        third[1, x] = mu[x] * dx[W, x]
        return carry

    lax.fori_loop(0, CX, plane, 0)


def kernel_flux_x(
    own, second, peer_first, mate_u, mate_w, across_u, across_w, dx, dy, mu,
    z_high, z_low, dz, flux, up, down,
):
    width = own.shape[-1]
    odd = lax.rem(lax.axis_index("gy"), 2)
    for f, (mate, across) in enumerate(((mate_u, across_u), (mate_w, across_w))):
        values = jnp.concatenate(
            [flat(own[f]), flat(peer_first[f]), flat(mate[...]), flat(across[...])], axis=1
        )
        dz[f] = right_product(values, z_high[odd], z_low[odd])

    rows = own.shape[2]

    def plane(x, carry):
        at = pl.ds(pl.multiple_of(x * rows, rows), rows)
        u, w, v, t = (own[f, x] for f in range(4))
        density = second[2, x]
        viscosity = mu[x]
        dil = dx[U, x] + dy[V, x] + dz[1, at, :width]
        s1 = viscosity * (2.0 * dx[U, x] - (2.0 / 3.0) * dil)
        s2 = viscosity * (dx[V, x] + dy[U, x])
        s3 = viscosity * (dx[W, x] + dz[0, at, :width])
        m = density * u
        total = m * (enthalpy * t + 0.5 * (u * u + v * v + w * w))
        flux[0, x] = m
        flux[1, x] = m * u + density * t - s1
        flux[2, x] = m * v - s2
        flux[3, x] = m * w - s3
        flux[4, x] = total - (s1 * u + s2 * v + s3 * w) - conduction * viscosity * dx[T, x]
        return carry

    lax.fori_loop(0, CX, plane, 0)

    def sums(f, carry):
        for chunk in row_chunks(rows):
            halo_sums(flux, f, chunk, up, down)
        return carry

    lax.fori_loop(0, 5, sums, 0)


def kernel_peer(peer_first, peer_second, flux, y_high, y_low, for_v, for_t, dy_peer):
    for_v[...] = peer_second[0]
    for_t[...] = peer_second[1]
    dy_peer[0] = left_product(y_high[...], y_low[...], flat(peer_second[0]))
    dy_peer[1] = left_product(y_high[...], y_low[...], flat(peer_first[1]))


def kernel_flux_yz(
    own, second, peer_first, peer_second, second_mate, across_v, across_t, dy_peer,
    dz, dx, dy, mu, y_high, y_low, z_high, z_low, f_high, f_low, part, part_mate,
    dz_more, flux, flux_y,
):
    rows, width = own.shape[2:]
    odd = lax.rem(lax.axis_index("gy"), 2)
    for f, across in enumerate((across_v, across_t)):
        values = jnp.concatenate(
            [flat(own[V + f]), flat(peer_second[f]), flat(second_mate[f]), flat(across[...])],
            axis=1,
        )
        dz_more[f] = right_product(values, z_high[odd], z_low[odd])

    def span_flux(at, lanes, u, w, v, t, density, viscosity, yv, yw):
        s1 = viscosity * dz[0, at, lanes]
        s2 = viscosity * (dz_more[0, at, lanes] + yw)
        s3 = viscosity * ((4.0 / 3.0) * dz[1, at, lanes] - (2.0 / 3.0) * yv)
        m = density * w
        total = m * (enthalpy * t + 0.5 * (u * u + v * v + w * w))
        flux[0, at, lanes] = m
        flux[1, at, lanes] = m * u - s1
        flux[2, at, lanes] = m * v - s2
        flux[3, at, lanes] = m * w + density * t - s3
        flux[4, at, lanes] = (
            total
            - (s1 * u + s2 * v + s3 * w)
            - conduction * viscosity * dz_more[1, at, lanes]
        )

    def plane(x, carry):
        at = pl.ds(pl.multiple_of(x * rows, rows), rows)
        here = slice(0, width)
        u, w, v, t = (own[f, x] for f in range(4))
        density = second[2, x]
        viscosity = mu[x]
        span_flux(at, here, u, w, v, t, density, viscosity, dy[V, x], dy[W, x])
        dil = dx[U, x] + dy[V, x] + dz[1, at, here]
        s1 = viscosity * (dy[U, x] + dx[V, x])
        s2 = viscosity * (2.0 * dy[V, x] - (2.0 / 3.0) * dil)
        s3 = viscosity * (dy[W, x] + dz_more[0, at, here])
        m = density * v
        total = m * (enthalpy * t + 0.5 * (u * u + v * v + w * w))
        flux_y[0, at, :] = m
        flux_y[1, at, :] = m * u - s1
        flux_y[2, at, :] = m * v + density * t - s2
        flux_y[3, at, :] = m * w - s3
        flux_y[4, at, :] = (
            total - (s1 * u + s2 * v + s3 * w) - conduction * viscosity * dy[T, x]
        )
        t = peer_second[1, x]
        viscosity = shear_resistance_reference * jnp.exp(sutherland_power_law * jnp.log(t))
        span_flux(
            at, slice(width, 2 * width), peer_first[0, x], peer_first[1, x],
            peer_second[0, x], t, peer_second[2, x], viscosity,
            dy_peer[0, at, :], dy_peer[1, at, :],
        )
        return carry

    lax.fori_loop(0, CX, plane, 0)
    shape = own.shape[1:]
    for f in range(5):
        spread = right_product(flux[f], f_high[odd], f_low[odd])
        local = left_product(y_high[...], y_low[...], flux_y[f])
        part[f] = (spread[:, :width] + local).reshape(shape)
        part_mate[f] = spread[:, width:].reshape(shape)


def kernel_corrections(
    own, peer_first, third, peer_third, part, part_mate, f_high, f_low, total, *for_mate
):
    width = own.shape[-1]
    odd = lax.rem(lax.axis_index("gy"), 2)
    shape = own.shape[1:]
    for f in (0, 2):
        total[f] = part[f]
        for_mate[f][...] = part_mate[f]
    pairs = ((own, third), (peer_first, peer_third))
    for f in (1, 3, 4):
        sides = []
        for speeds, shared in pairs:
            if f == 1:
                value = -shared[1]
            elif f == 3:
                value = shared[0]
            else:
                value = shared[0] * speeds[W] - shared[1] * speeds[U]
            sides.append(flat(value))
        spread = right_product(jnp.concatenate(sides, axis=1), f_high[odd], f_low[odd])
        total[f] = part[f] + spread[:, :width].reshape(shape)
        for_mate[f][...] = part_mate[f] + spread[:, width:].reshape(shape)


def kernel_add_stream(total, flux, before, after, result):
    def field(f, carry):
        for rows in row_chunks(flux.shape[2]):
            derived = compact_x(extended(before, flux, after, f, rows))
            for x in range(CX):
                result[f, x, rows, :] = total[f, x, rows, :] + derived[x]
        return carry

    lax.fori_loop(0, 5, field, 0)


def kernel_finish(
    conserved, total, mate_0, mate_1, mate_2, mate_3, mate_4, tendency, advanced
):
    for f, from_mate in enumerate((mate_0, mate_1, mate_2, mate_3, mate_4)):

        def plane(x, carry):
            value = -(total[f, x] + from_mate[x])
            tendency[f, x] = value
            advanced[f, x] = conserved[f, x] + section_step * value
            return carry

        lax.fori_loop(0, CX, plane, 0, unroll=2)


def call(kernel, outputs, operands, scratch=(), outside=False):
    space = pltpu.HBM if outside else pltpu.VMEM
    in_specs = [pl.BlockSpec(memory_space=space) for _ in operands]
    if outside:
        operands = [pltpu.with_memory_space_constraint(value, pltpu.HBM) for value in operands]
    touched = sum(value.size * value.dtype.itemsize for value in operands)
    touched += 4 * sum(int(np.prod(shape)) for shape in outputs)
    return pl.pallas_call(
        kernel,
        out_shape=[jax.ShapeDtypeStruct(shape, F32) for shape in outputs],
        in_specs=in_specs,
        out_specs=[pl.BlockSpec(memory_space=pltpu.VMEM) for _ in outputs],
        scratch_shapes=list(scratch),
        cost_estimate=pl.CostEstimate(flops=0, bytes_accessed=touched, transcendentals=0),
        compiler_params=pltpu.CompilerParams(vmem_limit_bytes=24 * 1024 * 1024),
    )(*operands)


def fast_device(mass_per_volume, momentum, energy):
    rho = jnp.transpose(mass_per_volume, (0, 2, 1))
    mom = jnp.transpose(momentum, (0, 1, 3, 2))
    ene = jnp.transpose(energy, (0, 2, 1))
    _, rows, width = rho.shape
    length = 4 * width
    z_high, z_low = span_blocks(length, PLACES, PLACES[:2])
    f_high, f_low = span_blocks(length, PLACES[:2], (0, 1))
    y_high, y_low = halves(np.kron(np.eye(CX, dtype=np.float32), pitch_matrix(rows, CY)))
    block = (CX, rows, width)
    sums = (2, rows, width)
    points = CX * rows
    devices = lax.axis_size("gx")
    ring_up = [(i, (i + 1) % devices) for i in range(devices)]
    ring_down = [(j, i) for i, j in ring_up]
    to_mate = [(i, i ^ 1) for i in range(4)]
    to_peer = [(i, i ^ 2) for i in range(4)]

    conserved, own, first, second, up, down = call(
        kernel_primitives,
        [(5,) + block, (4,) + block, (2,) + block, (3,) + block, (4,) + sums, (4,) + sums],
        (rho, mom, ene),
        scratch=(pltpu.SemaphoreType.DMA((3,)),),
        outside=True,
    )
    peer_first = lax.ppermute(first, "gy", to_peer)
    before = lax.ppermute(up, "gx", ring_up)
    after = lax.ppermute(down, "gx", ring_down)
    dy, mu, for_u, for_w, mate_b = call(
        kernel_pitch_gradients,
        [(4,) + block, block, block, block, (2,) + block],
        (own, y_high, y_low),
    )
    mate_u, mate_w = (lax.ppermute(value, "gy", to_mate) for value in (for_u, for_w))
    second_mate = lax.ppermute(mate_b, "gy", to_mate)
    peer_second = lax.ppermute(second, "gy", to_peer)
    dx, third, for_u, for_w = call(
        kernel_stream_gradients,
        [(4,) + block, (2,) + block, block, block],
        (own, before, after, mu, peer_first),
    )
    across_u, across_w = (lax.ppermute(value, "gy", to_mate) for value in (for_u, for_w))
    peer_third = lax.ppermute(third, "gy", to_peer)
    dz, flux, flux_up, flux_down = call(
        kernel_flux_x,
        [(2, points, 2 * width), (5,) + block, (5,) + sums, (5,) + sums],
        (
            own, second, peer_first, mate_u, mate_w, across_u, across_w, dx, dy, mu,
            z_high, z_low,
        ),
    )
    flux_before = lax.ppermute(flux_up, "gx", ring_up)
    flux_after = lax.ppermute(flux_down, "gx", ring_down)
    for_v, for_t, dy_peer = call(
        kernel_peer,
        [block, block, (2, points, width)],
        (peer_first, peer_second, flux, y_high, y_low),
    )
    across_v = lax.ppermute(for_v, "gy", to_mate)
    across_t = lax.ppermute(for_t, "gy", to_mate)
    part, part_mate = call(
        kernel_flux_yz,
        [(5,) + block, (5,) + block],
        (
            own, second, peer_first, peer_second, second_mate, across_v, across_t, dy_peer,
            dz, dx, dy, mu, y_high, y_low, z_high, z_low, f_high, f_low,
        ),
        scratch=(
            pltpu.VMEM((2, points, 2 * width), F32),
            pltpu.VMEM((5, points, 2 * width), F32),
            pltpu.VMEM((5, points, width), F32),
        ),
    )
    total, *for_mate = call(
        kernel_corrections,
        [(5,) + block] + 5 * [block],
        (own, peer_first, third, peer_third, part, part_mate, f_high, f_low),
    )
    from_mate = [lax.ppermute(value, "gy", to_mate) for value in for_mate]
    (total,) = call(
        kernel_add_stream, [(5,) + block], (total, flux, flux_before, flux_after)
    )
    tendency, advanced = call(
        kernel_finish, [(5,) + block, (5,) + block], (conserved, total, *from_mate)
    )
    return (
        jnp.transpose(tendency, (0, 1, 3, 2)),
        jnp.transpose(advanced, (0, 1, 3, 2)),
    )


def padded(array, sides, width):
    for axis, dim in sides:
        devices, length = (lax.axis_size(axis), array.shape[dim])
        up = [(i, (i + 1) % devices) for i in range(devices)]
        down = [(j, i) for i, j in up]
        last = lax.slice_in_dim(array, length - width, length, axis=dim)
        initial = lax.slice_in_dim(array, 0, width, axis=dim)
        before = lax.ppermute(last, axis, up)
        after = lax.ppermute(initial, axis, down)
        array = jnp.concatenate([before, array, after], axis=dim)
    return array


def right_side(conserved, gradients_of, derive_x, derive_y, derive_z):
    mass_per_volume = conserved[0]
    momentum = conserved[1:4]
    energy = conserved[4]
    local_speed_vector = momentum / mass_per_volume
    kinetic = 0.5 * jnp.sum(momentum * local_speed_vector, axis=0)
    normal_force_per_area = (heat_ratio - 1.0) * (energy - kinetic)
    thermal_state = normal_force_per_area / mass_per_volume
    basic_quantities = jnp.concatenate([local_speed_vector, thermal_state[None]], 0)
    gradients = gradients_of(basic_quantities)
    shear_resistance = shear_resistance_reference * jnp.power(thermal_state, sutherland_power_law)
    conductivity = shear_resistance * heat_ratio / ((heat_ratio - 1.0) * prandtl)
    dilatation = gradients[0][0] + gradients[1][1] + gradients[2][2]
    derivers = (derive_x, derive_y, derive_z)
    accumulated = None
    for direction in range(3):
        stress_column = [
            shear_resistance * (gradients[direction][component] + gradients[component][direction])
            for component in range(3)
        ]
        stress_column[direction] = (
            stress_column[direction] - 2.0 / 3.0 * shear_resistance * dilatation
        )
        fluxes = [momentum[direction]]
        for component in range(3):
            moment_flux = (
                momentum[component] * local_speed_vector[direction] - stress_column[component]
            )
            if component == direction:
                moment_flux = moment_flux + normal_force_per_area
            fluxes.append(moment_flux)
        work_term = (
            stress_column[0] * local_speed_vector[0]
            + stress_column[1] * local_speed_vector[1]
            + stress_column[2] * local_speed_vector[2]
        )
        fluxes.append(
            (energy + normal_force_per_area) * local_speed_vector[direction]
            - work_term
            - conductivity * gradients[direction][3]
        )
        divergence_part = derivers[direction](jnp.stack(fluxes))
        accumulated = divergence_part if accumulated is None else accumulated + divergence_part
    return -accumulated


def plain_device(mass_per_volume, momentum, energy):
    conserved = jnp.concatenate([mass_per_volume[None], momentum, energy[None]], 0)
    highest = lax.Precision.HIGHEST
    x_matrix = jnp.asarray(compact_matrix(CX, HALO))
    z_matrix = jnp.asarray(span_matrix(NZ))

    def apply_x(extended):
        return jnp.einsum("il,flab->fiab", x_matrix, extended, precision=highest)

    def flux_x(values):
        return apply_x(padded(values, (("gx", 1),), HALO))

    y_matrix = jnp.asarray(pitch_matrix(conserved.shape[3], CY))

    def apply_y(values):
        return jnp.einsum("fabk,jk->fabj", values, y_matrix, precision=highest)

    def derive_span(values):
        lines = jnp.transpose(
            lax.all_to_all(values, "gy", split_axis=3, concat_axis=2, tiled=True), (0, 1, 3, 2)
        )
        derived = jnp.einsum("fack,jk->facj", lines, z_matrix, precision=highest)
        returned = lax.all_to_all(derived, "gy", split_axis=3, concat_axis=2, tiled=True)
        return jnp.transpose(returned, (0, 1, 3, 2))

    def gradients_of(basic_quantities):
        extended = padded(basic_quantities, (("gx", 1),), HALO)
        return (apply_x(extended), apply_y(basic_quantities), derive_span(basic_quantities))

    tendency = right_side(conserved, gradients_of, flux_x, apply_y, derive_span)
    advanced = conserved + section_step * tendency
    return (tendency, advanced)


def per_device(mass_per_volume, momentum, energy):
    planes, width, rows = mass_per_volume.shape
    fits = planes == CX and width % 128 == 0 and rows <= 32 and rows % CY == 0
    if fits and lax.axis_size("gy") == 4:
        return fast_device(mass_per_volume, momentum, energy)
    return plain_device(mass_per_volume, momentum, energy)


def solution(mesh):
    in_specs = (P("gx", "gy", None), P(None, "gx", "gy", None), P("gx", "gy", None))
    out_specs = (P(None, "gx", "gy", None), P(None, "gx", "gy", None))
    return jax.shard_map(
        per_device, mesh=mesh, in_specs=in_specs, out_specs=out_specs, check_vma=False
    )
```

```python
import functools

import jax
import jax.numpy as jnp
import numpy as np
from jax import lax
from jax.experimental import pallas as pl
from jax.experimental.pallas import tpu as pltpu
from jax.sharding import PartitionSpec as P

CX = 8
CY = 8
NZ = 512
HALO = 4


heat_ratio = 1.4
shear_resistance_reference = 0.08
sutherland_power_law = 0.7
prandtl = 0.72
section_step = 0.05
compact_alpha = 1.0 / 3.0
compact_near = 14.0 / 9.0
compact_far = 1.0 / 9.0

conduction = heat_ratio / ((heat_ratio - 1.0) * prandtl)
enthalpy = heat_ratio / (heat_ratio - 1.0)


def tridiagonal_inverse_product(length, stencil):
    solved = np.array(stencil)
    upper_ratio = np.zeros(length)
    for row_index in range(length):
        if row_index == 0:
            pivot_value = 1.0
            solved[row_index] = solved[row_index] / pivot_value
        else:
            pivot_value = 1.0 - compact_alpha * upper_ratio[row_index - 1]
            solved[row_index] = (
                solved[row_index] - compact_alpha * solved[row_index - 1]
            ) / pivot_value
        upper_ratio[row_index] = compact_alpha / pivot_value
    for row_index in range(length - 2, -1, -1):
        solved[row_index] = solved[row_index] - upper_ratio[row_index] * solved[row_index + 1]
    return solved


def exact_compact_matrix(block_size, margin):
    length = block_size + 2 * margin
    stencil = compact_near / 2.0 * (np.eye(length, k=1) - np.eye(length, k=-1))
    stencil = stencil + compact_far / 4.0 * (np.eye(length, k=2) - np.eye(length, k=-2))
    inverse_product = tridiagonal_inverse_product(length, stencil)
    return inverse_product[margin : margin + block_size]


def compact_matrix(block_size, margin):
    return exact_compact_matrix(block_size, margin).astype(np.float32)


def pitch_matrix(total, block_size):
    matrix = compact_matrix(block_size, HALO)
    result = np.zeros((total, total), np.float32)
    rows_all = np.arange(total)
    block_start = rows_all // block_size * block_size
    for offset in range(block_size + 2 * HALO):
        columns = (block_start - HALO + offset) % total
        result[rows_all, columns] += matrix[rows_all % block_size, offset]
    return result


def span_matrix(total):
    offsets = np.arange(total)[:, None] - np.arange(total)[None, :]
    angles = np.pi * offsets / total
    signs = np.where(offsets % 2 == 0, 1.0, -1.0)
    sines = np.where(offsets == 0, 1.0, np.sin(angles))
    result = np.where(offsets == 0, 0.0, np.pi / total * signs * np.cos(angles) / sines)
    return result.astype(np.float32)


F32 = jnp.float32
BF16 = jnp.bfloat16
U, W, V, T, R = range(5)
PLACES = (0, 2, 1, 3)
HALF = CX // 2


def halves(matrix):
    high = np.asarray(matrix, np.float32).astype(BF16)
    low = (matrix - high.astype(np.float32)).astype(BF16)
    return jnp.asarray(high), jnp.asarray(low)


def span_blocks(length, sources, targets):
    width = length // 4
    matrix = span_matrix(length).T
    both = []
    for core in range(2):
        columns = []
        for target in targets:
            to = core ^ target
            columns.append(
                np.concatenate(
                    [
                        matrix[
                            (core ^ source) * width : (core ^ source) * width + width,
                            to * width : to * width + width,
                        ]
                        for source in sources
                    ],
                    axis=0,
                )
            )
        both.append(np.concatenate(columns, axis=1))
    return halves(np.stack(both))


def halo_basis():
    matrix = exact_compact_matrix(CX, HALO)
    left = matrix[:, :HALO]
    basis = np.linalg.svd(left)[2][:2]
    inner = left @ basis.T
    outer = -inner[::-1]
    return basis, np.concatenate(
        [inner, matrix[:, HALO : HALO + CX], outer[:, ::-1]], axis=1
    )


def split(values):
    high = values.astype(BF16)
    low = (values - high.astype(F32)).astype(BF16)
    return high, low


def dot(a, b):
    return jnp.dot(a, b, preferred_element_type=F32)


def right_product(values, matrix_high, matrix_low):
    high, low = split(values)
    return dot(high, matrix_high) + dot(low, matrix_high) + dot(high, matrix_low)


def left_product(matrix_high, matrix_low, values):
    high, low = split(values)
    return dot(matrix_high, high) + dot(matrix_high, low) + dot(matrix_low, high)


def compact_x(planes):
    matrix = halo_basis()[1]
    length = CX + 4
    half = length // 2
    odd = [planes[l] - planes[length - 1 - l] for l in range(half)]
    even = [planes[l] + planes[length - 1 - l] for l in range(half)]
    result = [None] * CX
    for i in range(HALF):
        first = None
        second = None
        for l in range(half):
            a = float(0.5 * (matrix[i, l] - matrix[i, length - 1 - l]))
            b = float(0.5 * (matrix[i, l] + matrix[i, length - 1 - l]))
            first = a * odd[l] if first is None else first + a * odd[l]
            second = b * even[l] if second is None else second + b * even[l]
        result[i] = first + second
        result[CX - 1 - i] = first - second
    return result


def extended(before, own, after, f, rows):
    return (
        [before[f, 0, rows, :], before[f, 1, rows, :]]
        + [own[f, l, rows, :] for l in range(CX)]
        + [after[f, 1, rows, :], after[f, 0, rows, :]]
    )


def halo_sums(values, f, rows, up, down):
    basis = halo_basis()[0]
    for k in range(2):
        top = None
        bottom = None
        for l in range(HALO):
            a = float(basis[k, l]) * values[f, CX - HALO + l, rows, :]
            b = float(basis[k, l]) * values[f, HALO - 1 - l, rows, :]
            top = a if top is None else top + a
            bottom = b if bottom is None else bottom + b
        up[f, k, rows, :] = top
        down[f, k, rows, :] = bottom


def row_chunks(rows):
    return [slice(start, start + 8) for start in range(0, rows, 8)]


def flat(values):
    return values.reshape(-1, values.shape[-1])


def kernel_inputs(rho_in, mom_in, ene_in, conserved, first, arrived):
    copies = [
        pltpu.make_async_copy(source, conserved.at[part], arrived.at[k])
        for k, (source, part) in enumerate(
            ((rho_in, 0), (mom_in, slice(1, 4)), (ene_in, 4))
        )
    ]
    for copy in copies:
        copy.start()
    for copy in copies:
        copy.wait()

    def plane(x, carry):
        inverse = 1.0 / conserved[0, x]
        first[0, x] = conserved[1, x] * inverse
        first[1, x] = conserved[3, x] * inverse
        return carry

    lax.fori_loop(0, CX, plane, 0, unroll=2)


def kernel_primitives(conserved, first, own, second, up, down):
    def plane(x, carry):
        density = conserved[0, x]
        inverse = 1.0 / density
        u = first[0, x]
        w = first[1, x]
        v = conserved[2, x] * inverse
        kinetic = 0.5 * (conserved[1, x] * u + conserved[2, x] * v + conserved[3, x] * w)
        temperature = (heat_ratio - 1.0) * (conserved[4, x] - kinetic) * inverse
        own[U, x] = u
        own[W, x] = w
        own[V, x] = v
        own[T, x] = temperature
        second[0, x] = v
        second[1, x] = temperature
        second[2, x] = density
        return carry

    lax.fori_loop(0, CX, plane, 0, unroll=2)

    def sums(f, carry):
        for rows in row_chunks(own.shape[2]):
            halo_sums(own, f, rows, up, down)
        return carry

    lax.fori_loop(0, 4, sums, 0)


def kernel_pitch_gradients(
    own, y_high, y_low, dy, mu, mate_u, mate_w, mate_b
):
    for f in range(4):
        dy[f] = left_product(y_high[...], y_low[...], flat(own[f])).reshape(own.shape[1:])

    def plane(x, carry):
        mu[x] = shear_resistance_reference * jnp.exp(
            sutherland_power_law * jnp.log(own[T, x])
        )
        mate_u[x] = own[U, x]
        mate_w[x] = own[W, x]
        for f in range(2):
            mate_b[f, x] = own[V + f, x]
        return carry

    lax.fori_loop(0, CX, plane, 0)


def kernel_stream_gradients(own, before, after, mu, peer_first, dx, third, for_u, for_w):
    for_u[...] = peer_first[0]
    for_w[...] = peer_first[1]

    def field(f, carry):
        for rows in row_chunks(own.shape[2]):
            derived = compact_x(extended(before, own, after, f, rows))
            for x in range(CX):
                dx[f, x, rows, :] = derived[x]
        return carry

    lax.fori_loop(0, 4, field, 0)

    def plane(x, carry):
        third[0, x] = (2.0 / 3.0) * mu[x] * dx[U, x]
        third[1, x] = mu[x] * dx[W, x]
        return carry

    lax.fori_loop(0, CX, plane, 0)


def kernel_flux_x(
    own, second, peer_first, mate_u, mate_w, across_u, across_w, dx, dy, mu,
    z_high, z_low, dz, flux, up, down,
):
    width = own.shape[-1]
    odd = lax.rem(lax.axis_index("gy"), 2)
    for f, (mate, across) in enumerate(((mate_u, across_u), (mate_w, across_w))):
        values = jnp.concatenate(
            [flat(own[f]), flat(peer_first[f]), flat(mate[...]), flat(across[...])], axis=1
        )
        dz[f] = right_product(values, z_high[odd], z_low[odd])

    rows = own.shape[2]

    def plane(x, carry):
        at = pl.ds(pl.multiple_of(x * rows, rows), rows)
        u, w, v, t = (own[f, x] for f in range(4))
        density = second[2, x]
        viscosity = mu[x]
        dil = dx[U, x] + dy[V, x] + dz[1, at, :width]
        s1 = viscosity * (2.0 * dx[U, x] - (2.0 / 3.0) * dil)
        s2 = viscosity * (dx[V, x] + dy[U, x])
        s3 = viscosity * (dx[W, x] + dz[0, at, :width])
        m = density * u
        total = m * (enthalpy * t + 0.5 * (u * u + v * v + w * w))
        flux[0, x] = m
        flux[1, x] = m * u + density * t - s1
        flux[2, x] = m * v - s2
        flux[3, x] = m * w - s3
        flux[4, x] = total - (s1 * u + s2 * v + s3 * w) - conduction * viscosity * dx[T, x]
        return carry

    lax.fori_loop(0, CX, plane, 0)

    def sums(f, carry):
        for chunk in row_chunks(rows):
            halo_sums(flux, f, chunk, up, down)
        return carry

    lax.fori_loop(0, 5, sums, 0)


def kernel_peer(peer_first, peer_second, flux, y_high, y_low, for_v, for_t, dy_peer):
    for_v[...] = peer_second[0]
    for_t[...] = peer_second[1]
    dy_peer[0] = left_product(y_high[...], y_low[...], flat(peer_second[0]))
    dy_peer[1] = left_product(y_high[...], y_low[...], flat(peer_first[1]))


def kernel_flux_yz(
    own, second, peer_first, peer_second, second_mate, across_v, across_t, dy_peer,
    dz, dx, dy, mu, y_high, y_low, z_high, z_low, f_high, f_low, part, part_mate,
    dz_more, flux, flux_y,
):
    rows, width = own.shape[2:]
    odd = lax.rem(lax.axis_index("gy"), 2)
    for f, across in enumerate((across_v, across_t)):
        values = jnp.concatenate(
            [flat(own[V + f]), flat(peer_second[f]), flat(second_mate[f]), flat(across[...])],
            axis=1,
        )
        dz_more[f] = right_product(values, z_high[odd], z_low[odd])

    def span_flux(at, lanes, u, w, v, t, density, viscosity, yv, yw):
        s1 = viscosity * dz[0, at, lanes]
        s2 = viscosity * (dz_more[0, at, lanes] + yw)
        s3 = viscosity * ((4.0 / 3.0) * dz[1, at, lanes] - (2.0 / 3.0) * yv)
        m = density * w
        total = m * (enthalpy * t + 0.5 * (u * u + v * v + w * w))
        flux[0, at, lanes] = m
        flux[1, at, lanes] = m * u - s1
        flux[2, at, lanes] = m * v - s2
        flux[3, at, lanes] = m * w + density * t - s3
        flux[4, at, lanes] = (
            total
            - (s1 * u + s2 * v + s3 * w)
            - conduction * viscosity * dz_more[1, at, lanes]
        )

    def plane(x, carry):
        at = pl.ds(pl.multiple_of(x * rows, rows), rows)
        here = slice(0, width)
        u, w, v, t = (own[f, x] for f in range(4))
        density = second[2, x]
        viscosity = mu[x]
        span_flux(at, here, u, w, v, t, density, viscosity, dy[V, x], dy[W, x])
        dil = dx[U, x] + dy[V, x] + dz[1, at, here]
        s1 = viscosity * (dy[U, x] + dx[V, x])
        s2 = viscosity * (2.0 * dy[V, x] - (2.0 / 3.0) * dil)
        s3 = viscosity * (dy[W, x] + dz_more[0, at, here])
        m = density * v
        total = m * (enthalpy * t + 0.5 * (u * u + v * v + w * w))
        flux_y[0, at, :] = m
        flux_y[1, at, :] = m * u - s1
        flux_y[2, at, :] = m * v + density * t - s2
        flux_y[3, at, :] = m * w - s3
        flux_y[4, at, :] = (
            total - (s1 * u + s2 * v + s3 * w) - conduction * viscosity * dy[T, x]
        )
        t = peer_second[1, x]
        viscosity = shear_resistance_reference * jnp.exp(sutherland_power_law * jnp.log(t))
        span_flux(
            at, slice(width, 2 * width), peer_first[0, x], peer_first[1, x],
            peer_second[0, x], t, peer_second[2, x], viscosity,
            dy_peer[0, at, :], dy_peer[1, at, :],
        )
        return carry

    lax.fori_loop(0, CX, plane, 0)
    shape = own.shape[1:]
    for f in range(5):
        spread = right_product(flux[f], f_high[odd], f_low[odd])
        local = left_product(y_high[...], y_low[...], flux_y[f])
        part[f] = (spread[:, :width] + local).reshape(shape)
        part_mate[f] = spread[:, width:].reshape(shape)


def kernel_corrections(
    own, peer_first, third, peer_third, part, part_mate, f_high, f_low, total, *for_mate
):
    width = own.shape[-1]
    odd = lax.rem(lax.axis_index("gy"), 2)
    shape = own.shape[1:]
    for f in (0, 2):
        total[f] = part[f]
        for_mate[f][...] = part_mate[f]
    pairs = ((own, third), (peer_first, peer_third))
    for f in (1, 3, 4):
        sides = []
        for speeds, shared in pairs:
            if f == 1:
                value = -shared[1]
            elif f == 3:
                value = shared[0]
            else:
                value = shared[0] * speeds[W] - shared[1] * speeds[U]
            sides.append(flat(value))
        spread = right_product(jnp.concatenate(sides, axis=1), f_high[odd], f_low[odd])
        total[f] = part[f] + spread[:, :width].reshape(shape)
        for_mate[f][...] = part_mate[f] + spread[:, width:].reshape(shape)


def kernel_add_stream(total, flux, before, after, result):
    def field(f, carry):
        for rows in row_chunks(flux.shape[2]):
            derived = compact_x(extended(before, flux, after, f, rows))
            for x in range(CX):
                result[f, x, rows, :] = total[f, x, rows, :] + derived[x]
        return carry

    lax.fori_loop(0, 5, field, 0)


def kernel_finish(
    conserved, total, mate_0, mate_1, mate_2, mate_3, mate_4, tendency, advanced,
    rate, state, sent,
):
    copies = []
    for f, from_mate in enumerate((mate_0, mate_1, mate_2, mate_3, mate_4)):
        value = -(total[f] + from_mate[...])
        rate[f] = value
        state[f] = conserved[f] + section_step * value
        for k, (source, target) in enumerate(((rate, tendency), (state, advanced))):
            copy = pltpu.make_async_copy(source.at[f], target.at[f], sent.at[2 * f + k])
            copy.start()
            copies.append(copy)
    for copy in copies:
        copy.wait()


def call(kernel, outputs, operands, scratch=(), outside=False, written=False):
    space = pltpu.HBM if outside else pltpu.VMEM
    target = pltpu.HBM if written else pltpu.VMEM
    in_specs = [pl.BlockSpec(memory_space=space) for _ in operands]
    if outside:
        operands = [pltpu.with_memory_space_constraint(value, pltpu.HBM) for value in operands]
    touched = sum(value.size * value.dtype.itemsize for value in operands)
    touched += 4 * sum(int(np.prod(shape)) for shape in outputs)
    return pl.pallas_call(
        kernel,
        out_shape=[jax.ShapeDtypeStruct(shape, F32) for shape in outputs],
        in_specs=in_specs,
        out_specs=[pl.BlockSpec(memory_space=target) for _ in outputs],
        scratch_shapes=list(scratch),
        cost_estimate=pl.CostEstimate(flops=0, bytes_accessed=touched, transcendentals=0),
        compiler_params=pltpu.CompilerParams(vmem_limit_bytes=24 * 1024 * 1024),
    )(*operands)


def fast_device(mass_per_volume, momentum, energy):
    rho = jnp.transpose(mass_per_volume, (0, 2, 1))
    mom = jnp.transpose(momentum, (0, 1, 3, 2))
    ene = jnp.transpose(energy, (0, 2, 1))
    _, rows, width = rho.shape
    length = 4 * width
    z_high, z_low = span_blocks(length, PLACES, PLACES[:2])
    f_high, f_low = span_blocks(length, PLACES[:2], (0, 1))
    y_high, y_low = halves(np.kron(np.eye(CX, dtype=np.float32), pitch_matrix(rows, CY)))
    block = (CX, rows, width)
    sums = (2, rows, width)
    points = CX * rows
    devices = lax.axis_size("gx")
    ring_up = [(i, (i + 1) % devices) for i in range(devices)]
    ring_down = [(j, i) for i, j in ring_up]
    to_mate = [(i, i ^ 1) for i in range(4)]
    to_peer = [(i, i ^ 2) for i in range(4)]

    conserved, first = call(
        kernel_inputs,
        [(5,) + block, (2,) + block],
        (rho, mom, ene),
        scratch=(pltpu.SemaphoreType.DMA((3,)),),
        outside=True,
    )
    own, second, up, down = call(
        kernel_primitives,
        [(4,) + block, (3,) + block, (4,) + sums, (4,) + sums],
        (conserved, first),
    )
    peer_first = lax.ppermute(first, "gy", to_peer)
    before = lax.ppermute(up, "gx", ring_up)
    after = lax.ppermute(down, "gx", ring_down)
    dy, mu, for_u, for_w, mate_b = call(
        kernel_pitch_gradients,
        [(4,) + block, block, block, block, (2,) + block],
        (own, y_high, y_low),
    )
    mate_u, mate_w = (lax.ppermute(value, "gy", to_mate) for value in (for_u, for_w))
    second_mate = lax.ppermute(mate_b, "gy", to_mate)
    peer_second = lax.ppermute(second, "gy", to_peer)
    dx, third, for_u, for_w = call(
        kernel_stream_gradients,
        [(4,) + block, (2,) + block, block, block],
        (own, before, after, mu, peer_first),
    )
    across_u, across_w = (lax.ppermute(value, "gy", to_mate) for value in (for_u, for_w))
    peer_third = lax.ppermute(third, "gy", to_peer)
    dz, flux, flux_up, flux_down = call(
        kernel_flux_x,
        [(2, points, 2 * width), (5,) + block, (5,) + sums, (5,) + sums],
        (
            own, second, peer_first, mate_u, mate_w, across_u, across_w, dx, dy, mu,
            z_high, z_low,
        ),
    )
    flux_before = lax.ppermute(flux_up, "gx", ring_up)
    flux_after = lax.ppermute(flux_down, "gx", ring_down)
    for_v, for_t, dy_peer = call(
        kernel_peer,
        [block, block, (2, points, width)],
        (peer_first, peer_second, flux, y_high, y_low),
    )
    across_v = lax.ppermute(for_v, "gy", to_mate)
    across_t = lax.ppermute(for_t, "gy", to_mate)
    part, part_mate = call(
        kernel_flux_yz,
        [(5,) + block, (5,) + block],
        (
            own, second, peer_first, peer_second, second_mate, across_v, across_t, dy_peer,
            dz, dx, dy, mu, y_high, y_low, z_high, z_low, f_high, f_low,
        ),
        scratch=(
            pltpu.VMEM((2, points, 2 * width), F32),
            pltpu.VMEM((5, points, 2 * width), F32),
            pltpu.VMEM((5, points, width), F32),
        ),
    )
    total, *for_mate = call(
        kernel_corrections,
        [(5,) + block] + 5 * [block],
        (own, peer_first, third, peer_third, part, part_mate, f_high, f_low),
    )
    from_mate = [lax.ppermute(value, "gy", to_mate) for value in for_mate]
    (total,) = call(
        kernel_add_stream, [(5,) + block], (total, flux, flux_before, flux_after)
    )
    tendency, advanced = call(
        kernel_finish,
        [(5,) + block, (5,) + block],
        (conserved, total, *from_mate),
        scratch=(
            pltpu.VMEM((5,) + block, F32),
            pltpu.VMEM((5,) + block, F32),
            pltpu.SemaphoreType.DMA((10,)),
        ),
        written=True,
    )
    return (
        jnp.transpose(tendency, (0, 1, 3, 2)),
        jnp.transpose(advanced, (0, 1, 3, 2)),
    )


def padded(array, sides, width):
    for axis, dim in sides:
        devices, length = (lax.axis_size(axis), array.shape[dim])
        up = [(i, (i + 1) % devices) for i in range(devices)]
        down = [(j, i) for i, j in up]
        last = lax.slice_in_dim(array, length - width, length, axis=dim)
        initial = lax.slice_in_dim(array, 0, width, axis=dim)
        before = lax.ppermute(last, axis, up)
        after = lax.ppermute(initial, axis, down)
        array = jnp.concatenate([before, array, after], axis=dim)
    return array


def right_side(conserved, gradients_of, derive_x, derive_y, derive_z):
    mass_per_volume = conserved[0]
    momentum = conserved[1:4]
    energy = conserved[4]
    local_speed_vector = momentum / mass_per_volume
    kinetic = 0.5 * jnp.sum(momentum * local_speed_vector, axis=0)
    normal_force_per_area = (heat_ratio - 1.0) * (energy - kinetic)
    thermal_state = normal_force_per_area / mass_per_volume
    basic_quantities = jnp.concatenate([local_speed_vector, thermal_state[None]], 0)
    gradients = gradients_of(basic_quantities)
    shear_resistance = shear_resistance_reference * jnp.power(thermal_state, sutherland_power_law)
    conductivity = shear_resistance * heat_ratio / ((heat_ratio - 1.0) * prandtl)
    dilatation = gradients[0][0] + gradients[1][1] + gradients[2][2]
    derivers = (derive_x, derive_y, derive_z)
    accumulated = None
    for direction in range(3):
        stress_column = [
            shear_resistance * (gradients[direction][component] + gradients[component][direction])
            for component in range(3)
        ]
        stress_column[direction] = (
            stress_column[direction] - 2.0 / 3.0 * shear_resistance * dilatation
        )
        fluxes = [momentum[direction]]
        for component in range(3):
            moment_flux = (
                momentum[component] * local_speed_vector[direction] - stress_column[component]
            )
            if component == direction:
                moment_flux = moment_flux + normal_force_per_area
            fluxes.append(moment_flux)
        work_term = (
            stress_column[0] * local_speed_vector[0]
            + stress_column[1] * local_speed_vector[1]
            + stress_column[2] * local_speed_vector[2]
        )
        fluxes.append(
            (energy + normal_force_per_area) * local_speed_vector[direction]
            - work_term
            - conductivity * gradients[direction][3]
        )
        divergence_part = derivers[direction](jnp.stack(fluxes))
        accumulated = divergence_part if accumulated is None else accumulated + divergence_part
    return -accumulated


def plain_device(mass_per_volume, momentum, energy):
    conserved = jnp.concatenate([mass_per_volume[None], momentum, energy[None]], 0)
    highest = lax.Precision.HIGHEST
    x_matrix = jnp.asarray(compact_matrix(CX, HALO))
    z_matrix = jnp.asarray(span_matrix(NZ))

    def apply_x(extended):
        return jnp.einsum("il,flab->fiab", x_matrix, extended, precision=highest)

    def flux_x(values):
        return apply_x(padded(values, (("gx", 1),), HALO))

    y_matrix = jnp.asarray(pitch_matrix(conserved.shape[3], CY))

    def apply_y(values):
        return jnp.einsum("fabk,jk->fabj", values, y_matrix, precision=highest)

    def derive_span(values):
        lines = jnp.transpose(
            lax.all_to_all(values, "gy", split_axis=3, concat_axis=2, tiled=True), (0, 1, 3, 2)
        )
        derived = jnp.einsum("fack,jk->facj", lines, z_matrix, precision=highest)
        returned = lax.all_to_all(derived, "gy", split_axis=3, concat_axis=2, tiled=True)
        return jnp.transpose(returned, (0, 1, 3, 2))

    def gradients_of(basic_quantities):
        extended = padded(basic_quantities, (("gx", 1),), HALO)
        return (apply_x(extended), apply_y(basic_quantities), derive_span(basic_quantities))

    tendency = right_side(conserved, gradients_of, flux_x, apply_y, derive_span)
    advanced = conserved + section_step * tendency
    return (tendency, advanced)


def per_device(mass_per_volume, momentum, energy):
    planes, width, rows = mass_per_volume.shape
    fits = planes == CX and width % 128 == 0 and rows <= 32 and rows % CY == 0
    if fits and lax.axis_size("gy") == 4:
        return fast_device(mass_per_volume, momentum, energy)
    return plain_device(mass_per_volume, momentum, energy)


def solution(mesh):
    in_specs = (P("gx", "gy", None), P(None, "gx", "gy", None), P("gx", "gy", None))
    out_specs = (P(None, "gx", "gy", None), P(None, "gx", "gy", None))
    return jax.shard_map(
        per_device, mesh=mesh, in_specs=in_specs, out_specs=out_specs, check_vma=False
    )
```

```python
import functools

import jax
import jax.numpy as jnp
import numpy as np
from jax import lax
from jax.experimental import pallas as pl
from jax.experimental.pallas import tpu as pltpu
from jax.sharding import PartitionSpec as P

CX = 8
CY = 8
NZ = 512
HALO = 4


heat_ratio = 1.4
shear_resistance_reference = 0.08
sutherland_power_law = 0.7
prandtl = 0.72
section_step = 0.05
compact_alpha = 1.0 / 3.0
compact_near = 14.0 / 9.0
compact_far = 1.0 / 9.0

conduction = heat_ratio / ((heat_ratio - 1.0) * prandtl)
enthalpy = heat_ratio / (heat_ratio - 1.0)


def tridiagonal_inverse_product(length, stencil):
    solved = np.array(stencil)
    upper_ratio = np.zeros(length)
    for row_index in range(length):
        if row_index == 0:
            pivot_value = 1.0
            solved[row_index] = solved[row_index] / pivot_value
        else:
            pivot_value = 1.0 - compact_alpha * upper_ratio[row_index - 1]
            solved[row_index] = (
                solved[row_index] - compact_alpha * solved[row_index - 1]
            ) / pivot_value
        upper_ratio[row_index] = compact_alpha / pivot_value
    for row_index in range(length - 2, -1, -1):
        solved[row_index] = solved[row_index] - upper_ratio[row_index] * solved[row_index + 1]
    return solved


def exact_compact_matrix(block_size, margin):
    length = block_size + 2 * margin
    stencil = compact_near / 2.0 * (np.eye(length, k=1) - np.eye(length, k=-1))
    stencil = stencil + compact_far / 4.0 * (np.eye(length, k=2) - np.eye(length, k=-2))
    inverse_product = tridiagonal_inverse_product(length, stencil)
    return inverse_product[margin : margin + block_size]


def compact_matrix(block_size, margin):
    return exact_compact_matrix(block_size, margin).astype(np.float32)


def pitch_matrix(total, block_size):
    matrix = compact_matrix(block_size, HALO)
    result = np.zeros((total, total), np.float32)
    rows_all = np.arange(total)
    block_start = rows_all // block_size * block_size
    for offset in range(block_size + 2 * HALO):
        columns = (block_start - HALO + offset) % total
        result[rows_all, columns] += matrix[rows_all % block_size, offset]
    return result


def span_matrix(total):
    offsets = np.arange(total)[:, None] - np.arange(total)[None, :]
    angles = np.pi * offsets / total
    signs = np.where(offsets % 2 == 0, 1.0, -1.0)
    sines = np.where(offsets == 0, 1.0, np.sin(angles))
    result = np.where(offsets == 0, 0.0, np.pi / total * signs * np.cos(angles) / sines)
    return result.astype(np.float32)


F32 = jnp.float32
BF16 = jnp.bfloat16
U, W, V, T, R = range(5)
PLACES = (0, 2, 1, 3)
HALF = CX // 2


def halves(matrix):
    high = np.asarray(matrix, np.float32).astype(BF16)
    low = (matrix - high.astype(np.float32)).astype(BF16)
    return jnp.asarray(high), jnp.asarray(low)


def span_blocks(length, sources, targets):
    width = length // 4
    matrix = span_matrix(length).T
    both = []
    for core in range(2):
        columns = []
        for target in targets:
            to = core ^ target
            columns.append(
                np.concatenate(
                    [
                        matrix[
                            (core ^ source) * width : (core ^ source) * width + width,
                            to * width : to * width + width,
                        ]
                        for source in sources
                    ],
                    axis=0,
                )
            )
        both.append(np.concatenate(columns, axis=1))
    return halves(np.stack(both))


def halo_basis():
    matrix = exact_compact_matrix(CX, HALO)
    left = matrix[:, :HALO]
    basis = np.linalg.svd(left)[2][:2]
    inner = left @ basis.T
    outer = -inner[::-1]
    return basis, np.concatenate(
        [inner, matrix[:, HALO : HALO + CX], outer[:, ::-1]], axis=1
    )


def split(values):
    high = values.astype(BF16)
    low = (values - high.astype(F32)).astype(BF16)
    return high, low


def dot(a, b):
    return jnp.dot(a, b, preferred_element_type=F32)


def right_product(values, matrix_high, matrix_low):
    high, low = split(values)
    return dot(high, matrix_high) + dot(low, matrix_high) + dot(high, matrix_low)


def left_product(matrix_high, matrix_low, values):
    high, low = split(values)
    return dot(matrix_high, high) + dot(matrix_high, low) + dot(matrix_low, high)


def compact_x(planes):
    matrix = halo_basis()[1]
    length = CX + 4
    half = length // 2
    odd = [planes[l] - planes[length - 1 - l] for l in range(half)]
    even = [planes[l] + planes[length - 1 - l] for l in range(half)]
    result = [None] * CX
    for i in range(HALF):
        first = None
        second = None
        for l in range(half):
            a = float(0.5 * (matrix[i, l] - matrix[i, length - 1 - l]))
            b = float(0.5 * (matrix[i, l] + matrix[i, length - 1 - l]))
            first = a * odd[l] if first is None else first + a * odd[l]
            second = b * even[l] if second is None else second + b * even[l]
        result[i] = first + second
        result[CX - 1 - i] = first - second
    return result


def extended(before, own, after, f, rows):
    return (
        [before[f, 0, rows, :], before[f, 1, rows, :]]
        + [own[f, l, rows, :] for l in range(CX)]
        + [after[f, 1, rows, :], after[f, 0, rows, :]]
    )


def halo_sums(values, f, rows, up, down):
    basis = halo_basis()[0]
    for k in range(2):
        top = None
        bottom = None
        for l in range(HALO):
            a = float(basis[k, l]) * values[f, CX - HALO + l, rows, :]
            b = float(basis[k, l]) * values[f, HALO - 1 - l, rows, :]
            top = a if top is None else top + a
            bottom = b if bottom is None else bottom + b
        up[f, k, rows, :] = top
        down[f, k, rows, :] = bottom


def row_chunks(rows):
    return [slice(start, start + 8) for start in range(0, rows, 8)]


def flat(values):
    return values.reshape(-1, values.shape[-1])


def kernel_inputs(rho_in, mom_in, ene_in, conserved, first, arrived):
    copies = [
        pltpu.make_async_copy(source, conserved.at[part], arrived.at[k])
        for k, (source, part) in enumerate(
            ((rho_in, 0), (mom_in, slice(1, 4)), (ene_in, 4))
        )
    ]
    for copy in copies:
        copy.start()
    for copy in copies:
        copy.wait()

    def plane(x, carry):
        inverse = 1.0 / conserved[0, x]
        first[0, x] = conserved[1, x] * inverse
        first[1, x] = conserved[3, x] * inverse
        return carry

    lax.fori_loop(0, CX, plane, 0, unroll=2)


def kernel_primitives(conserved, first, own, second, up, down):
    def plane(x, carry):
        density = conserved[0, x]
        inverse = 1.0 / density
        u = first[0, x]
        w = first[1, x]
        v = conserved[2, x] * inverse
        kinetic = 0.5 * (conserved[1, x] * u + conserved[2, x] * v + conserved[3, x] * w)
        temperature = (heat_ratio - 1.0) * (conserved[4, x] - kinetic) * inverse
        own[U, x] = u
        own[W, x] = w
        own[V, x] = v
        own[T, x] = temperature
        second[0, x] = v
        second[1, x] = temperature
        second[2, x] = density
        return carry

    lax.fori_loop(0, CX, plane, 0, unroll=2)

    def sums(f, carry):
        for rows in row_chunks(own.shape[2]):
            halo_sums(own, f, rows, up, down)
        return carry

    lax.fori_loop(0, 4, sums, 0)


def kernel_pitch_gradients(
    own, y_high, y_low, dy, mu, mate_u, mate_w, mate_b
):
    for f in range(4):
        dy[f] = left_product(y_high[...], y_low[...], flat(own[f])).reshape(own.shape[1:])

    def plane(x, carry):
        mu[x] = shear_resistance_reference * jnp.exp(
            sutherland_power_law * jnp.log(own[T, x])
        )
        mate_u[x] = own[U, x]
        mate_w[x] = own[W, x]
        for f in range(2):
            mate_b[f, x] = own[V + f, x]
        return carry

    lax.fori_loop(0, CX, plane, 0)


def kernel_stream_gradients(own, before, after, mu, peer_first, dx, third, for_u, for_w):
    for_u[...] = peer_first[0]
    for_w[...] = peer_first[1]

    def field(f, carry):
        for rows in row_chunks(own.shape[2]):
            derived = compact_x(extended(before, own, after, f, rows))
            for x in range(CX):
                dx[f, x, rows, :] = derived[x]
        return carry

    lax.fori_loop(0, 4, field, 0)

    def plane(x, carry):
        third[0, x] = (2.0 / 3.0) * mu[x] * dx[U, x]
        third[1, x] = mu[x] * dx[W, x]
        return carry

    lax.fori_loop(0, CX, plane, 0)


def kernel_flux_x(
    own, second, peer_first, mate_u, mate_w, across_u, across_w, dx, dy, mu,
    z_high, z_low, dz, flux, down, up,
):
    width = own.shape[-1]
    odd = lax.rem(lax.axis_index("gy"), 2)
    for f, (mate, across) in enumerate(((mate_u, across_u), (mate_w, across_w))):
        values = jnp.concatenate(
            [flat(own[f]), flat(peer_first[f]), flat(mate[...]), flat(across[...])], axis=1
        )
        dz[f] = right_product(values, z_high[odd], z_low[odd])

    rows = own.shape[2]

    def plane(x, carry):
        at = pl.ds(pl.multiple_of(x * rows, rows), rows)
        u, w, v, t = (own[f, x] for f in range(4))
        density = second[2, x]
        viscosity = mu[x]
        dil = dx[U, x] + dy[V, x] + dz[1, at, :width]
        s1 = viscosity * (2.0 * dx[U, x] - (2.0 / 3.0) * dil)
        s2 = viscosity * (dx[V, x] + dy[U, x])
        s3 = viscosity * (dx[W, x] + dz[0, at, :width])
        m = density * u
        total = m * (enthalpy * t + 0.5 * (u * u + v * v + w * w))
        flux[0, x] = m
        flux[1, x] = m * u + density * t - s1
        flux[2, x] = m * v - s2
        flux[3, x] = m * w - s3
        flux[4, x] = total - (s1 * u + s2 * v + s3 * w) - conduction * viscosity * dx[T, x]
        return carry

    lax.fori_loop(0, CX, plane, 0)

    def sums(f, carry):
        for chunk in row_chunks(rows):
            halo_sums(flux, f, chunk, up, down)
        return carry

    lax.fori_loop(0, 5, sums, 0)


def kernel_peer(peer_first, peer_second, flux, y_high, y_low, for_v, for_t, dy_peer):
    for_v[...] = peer_second[0]
    for_t[...] = peer_second[1]
    dy_peer[0] = left_product(y_high[...], y_low[...], flat(peer_second[0]))
    dy_peer[1] = left_product(y_high[...], y_low[...], flat(peer_first[1]))


def kernel_flux_yz(
    own, second, peer_first, peer_second, second_mate, across_v, across_t, dy_peer,
    dz, dx, dy, mu, y_high, y_low, z_high, z_low, f_high, f_low, part, part_mate,
    dz_more, flux, flux_y,
):
    rows, width = own.shape[2:]
    odd = lax.rem(lax.axis_index("gy"), 2)
    for f, across in enumerate((across_v, across_t)):
        values = jnp.concatenate(
            [flat(own[V + f]), flat(peer_second[f]), flat(second_mate[f]), flat(across[...])],
            axis=1,
        )
        dz_more[f] = right_product(values, z_high[odd], z_low[odd])

    def span_flux(at, lanes, u, w, v, t, density, viscosity, yv, yw):
        s1 = viscosity * dz[0, at, lanes]
        s2 = viscosity * (dz_more[0, at, lanes] + yw)
        s3 = viscosity * ((4.0 / 3.0) * dz[1, at, lanes] - (2.0 / 3.0) * yv)
        m = density * w
        total = m * (enthalpy * t + 0.5 * (u * u + v * v + w * w))
        flux[0, at, lanes] = m
        flux[1, at, lanes] = m * u - s1
        flux[2, at, lanes] = m * v - s2
        flux[3, at, lanes] = m * w + density * t - s3
        flux[4, at, lanes] = (
            total
            - (s1 * u + s2 * v + s3 * w)
            - conduction * viscosity * dz_more[1, at, lanes]
        )

    def plane(x, carry):
        at = pl.ds(pl.multiple_of(x * rows, rows), rows)
        here = slice(0, width)
        u, w, v, t = (own[f, x] for f in range(4))
        density = second[2, x]
        viscosity = mu[x]
        span_flux(at, here, u, w, v, t, density, viscosity, dy[V, x], dy[W, x])
        dil = dx[U, x] + dy[V, x] + dz[1, at, here]
        s1 = viscosity * (dy[U, x] + dx[V, x])
        s2 = viscosity * (2.0 * dy[V, x] - (2.0 / 3.0) * dil)
        s3 = viscosity * (dy[W, x] + dz_more[0, at, here])
        m = density * v
        total = m * (enthalpy * t + 0.5 * (u * u + v * v + w * w))
        flux_y[0, at, :] = m
        flux_y[1, at, :] = m * u - s1
        flux_y[2, at, :] = m * v + density * t - s2
        flux_y[3, at, :] = m * w - s3
        flux_y[4, at, :] = (
            total - (s1 * u + s2 * v + s3 * w) - conduction * viscosity * dy[T, x]
        )
        t = peer_second[1, x]
        viscosity = shear_resistance_reference * jnp.exp(sutherland_power_law * jnp.log(t))
        span_flux(
            at, slice(width, 2 * width), peer_first[0, x], peer_first[1, x],
            peer_second[0, x], t, peer_second[2, x], viscosity,
            dy_peer[0, at, :], dy_peer[1, at, :],
        )
        return carry

    lax.fori_loop(0, CX, plane, 0)
    shape = own.shape[1:]
    for f in range(5):
        spread = right_product(flux[f], f_high[odd], f_low[odd])
        local = left_product(y_high[...], y_low[...], flux_y[f])
        part[f] = (spread[:, :width] + local).reshape(shape)
        part_mate[f] = spread[:, width:].reshape(shape)


def kernel_corrections(
    own, peer_first, third, peer_third, part, part_mate, f_high, f_low, total, *for_mate
):
    width = own.shape[-1]
    odd = lax.rem(lax.axis_index("gy"), 2)
    shape = own.shape[1:]
    for f in (0, 2):
        total[f] = part[f]
        for_mate[f][...] = part_mate[f]
    pairs = ((own, third), (peer_first, peer_third))
    for f in (1, 3, 4):
        sides = []
        for speeds, shared in pairs:
            if f == 1:
                value = -shared[1]
            elif f == 3:
                value = shared[0]
            else:
                value = shared[0] * speeds[W] - shared[1] * speeds[U]
            sides.append(flat(value))
        spread = right_product(jnp.concatenate(sides, axis=1), f_high[odd], f_low[odd])
        total[f] = part[f] + spread[:, :width].reshape(shape)
        for_mate[f][...] = part_mate[f] + spread[:, width:].reshape(shape)


def kernel_add_stream(total, flux, after, before, result):
    def field(f, carry):
        for rows in row_chunks(flux.shape[2]):
            derived = compact_x(extended(before, flux, after, f, rows))
            for x in range(CX):
                result[f, x, rows, :] = total[f, x, rows, :] + derived[x]
        return carry

    lax.fori_loop(0, 5, field, 0)


def kernel_finish(
    conserved, total, mate_0, mate_1, mate_2, mate_3, mate_4, tendency, advanced,
    rate, state, sent,
):
    copies = []
    for f, from_mate in enumerate((mate_0, mate_1, mate_2, mate_3, mate_4)):
        value = -(total[f] + from_mate[...])
        rate[f] = value
        state[f] = conserved[f] + section_step * value
        for k, (source, target) in enumerate(((rate, tendency), (state, advanced))):
            copy = pltpu.make_async_copy(source.at[f], target.at[f], sent.at[2 * f + k])
            copy.start()
            copies.append(copy)
    for copy in copies:
        copy.wait()


def call(kernel, outputs, operands, scratch=(), outside=False, written=False):
    space = pltpu.HBM if outside else pltpu.VMEM
    target = pltpu.HBM if written else pltpu.VMEM
    in_specs = [pl.BlockSpec(memory_space=space) for _ in operands]
    if outside:
        operands = [pltpu.with_memory_space_constraint(value, pltpu.HBM) for value in operands]
    touched = sum(value.size * value.dtype.itemsize for value in operands)
    touched += 4 * sum(int(np.prod(shape)) for shape in outputs)
    return pl.pallas_call(
        kernel,
        out_shape=[jax.ShapeDtypeStruct(shape, F32) for shape in outputs],
        in_specs=in_specs,
        out_specs=[pl.BlockSpec(memory_space=target) for _ in outputs],
        scratch_shapes=list(scratch),
        cost_estimate=pl.CostEstimate(flops=0, bytes_accessed=touched, transcendentals=0),
        compiler_params=pltpu.CompilerParams(vmem_limit_bytes=24 * 1024 * 1024),
    )(*operands)


def fast_device(mass_per_volume, momentum, energy):
    rho = jnp.transpose(mass_per_volume, (0, 2, 1))
    mom = jnp.transpose(momentum, (0, 1, 3, 2))
    ene = jnp.transpose(energy, (0, 2, 1))
    _, rows, width = rho.shape
    length = 4 * width
    z_high, z_low = span_blocks(length, PLACES, PLACES[:2])
    f_high, f_low = span_blocks(length, PLACES[:2], (0, 1))
    y_high, y_low = halves(np.kron(np.eye(CX, dtype=np.float32), pitch_matrix(rows, CY)))
    block = (CX, rows, width)
    sums = (2, rows, width)
    points = CX * rows
    devices = lax.axis_size("gx")
    ring_up = [(i, (i + 1) % devices) for i in range(devices)]
    ring_down = [(j, i) for i, j in ring_up]
    to_mate = [(i, i ^ 1) for i in range(4)]
    to_peer = [(i, i ^ 2) for i in range(4)]

    conserved, first = call(
        kernel_inputs,
        [(5,) + block, (2,) + block],
        (rho, mom, ene),
        scratch=(pltpu.SemaphoreType.DMA((3,)),),
        outside=True,
    )
    own, second, up, down = call(
        kernel_primitives,
        [(4,) + block, (3,) + block, (4,) + sums, (4,) + sums],
        (conserved, first),
    )
    peer_first = lax.ppermute(first, "gy", to_peer)
    before = lax.ppermute(up, "gx", ring_up)
    after = lax.ppermute(down, "gx", ring_down)
    dy, mu, for_u, for_w, mate_b = call(
        kernel_pitch_gradients,
        [(4,) + block, block, block, block, (2,) + block],
        (own, y_high, y_low),
    )
    mate_u, mate_w = (lax.ppermute(value, "gy", to_mate) for value in (for_u, for_w))
    second_mate = lax.ppermute(mate_b, "gy", to_mate)
    peer_second = lax.ppermute(second, "gy", to_peer)
    dx, third, for_u, for_w = call(
        kernel_stream_gradients,
        [(4,) + block, (2,) + block, block, block],
        (own, before, after, mu, peer_first),
    )
    across_u, across_w = (lax.ppermute(value, "gy", to_mate) for value in (for_u, for_w))
    peer_third = lax.ppermute(third, "gy", to_peer)
    dz, flux, flux_down, flux_up = call(
        kernel_flux_x,
        [(2, points, 2 * width), (5,) + block, (5,) + sums, (5,) + sums],
        (
            own, second, peer_first, mate_u, mate_w, across_u, across_w, dx, dy, mu,
            z_high, z_low,
        ),
    )
    flux_after = lax.ppermute(flux_down, "gx", ring_down)
    flux_before = lax.ppermute(flux_up, "gx", ring_up)
    for_v, for_t, dy_peer = call(
        kernel_peer,
        [block, block, (2, points, width)],
        (peer_first, peer_second, flux, y_high, y_low),
    )
    across_v = lax.ppermute(for_v, "gy", to_mate)
    across_t = lax.ppermute(for_t, "gy", to_mate)
    part, part_mate = call(
        kernel_flux_yz,
        [(5,) + block, (5,) + block],
        (
            own, second, peer_first, peer_second, second_mate, across_v, across_t, dy_peer,
            dz, dx, dy, mu, y_high, y_low, z_high, z_low, f_high, f_low,
        ),
        scratch=(
            pltpu.VMEM((2, points, 2 * width), F32),
            pltpu.VMEM((5, points, 2 * width), F32),
            pltpu.VMEM((5, points, width), F32),
        ),
    )
    total, *for_mate = call(
        kernel_corrections,
        [(5,) + block] + 5 * [block],
        (own, peer_first, third, peer_third, part, part_mate, f_high, f_low),
    )
    from_mate = [lax.ppermute(value, "gy", to_mate) for value in for_mate]
    (total,) = call(
        kernel_add_stream, [(5,) + block], (total, flux, flux_after, flux_before)
    )
    tendency, advanced = call(
        kernel_finish,
        [(5,) + block, (5,) + block],
        (conserved, total, *from_mate),
        scratch=(
            pltpu.VMEM((5,) + block, F32),
            pltpu.VMEM((5,) + block, F32),
            pltpu.SemaphoreType.DMA((10,)),
        ),
        written=True,
    )
    return (
        jnp.transpose(tendency, (0, 1, 3, 2)),
        jnp.transpose(advanced, (0, 1, 3, 2)),
    )


def padded(array, sides, width):
    for axis, dim in sides:
        devices, length = (lax.axis_size(axis), array.shape[dim])
        up = [(i, (i + 1) % devices) for i in range(devices)]
        down = [(j, i) for i, j in up]
        last = lax.slice_in_dim(array, length - width, length, axis=dim)
        initial = lax.slice_in_dim(array, 0, width, axis=dim)
        before = lax.ppermute(last, axis, up)
        after = lax.ppermute(initial, axis, down)
        array = jnp.concatenate([before, array, after], axis=dim)
    return array


def right_side(conserved, gradients_of, derive_x, derive_y, derive_z):
    mass_per_volume = conserved[0]
    momentum = conserved[1:4]
    energy = conserved[4]
    local_speed_vector = momentum / mass_per_volume
    kinetic = 0.5 * jnp.sum(momentum * local_speed_vector, axis=0)
    normal_force_per_area = (heat_ratio - 1.0) * (energy - kinetic)
    thermal_state = normal_force_per_area / mass_per_volume
    basic_quantities = jnp.concatenate([local_speed_vector, thermal_state[None]], 0)
    gradients = gradients_of(basic_quantities)
    shear_resistance = shear_resistance_reference * jnp.power(thermal_state, sutherland_power_law)
    conductivity = shear_resistance * heat_ratio / ((heat_ratio - 1.0) * prandtl)
    dilatation = gradients[0][0] + gradients[1][1] + gradients[2][2]
    derivers = (derive_x, derive_y, derive_z)
    accumulated = None
    for direction in range(3):
        stress_column = [
            shear_resistance * (gradients[direction][component] + gradients[component][direction])
            for component in range(3)
        ]
        stress_column[direction] = (
            stress_column[direction] - 2.0 / 3.0 * shear_resistance * dilatation
        )
        fluxes = [momentum[direction]]
        for component in range(3):
            moment_flux = (
                momentum[component] * local_speed_vector[direction] - stress_column[component]
            )
            if component == direction:
                moment_flux = moment_flux + normal_force_per_area
            fluxes.append(moment_flux)
        work_term = (
            stress_column[0] * local_speed_vector[0]
            + stress_column[1] * local_speed_vector[1]
            + stress_column[2] * local_speed_vector[2]
        )
        fluxes.append(
            (energy + normal_force_per_area) * local_speed_vector[direction]
            - work_term
            - conductivity * gradients[direction][3]
        )
        divergence_part = derivers[direction](jnp.stack(fluxes))
        accumulated = divergence_part if accumulated is None else accumulated + divergence_part
    return -accumulated


def plain_device(mass_per_volume, momentum, energy):
    conserved = jnp.concatenate([mass_per_volume[None], momentum, energy[None]], 0)
    highest = lax.Precision.HIGHEST
    x_matrix = jnp.asarray(compact_matrix(CX, HALO))
    z_matrix = jnp.asarray(span_matrix(NZ))

    def apply_x(extended):
        return jnp.einsum("il,flab->fiab", x_matrix, extended, precision=highest)

    def flux_x(values):
        return apply_x(padded(values, (("gx", 1),), HALO))

    y_matrix = jnp.asarray(pitch_matrix(conserved.shape[3], CY))

    def apply_y(values):
        return jnp.einsum("fabk,jk->fabj", values, y_matrix, precision=highest)

    def derive_span(values):
        lines = jnp.transpose(
            lax.all_to_all(values, "gy", split_axis=3, concat_axis=2, tiled=True), (0, 1, 3, 2)
        )
        derived = jnp.einsum("fack,jk->facj", lines, z_matrix, precision=highest)
        returned = lax.all_to_all(derived, "gy", split_axis=3, concat_axis=2, tiled=True)
        return jnp.transpose(returned, (0, 1, 3, 2))

    def gradients_of(basic_quantities):
        extended = padded(basic_quantities, (("gx", 1),), HALO)
        return (apply_x(extended), apply_y(basic_quantities), derive_span(basic_quantities))

    tendency = right_side(conserved, gradients_of, flux_x, apply_y, derive_span)
    advanced = conserved + section_step * tendency
    return (tendency, advanced)


def per_device(mass_per_volume, momentum, energy):
    planes, width, rows = mass_per_volume.shape
    fits = planes == CX and width % 128 == 0 and rows <= 32 and rows % CY == 0
    if fits and lax.axis_size("gy") == 4:
        return fast_device(mass_per_volume, momentum, energy)
    return plain_device(mass_per_volume, momentum, energy)


def solution(mesh):
    in_specs = (P("gx", "gy", None), P(None, "gx", "gy", None), P("gx", "gy", None))
    out_specs = (P(None, "gx", "gy", None), P(None, "gx", "gy", None))
    return jax.shard_map(
        per_device, mesh=mesh, in_specs=in_specs, out_specs=out_specs, check_vma=False
    )
```

```python
import functools

import jax
import jax.numpy as jnp
import numpy as np
from jax import lax
from jax.experimental import pallas as pl
from jax.experimental.pallas import tpu as pltpu
from jax.sharding import PartitionSpec as P

CX = 8
CY = 8
NZ = 512
HALO = 4


heat_ratio = 1.4
shear_resistance_reference = 0.08
sutherland_power_law = 0.7
prandtl = 0.72
section_step = 0.05
compact_alpha = 1.0 / 3.0
compact_near = 14.0 / 9.0
compact_far = 1.0 / 9.0

conduction = heat_ratio / ((heat_ratio - 1.0) * prandtl)
enthalpy = heat_ratio / (heat_ratio - 1.0)


def tridiagonal_inverse_product(length, stencil):
    solved = np.array(stencil)
    upper_ratio = np.zeros(length)
    for row_index in range(length):
        if row_index == 0:
            pivot_value = 1.0
            solved[row_index] = solved[row_index] / pivot_value
        else:
            pivot_value = 1.0 - compact_alpha * upper_ratio[row_index - 1]
            solved[row_index] = (
                solved[row_index] - compact_alpha * solved[row_index - 1]
            ) / pivot_value
        upper_ratio[row_index] = compact_alpha / pivot_value
    for row_index in range(length - 2, -1, -1):
        solved[row_index] = solved[row_index] - upper_ratio[row_index] * solved[row_index + 1]
    return solved


def exact_compact_matrix(block_size, margin):
    length = block_size + 2 * margin
    stencil = compact_near / 2.0 * (np.eye(length, k=1) - np.eye(length, k=-1))
    stencil = stencil + compact_far / 4.0 * (np.eye(length, k=2) - np.eye(length, k=-2))
    inverse_product = tridiagonal_inverse_product(length, stencil)
    return inverse_product[margin : margin + block_size]


def compact_matrix(block_size, margin):
    return exact_compact_matrix(block_size, margin).astype(np.float32)


def pitch_matrix(total, block_size):
    matrix = compact_matrix(block_size, HALO)
    result = np.zeros((total, total), np.float32)
    rows_all = np.arange(total)
    block_start = rows_all // block_size * block_size
    for offset in range(block_size + 2 * HALO):
        columns = (block_start - HALO + offset) % total
        result[rows_all, columns] += matrix[rows_all % block_size, offset]
    return result


def span_matrix(total):
    offsets = np.arange(total)[:, None] - np.arange(total)[None, :]
    angles = np.pi * offsets / total
    signs = np.where(offsets % 2 == 0, 1.0, -1.0)
    sines = np.where(offsets == 0, 1.0, np.sin(angles))
    result = np.where(offsets == 0, 0.0, np.pi / total * signs * np.cos(angles) / sines)
    return result.astype(np.float32)


F32 = jnp.float32
BF16 = jnp.bfloat16
U, W, V, T, R = range(5)
PLACES = (0, 2, 1, 3)
HALF = CX // 2


def halves(matrix):
    high = np.asarray(matrix, np.float32).astype(BF16)
    low = (matrix - high.astype(np.float32)).astype(BF16)
    return jnp.asarray(high), jnp.asarray(low)


def span_blocks(length, sources, targets):
    width = length // 4
    matrix = span_matrix(length).T
    both = []
    for core in range(2):
        columns = []
        for target in targets:
            to = core ^ target
            columns.append(
                np.concatenate(
                    [
                        matrix[
                            (core ^ source) * width : (core ^ source) * width + width,
                            to * width : to * width + width,
                        ]
                        for source in sources
                    ],
                    axis=0,
                )
            )
        both.append(np.concatenate(columns, axis=1))
    return halves(np.stack(both))


def halo_basis():
    matrix = exact_compact_matrix(CX, HALO)
    left = matrix[:, :HALO]
    basis = np.linalg.svd(left)[2][:2]
    inner = left @ basis.T
    outer = -inner[::-1]
    return basis, np.concatenate(
        [inner, matrix[:, HALO : HALO + CX], outer[:, ::-1]], axis=1
    )


def split(values):
    high = values.astype(BF16)
    low = (values - high.astype(F32)).astype(BF16)
    return high, low


def dot(a, b):
    return jnp.dot(a, b, preferred_element_type=F32)


def right_product(values, matrix_high, matrix_low):
    high, low = split(values)
    return dot(high, matrix_high) + dot(low, matrix_high) + dot(high, matrix_low)


def left_product(matrix_high, matrix_low, values):
    high, low = split(values)
    return dot(matrix_high, high) + dot(matrix_high, low) + dot(matrix_low, high)


def compact_x(planes):
    matrix = halo_basis()[1]
    length = CX + 4
    half = length // 2
    odd = [planes[l] - planes[length - 1 - l] for l in range(half)]
    even = [planes[l] + planes[length - 1 - l] for l in range(half)]
    result = [None] * CX
    for i in range(HALF):
        first = None
        second = None
        for l in range(half):
            a = float(0.5 * (matrix[i, l] - matrix[i, length - 1 - l]))
            b = float(0.5 * (matrix[i, l] + matrix[i, length - 1 - l]))
            first = a * odd[l] if first is None else first + a * odd[l]
            second = b * even[l] if second is None else second + b * even[l]
        result[i] = first + second
        result[CX - 1 - i] = first - second
    return result


def extended(before, own, after, f, rows):
    return (
        [before[f, 0, rows, :], before[f, 1, rows, :]]
        + [own[f, l, rows, :] for l in range(CX)]
        + [after[f, 1, rows, :], after[f, 0, rows, :]]
    )


def halo_sums(values, f, rows, up, down):
    basis = halo_basis()[0]
    for k in range(2):
        top = None
        bottom = None
        for l in range(HALO):
            a = float(basis[k, l]) * values[f, CX - HALO + l, rows, :]
            b = float(basis[k, l]) * values[f, HALO - 1 - l, rows, :]
            top = a if top is None else top + a
            bottom = b if bottom is None else bottom + b
        up[f, k, rows, :] = top
        down[f, k, rows, :] = bottom


def row_chunks(rows):
    return [slice(start, start + 8) for start in range(0, rows, 8)]


def flat(values):
    return values.reshape(-1, values.shape[-1])


def kernel_inputs(rho_in, mom_in, ene_in, conserved, first, arrived):
    copies = [
        pltpu.make_async_copy(source, conserved.at[part], arrived.at[k])
        for k, (source, part) in enumerate(
            ((rho_in, 0), (mom_in, slice(1, 4)), (ene_in, 4))
        )
    ]
    for copy in copies:
        copy.start()
    for copy in copies:
        copy.wait()

    def plane(x, carry):
        inverse = 1.0 / conserved[0, x]
        first[0, x] = conserved[1, x] * inverse
        first[1, x] = conserved[3, x] * inverse
        return carry

    lax.fori_loop(0, CX, plane, 0, unroll=2)


def kernel_primitives(conserved, first, own, second, up, down):
    def plane(x, carry):
        density = conserved[0, x]
        inverse = 1.0 / density
        u = first[0, x]
        w = first[1, x]
        v = conserved[2, x] * inverse
        kinetic = 0.5 * (conserved[1, x] * u + conserved[2, x] * v + conserved[3, x] * w)
        temperature = (heat_ratio - 1.0) * (conserved[4, x] - kinetic) * inverse
        own[U, x] = u
        own[W, x] = w
        own[V, x] = v
        own[T, x] = temperature
        second[0, x] = v
        second[1, x] = temperature
        second[2, x] = density
        return carry

    lax.fori_loop(0, CX, plane, 0, unroll=2)

    def sums(f, carry):
        for rows in row_chunks(own.shape[2]):
            halo_sums(own, f, rows, up, down)
        return carry

    lax.fori_loop(0, 4, sums, 0)


def kernel_pitch_gradients(
    own, y_high, y_low, dy, mu, mate_u, mate_w, mate_b
):
    for f in range(4):
        dy[f] = left_product(y_high[...], y_low[...], flat(own[f])).reshape(own.shape[1:])

    def plane(x, carry):
        mu[x] = shear_resistance_reference * jnp.exp(
            sutherland_power_law * jnp.log(own[T, x])
        )
        mate_u[x] = own[U, x]
        mate_w[x] = own[W, x]
        for f in range(2):
            mate_b[f, x] = own[V + f, x]
        return carry

    lax.fori_loop(0, CX, plane, 0)


def kernel_stream_gradients(own, before, after, mu, peer_first, dx, third, for_u, for_w):
    for_u[...] = peer_first[0]
    for_w[...] = peer_first[1]

    def field(f, carry):
        for rows in row_chunks(own.shape[2]):
            derived = compact_x(extended(before, own, after, f, rows))
            for x in range(CX):
                dx[f, x, rows, :] = derived[x]
        return carry

    lax.fori_loop(0, 4, field, 0)

    def plane(x, carry):
        third[0, x] = (2.0 / 3.0) * mu[x] * dx[U, x]
        third[1, x] = mu[x] * dx[W, x]
        return carry

    lax.fori_loop(0, CX, plane, 0)


def kernel_flux_x(
    own, second, peer_first, mate_u, mate_w, across_u, across_w, dx, dy, mu,
    z_high, z_low, dz, flux, far, near,
):
    width = own.shape[-1]
    odd = lax.rem(lax.axis_index("gy"), 2)
    for f, (mate, across) in enumerate(((mate_u, across_u), (mate_w, across_w))):
        values = jnp.concatenate(
            [flat(own[f]), flat(peer_first[f]), flat(mate[...]), flat(across[...])], axis=1
        )
        dz[f] = right_product(values, z_high[odd], z_low[odd])

    rows = own.shape[2]

    def plane(x, carry):
        at = pl.ds(pl.multiple_of(x * rows, rows), rows)
        u, w, v, t = (own[f, x] for f in range(4))
        density = second[2, x]
        viscosity = mu[x]
        dil = dx[U, x] + dy[V, x] + dz[1, at, :width]
        s1 = viscosity * (2.0 * dx[U, x] - (2.0 / 3.0) * dil)
        s2 = viscosity * (dx[V, x] + dy[U, x])
        s3 = viscosity * (dx[W, x] + dz[0, at, :width])
        m = density * u
        total = m * (enthalpy * t + 0.5 * (u * u + v * v + w * w))
        flux[0, x] = m
        flux[1, x] = m * u + density * t - s1
        flux[2, x] = m * v - s2
        flux[3, x] = m * w - s3
        flux[4, x] = total - (s1 * u + s2 * v + s3 * w) - conduction * viscosity * dx[T, x]
        return carry

    lax.fori_loop(0, CX, plane, 0)
    even = lax.rem(lax.axis_index("gx"), 2) == 0
    basis = halo_basis()[0]

    def sums(f, carry):
        for chunk in row_chunks(rows):
            planes = [flux[f, x, chunk, :] for x in range(CX)]
            for k in range(2):
                top = sum(float(basis[k, l]) * planes[CX - HALO + l] for l in range(HALO))
                bottom = sum(float(basis[k, l]) * planes[HALO - 1 - l] for l in range(HALO))
                far[f, k, chunk, :] = jnp.where(even, bottom, top)
                near[f, k, chunk, :] = jnp.where(even, top, bottom)
        return carry

    lax.fori_loop(0, 5, sums, 0)


def kernel_peer(peer_first, peer_second, flux, y_high, y_low, for_v, for_t, dy_peer):
    for_v[...] = peer_second[0]
    for_t[...] = peer_second[1]
    dy_peer[0] = left_product(y_high[...], y_low[...], flat(peer_second[0]))
    dy_peer[1] = left_product(y_high[...], y_low[...], flat(peer_first[1]))


def kernel_flux_yz(
    own, second, peer_first, peer_second, second_mate, across_v, across_t, dy_peer,
    dz, dx, dy, mu, y_high, y_low, z_high, z_low, f_high, f_low, part, part_mate,
    dz_more, flux, flux_y,
):
    rows, width = own.shape[2:]
    odd = lax.rem(lax.axis_index("gy"), 2)
    for f, across in enumerate((across_v, across_t)):
        values = jnp.concatenate(
            [flat(own[V + f]), flat(peer_second[f]), flat(second_mate[f]), flat(across[...])],
            axis=1,
        )
        dz_more[f] = right_product(values, z_high[odd], z_low[odd])

    def span_flux(at, lanes, u, w, v, t, density, viscosity, yv, yw):
        s1 = viscosity * dz[0, at, lanes]
        s2 = viscosity * (dz_more[0, at, lanes] + yw)
        s3 = viscosity * ((4.0 / 3.0) * dz[1, at, lanes] - (2.0 / 3.0) * yv)
        m = density * w
        total = m * (enthalpy * t + 0.5 * (u * u + v * v + w * w))
        flux[0, at, lanes] = m
        flux[1, at, lanes] = m * u - s1
        flux[2, at, lanes] = m * v - s2
        flux[3, at, lanes] = m * w + density * t - s3
        flux[4, at, lanes] = (
            total
            - (s1 * u + s2 * v + s3 * w)
            - conduction * viscosity * dz_more[1, at, lanes]
        )

    def plane(x, carry):
        at = pl.ds(pl.multiple_of(x * rows, rows), rows)
        here = slice(0, width)
        u, w, v, t = (own[f, x] for f in range(4))
        density = second[2, x]
        viscosity = mu[x]
        span_flux(at, here, u, w, v, t, density, viscosity, dy[V, x], dy[W, x])
        dil = dx[U, x] + dy[V, x] + dz[1, at, here]
        s1 = viscosity * (dy[U, x] + dx[V, x])
        s2 = viscosity * (2.0 * dy[V, x] - (2.0 / 3.0) * dil)
        s3 = viscosity * (dy[W, x] + dz_more[0, at, here])
        m = density * v
        total = m * (enthalpy * t + 0.5 * (u * u + v * v + w * w))
        flux_y[0, at, :] = m
        flux_y[1, at, :] = m * u - s1
        flux_y[2, at, :] = m * v + density * t - s2
        flux_y[3, at, :] = m * w - s3
        flux_y[4, at, :] = (
            total - (s1 * u + s2 * v + s3 * w) - conduction * viscosity * dy[T, x]
        )
        t = peer_second[1, x]
        viscosity = shear_resistance_reference * jnp.exp(sutherland_power_law * jnp.log(t))
        span_flux(
            at, slice(width, 2 * width), peer_first[0, x], peer_first[1, x],
            peer_second[0, x], t, peer_second[2, x], viscosity,
            dy_peer[0, at, :], dy_peer[1, at, :],
        )
        return carry

    lax.fori_loop(0, CX, plane, 0)
    shape = own.shape[1:]
    for f in range(5):
        spread = right_product(flux[f], f_high[odd], f_low[odd])
        local = left_product(y_high[...], y_low[...], flux_y[f])
        part[f] = (spread[:, :width] + local).reshape(shape)
        part_mate[f] = spread[:, width:].reshape(shape)


def kernel_corrections(
    own, peer_first, third, peer_third, part, part_mate, f_high, f_low, total, *for_mate
):
    width = own.shape[-1]
    odd = lax.rem(lax.axis_index("gy"), 2)
    shape = own.shape[1:]
    for f in (0, 2):
        total[f] = part[f]
        for_mate[f][...] = part_mate[f]
    pairs = ((own, third), (peer_first, peer_third))
    for f in (1, 3, 4):
        sides = []
        for speeds, shared in pairs:
            if f == 1:
                value = -shared[1]
            elif f == 3:
                value = shared[0]
            else:
                value = shared[0] * speeds[W] - shared[1] * speeds[U]
            sides.append(flat(value))
        spread = right_product(jnp.concatenate(sides, axis=1), f_high[odd], f_low[odd])
        total[f] = part[f] + spread[:, :width].reshape(shape)
        for_mate[f][...] = part_mate[f] + spread[:, width:].reshape(shape)


def kernel_add_stream(total, flux, far, near, result):
    even = lax.rem(lax.axis_index("gx"), 2) == 0

    def field(f, carry):
        for rows in row_chunks(flux.shape[2]):
            before = [jnp.where(even, far[f, k, rows, :], near[f, k, rows, :]) for k in (0, 1)]
            after = [jnp.where(even, near[f, k, rows, :], far[f, k, rows, :]) for k in (1, 0)]
            derived = compact_x(before + [flux[f, l, rows, :] for l in range(CX)] + after)
            for x in range(CX):
                result[f, x, rows, :] = total[f, x, rows, :] + derived[x]
        return carry

    lax.fori_loop(0, 5, field, 0)


def kernel_finish(
    conserved, total, mate_0, mate_1, mate_2, mate_3, mate_4, tendency, advanced,
    rate, state, sent,
):
    copies = []
    for f, from_mate in enumerate((mate_0, mate_1, mate_2, mate_3, mate_4)):
        value = -(total[f] + from_mate[...])
        rate[f] = value
        state[f] = conserved[f] + section_step * value
        for k, (source, target) in enumerate(((rate, tendency), (state, advanced))):
            copy = pltpu.make_async_copy(source.at[f], target.at[f], sent.at[2 * f + k])
            copy.start()
            copies.append(copy)
    for copy in copies:
        copy.wait()


def call(kernel, outputs, operands, scratch=(), outside=False, written=False):
    space = pltpu.HBM if outside else pltpu.VMEM
    target = pltpu.HBM if written else pltpu.VMEM
    in_specs = [pl.BlockSpec(memory_space=space) for _ in operands]
    if outside:
        operands = [pltpu.with_memory_space_constraint(value, pltpu.HBM) for value in operands]
    touched = sum(value.size * value.dtype.itemsize for value in operands)
    touched += 4 * sum(int(np.prod(shape)) for shape in outputs)
    return pl.pallas_call(
        kernel,
        out_shape=[jax.ShapeDtypeStruct(shape, F32) for shape in outputs],
        in_specs=in_specs,
        out_specs=[pl.BlockSpec(memory_space=target) for _ in outputs],
        scratch_shapes=list(scratch),
        cost_estimate=pl.CostEstimate(flops=0, bytes_accessed=touched, transcendentals=0),
        compiler_params=pltpu.CompilerParams(vmem_limit_bytes=24 * 1024 * 1024),
    )(*operands)


def fast_device(mass_per_volume, momentum, energy):
    rho = jnp.transpose(mass_per_volume, (0, 2, 1))
    mom = jnp.transpose(momentum, (0, 1, 3, 2))
    ene = jnp.transpose(energy, (0, 2, 1))
    _, rows, width = rho.shape
    length = 4 * width
    z_high, z_low = span_blocks(length, PLACES, PLACES[:2])
    f_high, f_low = span_blocks(length, PLACES[:2], (0, 1))
    y_high, y_low = halves(np.kron(np.eye(CX, dtype=np.float32), pitch_matrix(rows, CY)))
    block = (CX, rows, width)
    sums = (2, rows, width)
    points = CX * rows
    devices = lax.axis_size("gx")
    ring_up = [(i, (i + 1) % devices) for i in range(devices)]
    ring_down = [(j, i) for i, j in ring_up]
    near_pairs = [(i, i ^ 1) for i in range(devices)]
    far_pairs = [(i, (i - 1 + 2 * (i % 2)) % devices) for i in range(devices)]
    to_mate = [(i, i ^ 1) for i in range(4)]
    to_peer = [(i, i ^ 2) for i in range(4)]

    conserved, first = call(
        kernel_inputs,
        [(5,) + block, (2,) + block],
        (rho, mom, ene),
        scratch=(pltpu.SemaphoreType.DMA((3,)),),
        outside=True,
    )
    own, second, up, down = call(
        kernel_primitives,
        [(4,) + block, (3,) + block, (4,) + sums, (4,) + sums],
        (conserved, first),
    )
    peer_first = lax.ppermute(first, "gy", to_peer)
    before = lax.ppermute(up, "gx", ring_up)
    after = lax.ppermute(down, "gx", ring_down)
    dy, mu, for_u, for_w, mate_b = call(
        kernel_pitch_gradients,
        [(4,) + block, block, block, block, (2,) + block],
        (own, y_high, y_low),
    )
    mate_u, mate_w = (lax.ppermute(value, "gy", to_mate) for value in (for_u, for_w))
    second_mate = lax.ppermute(mate_b, "gy", to_mate)
    peer_second = lax.ppermute(second, "gy", to_peer)
    dx, third, for_u, for_w = call(
        kernel_stream_gradients,
        [(4,) + block, (2,) + block, block, block],
        (own, before, after, mu, peer_first),
    )
    across_u, across_w = (lax.ppermute(value, "gy", to_mate) for value in (for_u, for_w))
    peer_third = lax.ppermute(third, "gy", to_peer)
    dz, flux, far, near = call(
        kernel_flux_x,
        [(2, points, 2 * width), (5,) + block, (5,) + sums, (5,) + sums],
        (
            own, second, peer_first, mate_u, mate_w, across_u, across_w, dx, dy, mu,
            z_high, z_low,
        ),
    )
    from_far = lax.ppermute(far, "gx", far_pairs)
    from_near = lax.ppermute(near, "gx", near_pairs)
    for_v, for_t, dy_peer = call(
        kernel_peer,
        [block, block, (2, points, width)],
        (peer_first, peer_second, flux, y_high, y_low),
    )
    across_v = lax.ppermute(for_v, "gy", to_mate)
    across_t = lax.ppermute(for_t, "gy", to_mate)
    part, part_mate = call(
        kernel_flux_yz,
        [(5,) + block, (5,) + block],
        (
            own, second, peer_first, peer_second, second_mate, across_v, across_t, dy_peer,
            dz, dx, dy, mu, y_high, y_low, z_high, z_low, f_high, f_low,
        ),
        scratch=(
            pltpu.VMEM((2, points, 2 * width), F32),
            pltpu.VMEM((5, points, 2 * width), F32),
            pltpu.VMEM((5, points, width), F32),
        ),
    )
    total, *for_mate = call(
        kernel_corrections,
        [(5,) + block] + 5 * [block],
        (own, peer_first, third, peer_third, part, part_mate, f_high, f_low),
    )
    from_mate = [lax.ppermute(value, "gy", to_mate) for value in for_mate]
    (total,) = call(
        kernel_add_stream, [(5,) + block], (total, flux, from_far, from_near)
    )
    tendency, advanced = call(
        kernel_finish,
        [(5,) + block, (5,) + block],
        (conserved, total, *from_mate),
        scratch=(
            pltpu.VMEM((5,) + block, F32),
            pltpu.VMEM((5,) + block, F32),
            pltpu.SemaphoreType.DMA((10,)),
        ),
        written=True,
    )
    return (
        jnp.transpose(tendency, (0, 1, 3, 2)),
        jnp.transpose(advanced, (0, 1, 3, 2)),
    )


def padded(array, sides, width):
    for axis, dim in sides:
        devices, length = (lax.axis_size(axis), array.shape[dim])
        up = [(i, (i + 1) % devices) for i in range(devices)]
        down = [(j, i) for i, j in up]
        last = lax.slice_in_dim(array, length - width, length, axis=dim)
        initial = lax.slice_in_dim(array, 0, width, axis=dim)
        before = lax.ppermute(last, axis, up)
        after = lax.ppermute(initial, axis, down)
        array = jnp.concatenate([before, array, after], axis=dim)
    return array


def right_side(conserved, gradients_of, derive_x, derive_y, derive_z):
    mass_per_volume = conserved[0]
    momentum = conserved[1:4]
    energy = conserved[4]
    local_speed_vector = momentum / mass_per_volume
    kinetic = 0.5 * jnp.sum(momentum * local_speed_vector, axis=0)
    normal_force_per_area = (heat_ratio - 1.0) * (energy - kinetic)
    thermal_state = normal_force_per_area / mass_per_volume
    basic_quantities = jnp.concatenate([local_speed_vector, thermal_state[None]], 0)
    gradients = gradients_of(basic_quantities)
    shear_resistance = shear_resistance_reference * jnp.power(thermal_state, sutherland_power_law)
    conductivity = shear_resistance * heat_ratio / ((heat_ratio - 1.0) * prandtl)
    dilatation = gradients[0][0] + gradients[1][1] + gradients[2][2]
    derivers = (derive_x, derive_y, derive_z)
    accumulated = None
    for direction in range(3):
        stress_column = [
            shear_resistance * (gradients[direction][component] + gradients[component][direction])
            for component in range(3)
        ]
        stress_column[direction] = (
            stress_column[direction] - 2.0 / 3.0 * shear_resistance * dilatation
        )
        fluxes = [momentum[direction]]
        for component in range(3):
            moment_flux = (
                momentum[component] * local_speed_vector[direction] - stress_column[component]
            )
            if component == direction:
                moment_flux = moment_flux + normal_force_per_area
            fluxes.append(moment_flux)
        work_term = (
            stress_column[0] * local_speed_vector[0]
            + stress_column[1] * local_speed_vector[1]
            + stress_column[2] * local_speed_vector[2]
        )
        fluxes.append(
            (energy + normal_force_per_area) * local_speed_vector[direction]
            - work_term
            - conductivity * gradients[direction][3]
        )
        divergence_part = derivers[direction](jnp.stack(fluxes))
        accumulated = divergence_part if accumulated is None else accumulated + divergence_part
    return -accumulated


def plain_device(mass_per_volume, momentum, energy):
    conserved = jnp.concatenate([mass_per_volume[None], momentum, energy[None]], 0)
    highest = lax.Precision.HIGHEST
    x_matrix = jnp.asarray(compact_matrix(CX, HALO))
    z_matrix = jnp.asarray(span_matrix(NZ))

    def apply_x(extended):
        return jnp.einsum("il,flab->fiab", x_matrix, extended, precision=highest)

    def flux_x(values):
        return apply_x(padded(values, (("gx", 1),), HALO))

    y_matrix = jnp.asarray(pitch_matrix(conserved.shape[3], CY))

    def apply_y(values):
        return jnp.einsum("fabk,jk->fabj", values, y_matrix, precision=highest)

    def derive_span(values):
        lines = jnp.transpose(
            lax.all_to_all(values, "gy", split_axis=3, concat_axis=2, tiled=True), (0, 1, 3, 2)
        )
        derived = jnp.einsum("fack,jk->facj", lines, z_matrix, precision=highest)
        returned = lax.all_to_all(derived, "gy", split_axis=3, concat_axis=2, tiled=True)
        return jnp.transpose(returned, (0, 1, 3, 2))

    def gradients_of(basic_quantities):
        extended = padded(basic_quantities, (("gx", 1),), HALO)
        return (apply_x(extended), apply_y(basic_quantities), derive_span(basic_quantities))

    tendency = right_side(conserved, gradients_of, flux_x, apply_y, derive_span)
    advanced = conserved + section_step * tendency
    return (tendency, advanced)


def per_device(mass_per_volume, momentum, energy):
    planes, width, rows = mass_per_volume.shape
    fits = planes == CX and width % 128 == 0 and rows <= 32 and rows % CY == 0
    if fits and lax.axis_size("gy") == 4 and lax.axis_size("gx") % 2 == 0:
        return fast_device(mass_per_volume, momentum, energy)
    return plain_device(mass_per_volume, momentum, energy)


def solution(mesh):
    in_specs = (P("gx", "gy", None), P(None, "gx", "gy", None), P("gx", "gy", None))
    out_specs = (P(None, "gx", "gy", None), P(None, "gx", "gy", None))
    return jax.shard_map(
        per_device, mesh=mesh, in_specs=in_specs, out_specs=out_specs, check_vma=False
    )
```

```python
import functools

import jax
import jax.numpy as jnp
import numpy as np
from jax import lax
from jax.experimental import pallas as pl
from jax.experimental.pallas import tpu as pltpu
from jax.sharding import PartitionSpec as P

CX = 8
CY = 8
NZ = 512
HALO = 4


heat_ratio = 1.4
shear_resistance_reference = 0.08
sutherland_power_law = 0.7
prandtl = 0.72
section_step = 0.05
compact_alpha = 1.0 / 3.0
compact_near = 14.0 / 9.0
compact_far = 1.0 / 9.0

conduction = heat_ratio / ((heat_ratio - 1.0) * prandtl)
enthalpy = heat_ratio / (heat_ratio - 1.0)


def tridiagonal_inverse_product(length, stencil):
    solved = np.array(stencil)
    upper_ratio = np.zeros(length)
    for row_index in range(length):
        if row_index == 0:
            pivot_value = 1.0
            solved[row_index] = solved[row_index] / pivot_value
        else:
            pivot_value = 1.0 - compact_alpha * upper_ratio[row_index - 1]
            solved[row_index] = (
                solved[row_index] - compact_alpha * solved[row_index - 1]
            ) / pivot_value
        upper_ratio[row_index] = compact_alpha / pivot_value
    for row_index in range(length - 2, -1, -1):
        solved[row_index] = solved[row_index] - upper_ratio[row_index] * solved[row_index + 1]
    return solved


def exact_compact_matrix(block_size, margin):
    length = block_size + 2 * margin
    stencil = compact_near / 2.0 * (np.eye(length, k=1) - np.eye(length, k=-1))
    stencil = stencil + compact_far / 4.0 * (np.eye(length, k=2) - np.eye(length, k=-2))
    inverse_product = tridiagonal_inverse_product(length, stencil)
    return inverse_product[margin : margin + block_size]


def compact_matrix(block_size, margin):
    return exact_compact_matrix(block_size, margin).astype(np.float32)


def pitch_matrix(total, block_size):
    matrix = compact_matrix(block_size, HALO)
    result = np.zeros((total, total), np.float32)
    rows_all = np.arange(total)
    block_start = rows_all // block_size * block_size
    for offset in range(block_size + 2 * HALO):
        columns = (block_start - HALO + offset) % total
        result[rows_all, columns] += matrix[rows_all % block_size, offset]
    return result


def span_matrix(total):
    offsets = np.arange(total)[:, None] - np.arange(total)[None, :]
    angles = np.pi * offsets / total
    signs = np.where(offsets % 2 == 0, 1.0, -1.0)
    sines = np.where(offsets == 0, 1.0, np.sin(angles))
    result = np.where(offsets == 0, 0.0, np.pi / total * signs * np.cos(angles) / sines)
    return result.astype(np.float32)


F32 = jnp.float32
BF16 = jnp.bfloat16
U, W, V, T, R = range(5)
PLACES = (0, 2, 1, 3)
HALF = CX // 2


def halves(matrix):
    high = np.asarray(matrix, np.float32).astype(BF16)
    low = (matrix - high.astype(np.float32)).astype(BF16)
    return jnp.asarray(high), jnp.asarray(low)


def span_blocks(length, sources, targets):
    width = length // 4
    matrix = span_matrix(length).T
    both = []
    for core in range(2):
        columns = []
        for target in targets:
            to = core ^ target
            columns.append(
                np.concatenate(
                    [
                        matrix[
                            (core ^ source) * width : (core ^ source) * width + width,
                            to * width : to * width + width,
                        ]
                        for source in sources
                    ],
                    axis=0,
                )
            )
        both.append(np.concatenate(columns, axis=1))
    return halves(np.stack(both))


def halo_basis():
    matrix = exact_compact_matrix(CX, HALO)
    left = matrix[:, :HALO]
    basis = np.linalg.svd(left)[2][:2]
    inner = left @ basis.T
    outer = -inner[::-1]
    return basis, np.concatenate(
        [inner, matrix[:, HALO : HALO + CX], outer[:, ::-1]], axis=1
    )


def split(values):
    high = values.astype(BF16)
    low = (values - high.astype(F32)).astype(BF16)
    return high, low


def dot(a, b):
    return jnp.dot(a, b, preferred_element_type=F32)


def right_product(values, matrix_high, matrix_low):
    high, low = split(values)
    return dot(high, matrix_high) + dot(low, matrix_high) + dot(high, matrix_low)


def left_product(matrix_high, matrix_low, values):
    high, low = split(values)
    return dot(matrix_high, high) + dot(matrix_high, low) + dot(matrix_low, high)


def compact_x(planes):
    matrix = halo_basis()[1]
    length = CX + 4
    half = length // 2
    odd = [planes[l] - planes[length - 1 - l] for l in range(half)]
    even = [planes[l] + planes[length - 1 - l] for l in range(half)]
    result = [None] * CX
    for i in range(HALF):
        first = None
        second = None
        for l in range(half):
            a = float(0.5 * (matrix[i, l] - matrix[i, length - 1 - l]))
            b = float(0.5 * (matrix[i, l] + matrix[i, length - 1 - l]))
            first = a * odd[l] if first is None else first + a * odd[l]
            second = b * even[l] if second is None else second + b * even[l]
        result[i] = first + second
        result[CX - 1 - i] = first - second
    return result


def extended(before, own, after, f, rows):
    return (
        [before[f, 0, rows, :], before[f, 1, rows, :]]
        + [own[f, l, rows, :] for l in range(CX)]
        + [after[f, 1, rows, :], after[f, 0, rows, :]]
    )


def halo_sums(values, f, rows, up, down):
    basis = halo_basis()[0]
    for k in range(2):
        top = None
        bottom = None
        for l in range(HALO):
            a = float(basis[k, l]) * values[f, CX - HALO + l, rows, :]
            b = float(basis[k, l]) * values[f, HALO - 1 - l, rows, :]
            top = a if top is None else top + a
            bottom = b if bottom is None else bottom + b
        up[f, k, rows, :] = top
        down[f, k, rows, :] = bottom


def row_chunks(rows):
    return [slice(start, start + 8) for start in range(0, rows, 8)]


def flat(values):
    return values.reshape(-1, values.shape[-1])


def kernel_inputs(rho_in, mom_in, ene_in, conserved, first, arrived):
    copies = [
        pltpu.make_async_copy(source, conserved.at[part], arrived.at[k])
        for k, (source, part) in enumerate(
            ((rho_in, 0), (mom_in, slice(1, 4)), (ene_in, 4))
        )
    ]
    for copy in copies:
        copy.start()
    for copy in copies:
        copy.wait()

    def plane(x, carry):
        inverse = 1.0 / conserved[0, x]
        first[0, x] = conserved[1, x] * inverse
        first[1, x] = conserved[3, x] * inverse
        return carry

    lax.fori_loop(0, CX, plane, 0, unroll=2)


def kernel_primitives(conserved, first, own, second, up, down):
    def plane(x, carry):
        density = conserved[0, x]
        inverse = 1.0 / density
        u = first[0, x]
        w = first[1, x]
        v = conserved[2, x] * inverse
        kinetic = 0.5 * (conserved[1, x] * u + conserved[2, x] * v + conserved[3, x] * w)
        temperature = (heat_ratio - 1.0) * (conserved[4, x] - kinetic) * inverse
        own[U, x] = u
        own[W, x] = w
        own[V, x] = v
        own[T, x] = temperature
        second[0, x] = v
        second[1, x] = temperature
        second[2, x] = density
        return carry

    lax.fori_loop(0, CX, plane, 0, unroll=2)

    def sums(f, carry):
        for rows in row_chunks(own.shape[2]):
            halo_sums(own, f, rows, up, down)
        return carry

    lax.fori_loop(0, 4, sums, 0)


def kernel_pitch_gradients(
    own, y_high, y_low, dy, mu, mate_u, mate_w, mate_b
):
    for f in range(4):
        dy[f] = left_product(y_high[...], y_low[...], flat(own[f])).reshape(own.shape[1:])

    def plane(x, carry):
        mu[x] = shear_resistance_reference * jnp.exp(
            sutherland_power_law * jnp.log(own[T, x])
        )
        mate_u[x] = own[U, x]
        mate_w[x] = own[W, x]
        for f in range(2):
            mate_b[f, x] = own[V + f, x]
        return carry

    lax.fori_loop(0, CX, plane, 0)


def kernel_stream_gradients(own, before, after, mu, peer_first, dx, third, for_u, for_w):
    for_u[...] = peer_first[0]
    for_w[...] = peer_first[1]

    def field(f, carry):
        for rows in row_chunks(own.shape[2]):
            derived = compact_x(extended(before, own, after, f, rows))
            for x in range(CX):
                dx[f, x, rows, :] = derived[x]
        return carry

    lax.fori_loop(0, 4, field, 0)

    def plane(x, carry):
        third[0, x] = (2.0 / 3.0) * mu[x] * dx[U, x]
        third[1, x] = mu[x] * dx[W, x]
        return carry

    lax.fori_loop(0, CX, plane, 0)


def kernel_flux_x(
    own, second, peer_first, mate_u, mate_w, across_u, across_w, dx, dy, mu,
    z_high, z_low, dz, flux, up, down,
):
    width = own.shape[-1]
    odd = lax.rem(lax.axis_index("gy"), 2)
    for f, (mate, across) in enumerate(((mate_u, across_u), (mate_w, across_w))):
        values = jnp.concatenate(
            [flat(own[f]), flat(peer_first[f]), flat(mate[...]), flat(across[...])], axis=1
        )
        dz[f] = right_product(values, z_high[odd], z_low[odd])

    rows = own.shape[2]

    def plane(x, carry):
        at = pl.ds(pl.multiple_of(x * rows, rows), rows)
        u, w, v, t = (own[f, x] for f in range(4))
        density = second[2, x]
        viscosity = mu[x]
        dil = dx[U, x] + dy[V, x] + dz[1, at, :width]
        s1 = viscosity * (2.0 * dx[U, x] - (2.0 / 3.0) * dil)
        s2 = viscosity * (dx[V, x] + dy[U, x])
        s3 = viscosity * (dx[W, x] + dz[0, at, :width])
        m = density * u
        total = m * (enthalpy * t + 0.5 * (u * u + v * v + w * w))
        flux[0, x] = m
        flux[1, x] = m * u + density * t - s1
        flux[2, x] = m * v - s2
        flux[3, x] = m * w - s3
        flux[4, x] = total - (s1 * u + s2 * v + s3 * w) - conduction * viscosity * dx[T, x]
        return carry

    lax.fori_loop(0, CX, plane, 0)

    def sums(f, carry):
        for chunk in row_chunks(rows):
            halo_sums(flux, f, chunk, up, down)
        return carry

    lax.fori_loop(0, 5, sums, 0)


def kernel_peer(peer_second, flux, for_v, for_t):
    for_v[...] = peer_second[0]
    for_t[...] = peer_second[1]


def kernel_flux_yz_early(
    own, second, peer_first, peer_second, for_v, dz, dx, dy, mu, y_high, y_low, f_high, f_low,
    spread, local, dy_peer, mu_peer, flux, flux_y,
):
    rows, width = own.shape[2:]
    odd = lax.rem(lax.axis_index("gy"), 2)
    dy_peer[0] = left_product(y_high[...], y_low[...], flat(peer_second[0]))
    dy_peer[1] = left_product(y_high[...], y_low[...], flat(peer_first[1]))

    def plane(x, carry):
        at = pl.ds(pl.multiple_of(x * rows, rows), rows)
        here = slice(0, width)
        there = slice(width, 2 * width)

        def span(lanes, u, w, t, density, viscosity, yv):
            m = density * w
            flux[0, at, lanes] = m
            flux[1, at, lanes] = m * u - viscosity * dz[0, at, lanes]
            flux[2, at, lanes] = (
                m * w
                + density * t
                - viscosity * ((4.0 / 3.0) * dz[1, at, lanes] - (2.0 / 3.0) * yv)
            )

        u, w, v, t = (own[f, x] for f in range(4))
        density = second[2, x]
        viscosity = mu[x]
        span(here, u, w, t, density, viscosity, dy[V, x])
        dil = dx[U, x] + dy[V, x] + dz[1, at, here]
        m = density * v
        flux_y[0, at, :] = m
        flux_y[1, at, :] = m * u - viscosity * (dy[U, x] + dx[V, x])
        flux_y[2, at, :] = (
            m * v + density * t - viscosity * (2.0 * dy[V, x] - (2.0 / 3.0) * dil)
        )
        t = peer_second[1, x]
        viscosity = shear_resistance_reference * jnp.exp(sutherland_power_law * jnp.log(t))
        mu_peer[at, :] = viscosity
        span(
            there, peer_first[0, x], peer_first[1, x], t, peer_second[2, x], viscosity,
            dy_peer[0, at, :],
        )
        return carry

    lax.fori_loop(0, CX, plane, 0)
    for k in range(3):
        spread[k] = right_product(flux[k], f_high[odd], f_low[odd])
        local[k] = left_product(y_high[...], y_low[...], flux_y[k])


def kernel_flux_yz(
    own, second, peer_first, peer_second, second_mate, across_v, across_t, dy_peer, mu_peer,
    spread_early, local_early, dz, dx, dy, mu, y_high, y_low, z_high, z_low, f_high, f_low,
    part, part_mate, dz_more, flux, flux_y,
):
    rows, width = own.shape[2:]
    odd = lax.rem(lax.axis_index("gy"), 2)
    for f, across in enumerate((across_v, across_t)):
        values = jnp.concatenate(
            [flat(own[V + f]), flat(peer_second[f]), flat(second_mate[f]), flat(across[...])],
            axis=1,
        )
        dz_more[f] = right_product(values, z_high[odd], z_low[odd])

    def plane(x, carry):
        at = pl.ds(pl.multiple_of(x * rows, rows), rows)
        here = slice(0, width)
        there = slice(width, 2 * width)

        def span(lanes, u, w, v, t, density, viscosity, yv, yw):
            s1 = viscosity * dz[0, at, lanes]
            s2 = viscosity * (dz_more[0, at, lanes] + yw)
            s3 = viscosity * ((4.0 / 3.0) * dz[1, at, lanes] - (2.0 / 3.0) * yv)
            energy = density * (enthalpy * t + 0.5 * (u * u + v * v + w * w))
            flux[0, at, lanes] = density * w * v - s2
            flux[1, at, lanes] = (
                energy * w
                - (s1 * u + s2 * v + s3 * w)
                - conduction * viscosity * dz_more[1, at, lanes]
            )
            return energy

        u, w, v, t = (own[f, x] for f in range(4))
        density = second[2, x]
        viscosity = mu[x]
        energy = span(here, u, w, v, t, density, viscosity, dy[V, x], dy[W, x])
        dil = dx[U, x] + dy[V, x] + dz[1, at, here]
        s1 = viscosity * (dy[U, x] + dx[V, x])
        s2 = viscosity * (2.0 * dy[V, x] - (2.0 / 3.0) * dil)
        s3 = viscosity * (dy[W, x] + dz_more[0, at, here])
        flux_y[0, at, :] = density * v * w - s3
        flux_y[1, at, :] = (
            energy * v - (s1 * u + s2 * v + s3 * w) - conduction * viscosity * dy[T, x]
        )
        span(
            there, peer_first[0, x], peer_first[1, x], peer_second[0, x], peer_second[1, x],
            peer_second[2, x], mu_peer[at, :], dy_peer[0, at, :], dy_peer[1, at, :],
        )
        return carry

    lax.fori_loop(0, CX, plane, 0)
    shape = own.shape[1:]
    spreads = {0: spread_early[0], 1: spread_early[1], 3: spread_early[2]}
    locals_y = {0: local_early[0], 1: local_early[1], 2: local_early[2]}
    for k in range(2):
        spreads[2 + 2 * k] = right_product(flux[k], f_high[odd], f_low[odd])
        locals_y[3 + k] = left_product(y_high[...], y_low[...], flux_y[k])
    for f in range(5):
        part[f] = (spreads[f][:, :width] + locals_y[f]).reshape(shape)
        part_mate[f] = spreads[f][:, width:].reshape(shape)


def kernel_corrections(
    own, peer_first, third, peer_third, part, part_mate, f_high, f_low, total, *for_mate
):
    width = own.shape[-1]
    odd = lax.rem(lax.axis_index("gy"), 2)
    shape = own.shape[1:]
    for f in (0, 2):
        total[f] = part[f]
        for_mate[f][...] = part_mate[f]
    pairs = ((own, third), (peer_first, peer_third))
    for f in (1, 3, 4):
        sides = []
        for speeds, shared in pairs:
            if f == 1:
                value = -shared[1]
            elif f == 3:
                value = shared[0]
            else:
                value = shared[0] * speeds[W] - shared[1] * speeds[U]
            sides.append(flat(value))
        spread = right_product(jnp.concatenate(sides, axis=1), f_high[odd], f_low[odd])
        total[f] = part[f] + spread[:, :width].reshape(shape)
        for_mate[f][...] = part_mate[f] + spread[:, width:].reshape(shape)


def kernel_add_stream(total, flux, before, after, result):
    def field(f, carry):
        for rows in row_chunks(flux.shape[2]):
            derived = compact_x(extended(before, flux, after, f, rows))
            for x in range(CX):
                result[f, x, rows, :] = total[f, x, rows, :] + derived[x]
        return carry

    lax.fori_loop(0, 5, field, 0)


def kernel_finish(
    conserved, total, mate_0, mate_1, mate_2, mate_3, mate_4, tendency, advanced,
    rate, state, sent,
):
    copies = []
    for f, from_mate in enumerate((mate_0, mate_1, mate_2, mate_3, mate_4)):
        value = -(total[f] + from_mate[...])
        rate[f] = value
        state[f] = conserved[f] + section_step * value
        for k, (source, target) in enumerate(((rate, tendency), (state, advanced))):
            copy = pltpu.make_async_copy(source.at[f], target.at[f], sent.at[2 * f + k])
            copy.start()
            copies.append(copy)
    for copy in copies:
        copy.wait()


def call(kernel, outputs, operands, scratch=(), outside=False, written=False):
    space = pltpu.HBM if outside else pltpu.VMEM
    target = pltpu.HBM if written else pltpu.VMEM
    in_specs = [pl.BlockSpec(memory_space=space) for _ in operands]
    if outside:
        operands = [pltpu.with_memory_space_constraint(value, pltpu.HBM) for value in operands]
    touched = sum(value.size * value.dtype.itemsize for value in operands)
    touched += 4 * sum(int(np.prod(shape)) for shape in outputs)
    return pl.pallas_call(
        kernel,
        out_shape=[jax.ShapeDtypeStruct(shape, F32) for shape in outputs],
        in_specs=in_specs,
        out_specs=[pl.BlockSpec(memory_space=target) for _ in outputs],
        scratch_shapes=list(scratch),
        cost_estimate=pl.CostEstimate(flops=0, bytes_accessed=touched, transcendentals=0),
        compiler_params=pltpu.CompilerParams(vmem_limit_bytes=24 * 1024 * 1024),
    )(*operands)


def fast_device(mass_per_volume, momentum, energy):
    rho = jnp.transpose(mass_per_volume, (0, 2, 1))
    mom = jnp.transpose(momentum, (0, 1, 3, 2))
    ene = jnp.transpose(energy, (0, 2, 1))
    _, rows, width = rho.shape
    length = 4 * width
    z_high, z_low = span_blocks(length, PLACES, PLACES[:2])
    f_high, f_low = span_blocks(length, PLACES[:2], (0, 1))
    y_high, y_low = halves(np.kron(np.eye(CX, dtype=np.float32), pitch_matrix(rows, CY)))
    block = (CX, rows, width)
    sums = (2, rows, width)
    points = CX * rows
    devices = lax.axis_size("gx")
    ring_up = [(i, (i + 1) % devices) for i in range(devices)]
    ring_down = [(j, i) for i, j in ring_up]
    to_mate = [(i, i ^ 1) for i in range(4)]
    to_peer = [(i, i ^ 2) for i in range(4)]

    conserved, first = call(
        kernel_inputs,
        [(5,) + block, (2,) + block],
        (rho, mom, ene),
        scratch=(pltpu.SemaphoreType.DMA((3,)),),
        outside=True,
    )
    own, second, up, down = call(
        kernel_primitives,
        [(4,) + block, (3,) + block, (4,) + sums, (4,) + sums],
        (conserved, first),
    )
    peer_first = lax.ppermute(first, "gy", to_peer)
    before = lax.ppermute(up, "gx", ring_up)
    after = lax.ppermute(down, "gx", ring_down)
    dy, mu, for_u, for_w, mate_b = call(
        kernel_pitch_gradients,
        [(4,) + block, block, block, block, (2,) + block],
        (own, y_high, y_low),
    )
    mate_u, mate_w = (lax.ppermute(value, "gy", to_mate) for value in (for_u, for_w))
    second_mate = lax.ppermute(mate_b, "gy", to_mate)
    peer_second = lax.ppermute(second, "gy", to_peer)
    dx, third, for_u, for_w = call(
        kernel_stream_gradients,
        [(4,) + block, (2,) + block, block, block],
        (own, before, after, mu, peer_first),
    )
    across_u, across_w = (lax.ppermute(value, "gy", to_mate) for value in (for_u, for_w))
    peer_third = lax.ppermute(third, "gy", to_peer)
    dz, flux, flux_up, flux_down = call(
        kernel_flux_x,
        [(2, points, 2 * width), (5,) + block, (5,) + sums, (5,) + sums],
        (
            own, second, peer_first, mate_u, mate_w, across_u, across_w, dx, dy, mu,
            z_high, z_low,
        ),
    )
    flux_before = lax.ppermute(flux_up, "gx", ring_up)
    flux_after = lax.ppermute(flux_down, "gx", ring_down)
    for_v, for_t = call(kernel_peer, [block, block], (peer_second, flux))
    across_v = lax.ppermute(for_v, "gy", to_mate)
    across_t = lax.ppermute(for_t, "gy", to_mate)
    spread, local, dy_peer, mu_peer = call(
        kernel_flux_yz_early,
        [(3, points, 2 * width), (3, points, width), (2, points, width), (points, width)],
        (
            own, second, peer_first, peer_second, for_v, dz, dx, dy, mu,
            y_high, y_low, f_high, f_low,
        ),
        scratch=(
            pltpu.VMEM((3, points, 2 * width), F32),
            pltpu.VMEM((3, points, width), F32),
        ),
    )
    part, part_mate = call(
        kernel_flux_yz,
        [(5,) + block, (5,) + block],
        (
            own, second, peer_first, peer_second, second_mate, across_v, across_t,
            dy_peer, mu_peer, spread, local, dz, dx, dy, mu,
            y_high, y_low, z_high, z_low, f_high, f_low,
        ),
        scratch=(
            pltpu.VMEM((2, points, 2 * width), F32),
            pltpu.VMEM((2, points, 2 * width), F32),
            pltpu.VMEM((2, points, width), F32),
        ),
    )
    total, *for_mate = call(
        kernel_corrections,
        [(5,) + block] + 5 * [block],
        (own, peer_first, third, peer_third, part, part_mate, f_high, f_low),
    )
    from_mate = [lax.ppermute(value, "gy", to_mate) for value in for_mate]
    (total,) = call(
        kernel_add_stream, [(5,) + block], (total, flux, flux_before, flux_after)
    )
    tendency, advanced = call(
        kernel_finish,
        [(5,) + block, (5,) + block],
        (conserved, total, *from_mate),
        scratch=(
            pltpu.VMEM((5,) + block, F32),
            pltpu.VMEM((5,) + block, F32),
            pltpu.SemaphoreType.DMA((10,)),
        ),
        written=True,
    )
    return (
        jnp.transpose(tendency, (0, 1, 3, 2)),
        jnp.transpose(advanced, (0, 1, 3, 2)),
    )


def padded(array, sides, width):
    for axis, dim in sides:
        devices, length = (lax.axis_size(axis), array.shape[dim])
        up = [(i, (i + 1) % devices) for i in range(devices)]
        down = [(j, i) for i, j in up]
        last = lax.slice_in_dim(array, length - width, length, axis=dim)
        initial = lax.slice_in_dim(array, 0, width, axis=dim)
        before = lax.ppermute(last, axis, up)
        after = lax.ppermute(initial, axis, down)
        array = jnp.concatenate([before, array, after], axis=dim)
    return array


def right_side(conserved, gradients_of, derive_x, derive_y, derive_z):
    mass_per_volume = conserved[0]
    momentum = conserved[1:4]
    energy = conserved[4]
    local_speed_vector = momentum / mass_per_volume
    kinetic = 0.5 * jnp.sum(momentum * local_speed_vector, axis=0)
    normal_force_per_area = (heat_ratio - 1.0) * (energy - kinetic)
    thermal_state = normal_force_per_area / mass_per_volume
    basic_quantities = jnp.concatenate([local_speed_vector, thermal_state[None]], 0)
    gradients = gradients_of(basic_quantities)
    shear_resistance = shear_resistance_reference * jnp.power(thermal_state, sutherland_power_law)
    conductivity = shear_resistance * heat_ratio / ((heat_ratio - 1.0) * prandtl)
    dilatation = gradients[0][0] + gradients[1][1] + gradients[2][2]
    derivers = (derive_x, derive_y, derive_z)
    accumulated = None
    for direction in range(3):
        stress_column = [
            shear_resistance * (gradients[direction][component] + gradients[component][direction])
            for component in range(3)
        ]
        stress_column[direction] = (
            stress_column[direction] - 2.0 / 3.0 * shear_resistance * dilatation
        )
        fluxes = [momentum[direction]]
        for component in range(3):
            moment_flux = (
                momentum[component] * local_speed_vector[direction] - stress_column[component]
            )
            if component == direction:
                moment_flux = moment_flux + normal_force_per_area
            fluxes.append(moment_flux)
        work_term = (
            stress_column[0] * local_speed_vector[0]
            + stress_column[1] * local_speed_vector[1]
            + stress_column[2] * local_speed_vector[2]
        )
        fluxes.append(
            (energy + normal_force_per_area) * local_speed_vector[direction]
            - work_term
            - conductivity * gradients[direction][3]
        )
        divergence_part = derivers[direction](jnp.stack(fluxes))
        accumulated = divergence_part if accumulated is None else accumulated + divergence_part
    return -accumulated


def plain_device(mass_per_volume, momentum, energy):
    conserved = jnp.concatenate([mass_per_volume[None], momentum, energy[None]], 0)
    highest = lax.Precision.HIGHEST
    x_matrix = jnp.asarray(compact_matrix(CX, HALO))
    z_matrix = jnp.asarray(span_matrix(NZ))

    def apply_x(extended):
        return jnp.einsum("il,flab->fiab", x_matrix, extended, precision=highest)

    def flux_x(values):
        return apply_x(padded(values, (("gx", 1),), HALO))

    y_matrix = jnp.asarray(pitch_matrix(conserved.shape[3], CY))

    def apply_y(values):
        return jnp.einsum("fabk,jk->fabj", values, y_matrix, precision=highest)

    def derive_span(values):
        lines = jnp.transpose(
            lax.all_to_all(values, "gy", split_axis=3, concat_axis=2, tiled=True), (0, 1, 3, 2)
        )
        derived = jnp.einsum("fack,jk->facj", lines, z_matrix, precision=highest)
        returned = lax.all_to_all(derived, "gy", split_axis=3, concat_axis=2, tiled=True)
        return jnp.transpose(returned, (0, 1, 3, 2))

    def gradients_of(basic_quantities):
        extended = padded(basic_quantities, (("gx", 1),), HALO)
        return (apply_x(extended), apply_y(basic_quantities), derive_span(basic_quantities))

    tendency = right_side(conserved, gradients_of, flux_x, apply_y, derive_span)
    advanced = conserved + section_step * tendency
    return (tendency, advanced)


def per_device(mass_per_volume, momentum, energy):
    planes, width, rows = mass_per_volume.shape
    fits = planes == CX and width % 128 == 0 and rows <= 32 and rows % CY == 0
    if fits and lax.axis_size("gy") == 4 and lax.axis_size("gx") % 2 == 0:
        return fast_device(mass_per_volume, momentum, energy)
    return plain_device(mass_per_volume, momentum, energy)


def solution(mesh):
    in_specs = (P("gx", "gy", None), P(None, "gx", "gy", None), P("gx", "gy", None))
    out_specs = (P(None, "gx", "gy", None), P(None, "gx", "gy", None))
    return jax.shard_map(
        per_device, mesh=mesh, in_specs=in_specs, out_specs=out_specs, check_vma=False
    )
```

```python
import functools

import jax
import jax.numpy as jnp
import numpy as np
from jax import lax
from jax.experimental import pallas as pl
from jax.experimental.pallas import tpu as pltpu
from jax.sharding import PartitionSpec as P

CX = 8
CY = 8
NZ = 512
HALO = 4


heat_ratio = 1.4
shear_resistance_reference = 0.08
sutherland_power_law = 0.7
prandtl = 0.72
section_step = 0.05
compact_alpha = 1.0 / 3.0
compact_near = 14.0 / 9.0
compact_far = 1.0 / 9.0

conduction = heat_ratio / ((heat_ratio - 1.0) * prandtl)
enthalpy = heat_ratio / (heat_ratio - 1.0)


def tridiagonal_inverse_product(length, stencil):
    solved = np.array(stencil)
    upper_ratio = np.zeros(length)
    for row_index in range(length):
        if row_index == 0:
            pivot_value = 1.0
            solved[row_index] = solved[row_index] / pivot_value
        else:
            pivot_value = 1.0 - compact_alpha * upper_ratio[row_index - 1]
            solved[row_index] = (
                solved[row_index] - compact_alpha * solved[row_index - 1]
            ) / pivot_value
        upper_ratio[row_index] = compact_alpha / pivot_value
    for row_index in range(length - 2, -1, -1):
        solved[row_index] = solved[row_index] - upper_ratio[row_index] * solved[row_index + 1]
    return solved


def exact_compact_matrix(block_size, margin):
    length = block_size + 2 * margin
    stencil = compact_near / 2.0 * (np.eye(length, k=1) - np.eye(length, k=-1))
    stencil = stencil + compact_far / 4.0 * (np.eye(length, k=2) - np.eye(length, k=-2))
    inverse_product = tridiagonal_inverse_product(length, stencil)
    return inverse_product[margin : margin + block_size]


def compact_matrix(block_size, margin):
    return exact_compact_matrix(block_size, margin).astype(np.float32)


def pitch_matrix(total, block_size):
    matrix = compact_matrix(block_size, HALO)
    result = np.zeros((total, total), np.float32)
    rows_all = np.arange(total)
    block_start = rows_all // block_size * block_size
    for offset in range(block_size + 2 * HALO):
        columns = (block_start - HALO + offset) % total
        result[rows_all, columns] += matrix[rows_all % block_size, offset]
    return result


def span_matrix(total):
    offsets = np.arange(total)[:, None] - np.arange(total)[None, :]
    angles = np.pi * offsets / total
    signs = np.where(offsets % 2 == 0, 1.0, -1.0)
    sines = np.where(offsets == 0, 1.0, np.sin(angles))
    result = np.where(offsets == 0, 0.0, np.pi / total * signs * np.cos(angles) / sines)
    return result.astype(np.float32)


F32 = jnp.float32
BF16 = jnp.bfloat16
U, W, V, T, R = range(5)
PLACES = (0, 2, 1, 3)
HALF = CX // 2


def halves(matrix):
    high = np.asarray(matrix, np.float32).astype(BF16)
    low = (matrix - high.astype(np.float32)).astype(BF16)
    return jnp.asarray(high), jnp.asarray(low)


def span_blocks(length, sources, targets):
    width = length // 4
    matrix = span_matrix(length).T
    both = []
    for core in range(2):
        columns = []
        for target in targets:
            to = core ^ target
            columns.append(
                np.concatenate(
                    [
                        matrix[
                            (core ^ source) * width : (core ^ source) * width + width,
                            to * width : to * width + width,
                        ]
                        for source in sources
                    ],
                    axis=0,
                )
            )
        both.append(np.concatenate(columns, axis=1))
    return halves(np.stack(both))


def halo_basis():
    matrix = exact_compact_matrix(CX, HALO)
    left = matrix[:, :HALO]
    basis = np.linalg.svd(left)[2][:2]
    inner = left @ basis.T
    outer = -inner[::-1]
    return basis, np.concatenate(
        [inner, matrix[:, HALO : HALO + CX], outer[:, ::-1]], axis=1
    )


def split(values):
    high = values.astype(BF16)
    low = (values - high.astype(F32)).astype(BF16)
    return high, low


def dot(a, b):
    return jnp.dot(a, b, preferred_element_type=F32)


def right_product(values, matrix_high, matrix_low):
    high, low = split(values)
    return dot(high, matrix_high) + dot(low, matrix_high) + dot(high, matrix_low)


def left_product(matrix_high, matrix_low, values):
    high, low = split(values)
    return dot(matrix_high, high) + dot(matrix_high, low) + dot(matrix_low, high)


def compact_x(planes):
    matrix = halo_basis()[1]
    length = CX + 4
    half = length // 2
    odd = [planes[l] - planes[length - 1 - l] for l in range(half)]
    even = [planes[l] + planes[length - 1 - l] for l in range(half)]
    result = [None] * CX
    for i in range(HALF):
        first = None
        second = None
        for l in range(half):
            a = float(0.5 * (matrix[i, l] - matrix[i, length - 1 - l]))
            b = float(0.5 * (matrix[i, l] + matrix[i, length - 1 - l]))
            first = a * odd[l] if first is None else first + a * odd[l]
            second = b * even[l] if second is None else second + b * even[l]
        result[i] = first + second
        result[CX - 1 - i] = first - second
    return result


def extended(before, own, after, f, rows):
    return (
        [before[f, 0, rows, :], before[f, 1, rows, :]]
        + [own[f, l, rows, :] for l in range(CX)]
        + [after[f, 1, rows, :], after[f, 0, rows, :]]
    )


def halo_sums(values, f, rows, up, down):
    basis = halo_basis()[0]
    for k in range(2):
        top = None
        bottom = None
        for l in range(HALO):
            a = float(basis[k, l]) * values[f, CX - HALO + l, rows, :]
            b = float(basis[k, l]) * values[f, HALO - 1 - l, rows, :]
            top = a if top is None else top + a
            bottom = b if bottom is None else bottom + b
        up[f, k, rows, :] = top
        down[f, k, rows, :] = bottom


def row_chunks(rows):
    return [slice(start, start + 8) for start in range(0, rows, 8)]


def flat(values):
    return values.reshape(-1, values.shape[-1])


def kernel_inputs(rho_in, mom_in, ene_in, conserved, first, arrived):
    copies = [
        pltpu.make_async_copy(source, conserved.at[part], arrived.at[k])
        for k, (source, part) in enumerate(
            ((rho_in, 0), (mom_in, slice(1, 4)), (ene_in, 4))
        )
    ]
    for copy in copies:
        copy.start()
    for copy in copies:
        copy.wait()

    def plane(x, carry):
        inverse = 1.0 / conserved[0, x]
        first[0, x] = conserved[1, x] * inverse
        first[1, x] = conserved[3, x] * inverse
        return carry

    lax.fori_loop(0, CX, plane, 0, unroll=2)


def kernel_primitives(conserved, first, own, second, up, down):
    def plane(x, carry):
        density = conserved[0, x]
        inverse = 1.0 / density
        u = first[0, x]
        w = first[1, x]
        v = conserved[2, x] * inverse
        kinetic = 0.5 * (conserved[1, x] * u + conserved[2, x] * v + conserved[3, x] * w)
        temperature = (heat_ratio - 1.0) * (conserved[4, x] - kinetic) * inverse
        own[U, x] = u
        own[W, x] = w
        own[V, x] = v
        own[T, x] = temperature
        second[0, x] = v
        second[1, x] = temperature
        second[2, x] = density
        return carry

    lax.fori_loop(0, CX, plane, 0, unroll=2)

    def sums(f, carry):
        for rows in row_chunks(own.shape[2]):
            halo_sums(own, f, rows, up, down)
        return carry

    lax.fori_loop(0, 4, sums, 0)


def kernel_pitch_gradients(
    own, y_high, y_low, dy, mu, mate_u, mate_w, mate_b
):
    for f in range(4):
        dy[f] = left_product(y_high[...], y_low[...], flat(own[f])).reshape(own.shape[1:])

    def plane(x, carry):
        mu[x] = shear_resistance_reference * jnp.exp(
            sutherland_power_law * jnp.log(own[T, x])
        )
        mate_u[x] = own[U, x]
        mate_w[x] = own[W, x]
        for f in range(2):
            mate_b[f, x] = own[V + f, x]
        return carry

    lax.fori_loop(0, CX, plane, 0)


def kernel_stream_gradients(own, before, after, mu, peer_first, dx, third, for_u, for_w):
    for_u[...] = peer_first[0]
    for_w[...] = peer_first[1]

    def field(f, carry):
        for rows in row_chunks(own.shape[2]):
            derived = compact_x(extended(before, own, after, f, rows))
            for x in range(CX):
                dx[f, x, rows, :] = derived[x]
        return carry

    lax.fori_loop(0, 4, field, 0)

    def plane(x, carry):
        third[0, x] = (2.0 / 3.0) * mu[x] * dx[U, x]
        third[1, x] = mu[x] * dx[W, x]
        return carry

    lax.fori_loop(0, CX, plane, 0)


def kernel_flux_x(
    own, second, peer_first, mate_u, mate_w, across_u, across_w, dx, dy, mu,
    z_high, z_low, f_high, f_low, dz, flux, up, down,
):
    width = own.shape[-1]
    odd = lax.rem(lax.axis_index("gy"), 2)
    for f, (mate, across) in enumerate(((mate_u, across_u), (mate_w, across_w))):
        values = jnp.concatenate(
            [flat(own[f]), flat(peer_first[f]), flat(mate[...]), flat(across[...])], axis=1
        )
        dz[f] = right_product(values, z_high[odd], z_low[odd])

    rows = own.shape[2]

    def plane(x, carry):
        at = pl.ds(pl.multiple_of(x * rows, rows), rows)
        u, w, v, t = (own[f, x] for f in range(4))
        density = second[2, x]
        viscosity = mu[x]
        dil = dx[U, x] + dy[V, x] + dz[1, at, :width]
        s1 = viscosity * (2.0 * dx[U, x] - (2.0 / 3.0) * dil)
        s2 = viscosity * (dx[V, x] + dy[U, x])
        s3 = viscosity * (dx[W, x] + dz[0, at, :width])
        m = density * u
        total = m * (enthalpy * t + 0.5 * (u * u + v * v + w * w))
        flux[0, x] = m
        flux[1, x] = m * u + density * t - s1
        flux[2, x] = m * v - s2
        flux[3, x] = m * w - s3
        flux[4, x] = total - (s1 * u + s2 * v + s3 * w) - conduction * viscosity * dx[T, x]
        return carry

    lax.fori_loop(0, CX, plane, 0)

    def sums(f, carry):
        for chunk in row_chunks(rows):
            halo_sums(flux, f, chunk, up, down)
        return carry

    lax.fori_loop(0, 5, sums, 0)


def kernel_peer(peer_second, flux, for_v, for_t):
    for_v[...] = peer_second[0]
    for_t[...] = peer_second[1]


def kernel_flux_yz_early(
    own, second, peer_first, peer_second, for_v, dz, dx, dy, mu, y_high, y_low, f_high, f_low,
    spread, local, dy_peer, mu_peer, flux, flux_y,
):
    rows, width = own.shape[2:]
    odd = lax.rem(lax.axis_index("gy"), 2)
    dy_peer[0] = left_product(y_high[...], y_low[...], flat(peer_second[0]))
    dy_peer[1] = left_product(y_high[...], y_low[...], flat(peer_first[1]))

    def plane(x, carry):
        at = pl.ds(pl.multiple_of(x * rows, rows), rows)
        here = slice(0, width)
        there = slice(width, 2 * width)

        def span(lanes, u, w, t, density, viscosity, yv):
            m = density * w
            flux[0, at, lanes] = m
            flux[1, at, lanes] = m * u - viscosity * dz[0, at, lanes]
            flux[2, at, lanes] = (
                m * w
                + density * t
                - viscosity * ((4.0 / 3.0) * dz[1, at, lanes] - (2.0 / 3.0) * yv)
            )

        u, w, v, t = (own[f, x] for f in range(4))
        density = second[2, x]
        viscosity = mu[x]
        span(here, u, w, t, density, viscosity, dy[V, x])
        dil = dx[U, x] + dy[V, x] + dz[1, at, here]
        m = density * v
        flux_y[0, at, :] = m
        flux_y[1, at, :] = m * u - viscosity * (dy[U, x] + dx[V, x])
        flux_y[2, at, :] = (
            m * v + density * t - viscosity * (2.0 * dy[V, x] - (2.0 / 3.0) * dil)
        )
        t = peer_second[1, x]
        viscosity = shear_resistance_reference * jnp.exp(sutherland_power_law * jnp.log(t))
        mu_peer[at, :] = viscosity
        span(
            there, peer_first[0, x], peer_first[1, x], t, peer_second[2, x], viscosity,
            dy_peer[0, at, :],
        )
        return carry

    lax.fori_loop(0, CX, plane, 0)
    for k in range(3):
        spread[k] = right_product(flux[k], f_high[odd], f_low[odd])
        local[k] = left_product(y_high[...], y_low[...], flux_y[k])


def kernel_flux_yz(
    own, second, peer_first, peer_second, second_mate, across_v, across_t, dy_peer, mu_peer,
    spread_early, local_early, dz, dx, dy, mu, y_high, y_low, z_high, z_low, f_high, f_low,
    part, part_mate, dz_more, flux, flux_y,
):
    rows, width = own.shape[2:]
    odd = lax.rem(lax.axis_index("gy"), 2)
    for f, across in enumerate((across_v, across_t)):
        values = jnp.concatenate(
            [flat(own[V + f]), flat(peer_second[f]), flat(second_mate[f]), flat(across[...])],
            axis=1,
        )
        dz_more[f] = right_product(values, z_high[odd], z_low[odd])

    def plane(x, carry):
        at = pl.ds(pl.multiple_of(x * rows, rows), rows)
        here = slice(0, width)
        there = slice(width, 2 * width)

        def span(lanes, u, w, v, t, density, viscosity, yv, yw):
            s1 = viscosity * dz[0, at, lanes]
            s2 = viscosity * (dz_more[0, at, lanes] + yw)
            s3 = viscosity * ((4.0 / 3.0) * dz[1, at, lanes] - (2.0 / 3.0) * yv)
            energy = density * (enthalpy * t + 0.5 * (u * u + v * v + w * w))
            flux[0, at, lanes] = density * w * v - s2
            flux[1, at, lanes] = (
                energy * w
                - (s1 * u + s2 * v + s3 * w)
                - conduction * viscosity * dz_more[1, at, lanes]
            )
            return energy

        u, w, v, t = (own[f, x] for f in range(4))
        density = second[2, x]
        viscosity = mu[x]
        energy = span(here, u, w, v, t, density, viscosity, dy[V, x], dy[W, x])
        dil = dx[U, x] + dy[V, x] + dz[1, at, here]
        s1 = viscosity * (dy[U, x] + dx[V, x])
        s2 = viscosity * (2.0 * dy[V, x] - (2.0 / 3.0) * dil)
        s3 = viscosity * (dy[W, x] + dz_more[0, at, here])
        flux_y[0, at, :] = density * v * w - s3
        flux_y[1, at, :] = (
            energy * v - (s1 * u + s2 * v + s3 * w) - conduction * viscosity * dy[T, x]
        )
        span(
            there, peer_first[0, x], peer_first[1, x], peer_second[0, x], peer_second[1, x],
            peer_second[2, x], mu_peer[at, :], dy_peer[0, at, :], dy_peer[1, at, :],
        )
        return carry

    lax.fori_loop(0, CX, plane, 0)
    shape = own.shape[1:]
    spreads = {0: spread_early[0], 1: spread_early[1], 3: spread_early[2]}
    locals_y = {0: local_early[0], 1: local_early[1], 2: local_early[2]}
    for k in range(2):
        spreads[2 + 2 * k] = right_product(flux[k], f_high[odd], f_low[odd])
        locals_y[3 + k] = left_product(y_high[...], y_low[...], flux_y[k])
    for f in range(5):
        part[f] = (spreads[f][:, :width] + locals_y[f]).reshape(shape)
        part_mate[f] = spreads[f][:, width:].reshape(shape)


def kernel_corrections(
    own, peer_first, third, peer_third, part, part_mate, f_high, f_low, total, *for_mate
):
    width = own.shape[-1]
    odd = lax.rem(lax.axis_index("gy"), 2)
    shape = own.shape[1:]
    for f in (0, 2):
        total[f] = part[f]
        for_mate[f][...] = part_mate[f]
    pairs = ((own, third), (peer_first, peer_third))
    for f in (1, 3, 4):
        sides = []
        for speeds, shared in pairs:
            if f == 1:
                value = -shared[1]
            elif f == 3:
                value = shared[0]
            else:
                value = shared[0] * speeds[W] - shared[1] * speeds[U]
            sides.append(flat(value))
        spread = right_product(jnp.concatenate(sides, axis=1), f_high[odd], f_low[odd])
        total[f] = part[f] + spread[:, :width].reshape(shape)
        for_mate[f][...] = part_mate[f] + spread[:, width:].reshape(shape)


def kernel_add_stream(total, flux, before, after, result):
    def field(f, carry):
        for rows in row_chunks(flux.shape[2]):
            derived = compact_x(extended(before, flux, after, f, rows))
            for x in range(CX):
                result[f, x, rows, :] = total[f, x, rows, :] + derived[x]
        return carry

    lax.fori_loop(0, 5, field, 0)


def kernel_finish(
    conserved, total, mate_0, mate_1, mate_2, mate_3, mate_4, tendency, advanced,
    rate, state, sent,
):
    copies = []
    for f, from_mate in enumerate((mate_0, mate_1, mate_2, mate_3, mate_4)):
        value = -(total[f] + from_mate[...])
        rate[f] = value
        state[f] = conserved[f] + section_step * value
        for k, (source, target) in enumerate(((rate, tendency), (state, advanced))):
            copy = pltpu.make_async_copy(source.at[f], target.at[f], sent.at[2 * f + k])
            copy.start()
            copies.append(copy)
    for copy in copies:
        copy.wait()


def call(kernel, outputs, operands, scratch=(), outside=False, written=False):
    space = pltpu.HBM if outside else pltpu.VMEM
    target = pltpu.HBM if written else pltpu.VMEM
    in_specs = [pl.BlockSpec(memory_space=space) for _ in operands]
    if outside:
        operands = [pltpu.with_memory_space_constraint(value, pltpu.HBM) for value in operands]
    touched = sum(value.size * value.dtype.itemsize for value in operands)
    touched += 4 * sum(int(np.prod(shape)) for shape in outputs)
    return pl.pallas_call(
        kernel,
        out_shape=[jax.ShapeDtypeStruct(shape, F32) for shape in outputs],
        in_specs=in_specs,
        out_specs=[pl.BlockSpec(memory_space=target) for _ in outputs],
        scratch_shapes=list(scratch),
        cost_estimate=pl.CostEstimate(flops=0, bytes_accessed=touched, transcendentals=0),
        compiler_params=pltpu.CompilerParams(vmem_limit_bytes=24 * 1024 * 1024),
    )(*operands)


def fast_device(mass_per_volume, momentum, energy):
    rho = jnp.transpose(mass_per_volume, (0, 2, 1))
    mom = jnp.transpose(momentum, (0, 1, 3, 2))
    ene = jnp.transpose(energy, (0, 2, 1))
    _, rows, width = rho.shape
    length = 4 * width
    z_high, z_low = span_blocks(length, PLACES, PLACES[:2])
    f_high, f_low = span_blocks(length, PLACES[:2], (0, 1))
    y_high, y_low = halves(np.kron(np.eye(CX, dtype=np.float32), pitch_matrix(rows, CY)))
    block = (CX, rows, width)
    sums = (2, rows, width)
    points = CX * rows
    devices = lax.axis_size("gx")
    ring_up = [(i, (i + 1) % devices) for i in range(devices)]
    ring_down = [(j, i) for i, j in ring_up]
    to_mate = [(i, i ^ 1) for i in range(4)]
    to_peer = [(i, i ^ 2) for i in range(4)]

    conserved, first = call(
        kernel_inputs,
        [(5,) + block, (2,) + block],
        (rho, mom, ene),
        scratch=(pltpu.SemaphoreType.DMA((3,)),),
        outside=True,
    )
    own, second, up, down = call(
        kernel_primitives,
        [(4,) + block, (3,) + block, (4,) + sums, (4,) + sums],
        (conserved, first),
    )
    peer_first = lax.ppermute(first, "gy", to_peer)
    before = lax.ppermute(up, "gx", ring_up)
    after = lax.ppermute(down, "gx", ring_down)
    dy, mu, for_u, for_w, mate_b = call(
        kernel_pitch_gradients,
        [(4,) + block, block, block, block, (2,) + block],
        (own, y_high, y_low),
    )
    mate_u, mate_w = (lax.ppermute(value, "gy", to_mate) for value in (for_u, for_w))
    second_mate = lax.ppermute(mate_b, "gy", to_mate)
    peer_second = lax.ppermute(second, "gy", to_peer)
    dx, third, for_u, for_w = call(
        kernel_stream_gradients,
        [(4,) + block, (2,) + block, block, block],
        (own, before, after, mu, peer_first),
    )
    across_u, across_w = (lax.ppermute(value, "gy", to_mate) for value in (for_u, for_w))
    peer_third = lax.ppermute(third, "gy", to_peer)
    dz, flux, flux_up, flux_down = call(
        kernel_flux_x,
        [(2, points, 2 * width), (5,) + block, (5,) + sums, (5,) + sums],
        (
            own, second, peer_first, mate_u, mate_w, across_u, across_w, dx, dy, mu,
            z_high, z_low, f_high, f_low,
        ),
    )
    flux_before = lax.ppermute(flux_up, "gx", ring_up)
    flux_after = lax.ppermute(flux_down, "gx", ring_down)
    for_v, for_t = call(kernel_peer, [block, block], (peer_second, flux))
    across_v = lax.ppermute(for_v, "gy", to_mate)
    across_t = lax.ppermute(for_t, "gy", to_mate)
    spread, local, dy_peer, mu_peer = call(
        kernel_flux_yz_early,
        [(3, points, 2 * width), (3, points, width), (2, points, width), (points, width)],
        (
            own, second, peer_first, peer_second, for_v, dz, dx, dy, mu,
            y_high, y_low, f_high, f_low,
        ),
        scratch=(
            pltpu.VMEM((3, points, 2 * width), F32),
            pltpu.VMEM((3, points, width), F32),
        ),
    )
    part, part_mate = call(
        kernel_flux_yz,
        [(5,) + block, (5,) + block],
        (
            own, second, peer_first, peer_second, second_mate, across_v, across_t,
            dy_peer, mu_peer, spread, local, dz, dx, dy, mu,
            y_high, y_low, z_high, z_low, f_high, f_low,
        ),
        scratch=(
            pltpu.VMEM((2, points, 2 * width), F32),
            pltpu.VMEM((2, points, 2 * width), F32),
            pltpu.VMEM((2, points, width), F32),
        ),
    )
    total, *for_mate = call(
        kernel_corrections,
        [(5,) + block] + 5 * [block],
        (own, peer_first, third, peer_third, part, part_mate, f_high, f_low),
    )
    from_mate = [lax.ppermute(value, "gy", to_mate) for value in for_mate]
    (total,) = call(
        kernel_add_stream, [(5,) + block], (total, flux, flux_before, flux_after)
    )
    tendency, advanced = call(
        kernel_finish,
        [(5,) + block, (5,) + block],
        (conserved, total, *from_mate),
        scratch=(
            pltpu.VMEM((5,) + block, F32),
            pltpu.VMEM((5,) + block, F32),
            pltpu.SemaphoreType.DMA((10,)),
        ),
        written=True,
    )
    return (
        jnp.transpose(tendency, (0, 1, 3, 2)),
        jnp.transpose(advanced, (0, 1, 3, 2)),
    )


def padded(array, sides, width):
    for axis, dim in sides:
        devices, length = (lax.axis_size(axis), array.shape[dim])
        up = [(i, (i + 1) % devices) for i in range(devices)]
        down = [(j, i) for i, j in up]
        last = lax.slice_in_dim(array, length - width, length, axis=dim)
        initial = lax.slice_in_dim(array, 0, width, axis=dim)
        before = lax.ppermute(last, axis, up)
        after = lax.ppermute(initial, axis, down)
        array = jnp.concatenate([before, array, after], axis=dim)
    return array


def right_side(conserved, gradients_of, derive_x, derive_y, derive_z):
    mass_per_volume = conserved[0]
    momentum = conserved[1:4]
    energy = conserved[4]
    local_speed_vector = momentum / mass_per_volume
    kinetic = 0.5 * jnp.sum(momentum * local_speed_vector, axis=0)
    normal_force_per_area = (heat_ratio - 1.0) * (energy - kinetic)
    thermal_state = normal_force_per_area / mass_per_volume
    basic_quantities = jnp.concatenate([local_speed_vector, thermal_state[None]], 0)
    gradients = gradients_of(basic_quantities)
    shear_resistance = shear_resistance_reference * jnp.power(thermal_state, sutherland_power_law)
    conductivity = shear_resistance * heat_ratio / ((heat_ratio - 1.0) * prandtl)
    dilatation = gradients[0][0] + gradients[1][1] + gradients[2][2]
    derivers = (derive_x, derive_y, derive_z)
    accumulated = None
    for direction in range(3):
        stress_column = [
            shear_resistance * (gradients[direction][component] + gradients[component][direction])
            for component in range(3)
        ]
        stress_column[direction] = (
            stress_column[direction] - 2.0 / 3.0 * shear_resistance * dilatation
        )
        fluxes = [momentum[direction]]
        for component in range(3):
            moment_flux = (
                momentum[component] * local_speed_vector[direction] - stress_column[component]
            )
            if component == direction:
                moment_flux = moment_flux + normal_force_per_area
            fluxes.append(moment_flux)
        work_term = (
            stress_column[0] * local_speed_vector[0]
            + stress_column[1] * local_speed_vector[1]
            + stress_column[2] * local_speed_vector[2]
        )
        fluxes.append(
            (energy + normal_force_per_area) * local_speed_vector[direction]
            - work_term
            - conductivity * gradients[direction][3]
        )
        divergence_part = derivers[direction](jnp.stack(fluxes))
        accumulated = divergence_part if accumulated is None else accumulated + divergence_part
    return -accumulated


def plain_device(mass_per_volume, momentum, energy):
    conserved = jnp.concatenate([mass_per_volume[None], momentum, energy[None]], 0)
    highest = lax.Precision.HIGHEST
    x_matrix = jnp.asarray(compact_matrix(CX, HALO))
    z_matrix = jnp.asarray(span_matrix(NZ))

    def apply_x(extended):
        return jnp.einsum("il,flab->fiab", x_matrix, extended, precision=highest)

    def flux_x(values):
        return apply_x(padded(values, (("gx", 1),), HALO))

    y_matrix = jnp.asarray(pitch_matrix(conserved.shape[3], CY))

    def apply_y(values):
        return jnp.einsum("fabk,jk->fabj", values, y_matrix, precision=highest)

    def derive_span(values):
        lines = jnp.transpose(
            lax.all_to_all(values, "gy", split_axis=3, concat_axis=2, tiled=True), (0, 1, 3, 2)
        )
        derived = jnp.einsum("fack,jk->facj", lines, z_matrix, precision=highest)
        returned = lax.all_to_all(derived, "gy", split_axis=3, concat_axis=2, tiled=True)
        return jnp.transpose(returned, (0, 1, 3, 2))

    def gradients_of(basic_quantities):
        extended = padded(basic_quantities, (("gx", 1),), HALO)
        return (apply_x(extended), apply_y(basic_quantities), derive_span(basic_quantities))

    tendency = right_side(conserved, gradients_of, flux_x, apply_y, derive_span)
    advanced = conserved + section_step * tendency
    return (tendency, advanced)


def per_device(mass_per_volume, momentum, energy):
    planes, width, rows = mass_per_volume.shape
    fits = planes == CX and width % 128 == 0 and rows <= 32 and rows % CY == 0
    if fits and lax.axis_size("gy") == 4 and lax.axis_size("gx") % 2 == 0:
        return fast_device(mass_per_volume, momentum, energy)
    return plain_device(mass_per_volume, momentum, energy)


def solution(mesh):
    in_specs = (P("gx", "gy", None), P(None, "gx", "gy", None), P("gx", "gy", None))
    out_specs = (P(None, "gx", "gy", None), P(None, "gx", "gy", None))
    return jax.shard_map(
        per_device, mesh=mesh, in_specs=in_specs, out_specs=out_specs, check_vma=False
    )
```
